32 devices in a mesh: inline: 8 (over y, x, core), xline: 4 (over z).
Axes of the slice: x: 2, y: 2, z: 4, core: 2. Of those that a mesh axis runs over, the one named last changes fastest.
Arguments:
- traces: bfloat16 [8192, 2048], P(('inline', 'xline')), may hold values from -6 to 6
- owners: int32 [8192, 1], P(('inline', 'xline')), may hold values from 0 to 31, as said below
- midpoint: int32 [8192], P(('inline', 'xline')), may hold values from 0 to 7
- offset_class: int32 [8192], P(('inline', 'xline')), may hold values from 0 to 3
- offsets: float32 [4], replicated, may hold values from 51 to 1024
- velocities: float32 [16], replicated, may hold values from 1 to 4
Outputs:
- stacked: bfloat16 [256, 16, 2048], P(('inline', 'xline'))
- semblance: float32 [256, 16, 2048], P(('inline', 'xline'))
The draws below stay inside these ranges and needn't reach their ends.
Inputs may be any that keep to these rules, and one draw needn't show every extreme that they name: The 256 traces of one device name one owner at most 16 times; some owners receive 16 traces from every device, and some owners receive none.
All inputs are finite; a program needn't handle non-finite values.
Results may differ from the reference program's by a relative error of at most 0.0053.
Values may be sent and summed in bfloat16 or wider, within the bound.
No kernel may reach another device: no remote copies, remote signals or barrier semaphores. Data moves between devices by JAX's collectives and lax.ppermute only.
A program may use at most 64 MiB of HBM per device.

```python
import math
import jax
import jax.numpy as jnp
from jax import lax

NT = 2048
VEL = 16
H = 4
HALF_WIN = 4
TR_DEV = 256
CMP_DEV = 8
CAP = 16
TRACES = 8192
NCMP = 256
DEVICES = 32


def draw_owners(key, part):
    slot_count = DEVICES * CAP
    base_key = jax.random.fold_in(key, 7301)
    key_pair, key_single, key_order, key_level, key_rows = jax.random.split(base_key, 5)
    first_dead = jax.random.randint(key_pair, (), 0, DEVICES - 1)
    lone_dead = (first_dead + 2 + jax.random.randint(key_single, (), 0, DEVICES - 2)) % DEVICES
    owner_ids = jnp.arange(DEVICES)
    dead_owner = (owner_ids == first_dead) | (owner_ids == first_dead + 1) | (owner_ids == lone_dead)
    priority = jax.random.permutation(key_order, DEVICES)
    busiest_owner = (priority < max(1, DEVICES // 16) + 3) & jnp.logical_not(dead_owner)
    workload_level = jax.random.randint(key_level, (DEVICES,), 0, 4)
    reward_score = jnp.where(busiest_owner, 16384, workload_level * 256)
    position_owner = jnp.arange(slot_count) // CAP
    position_empty = dead_owner[position_owner]
    position_reward = reward_score[position_owner]

    def one_block(block_key):
        key_score, key_shuffle = jax.random.split(block_key)
        random_perturbation = jax.random.randint(key_score, (slot_count,), 0, 1024)
        position_score = jnp.where(position_empty, -1, position_reward + random_perturbation)
        distinct = position_score * slot_count + jnp.arange(slot_count)
        chosen = lax.top_k(distinct, TR_DEV)[1]
        return jax.random.permutation(key_shuffle, chosen // CAP)
    blocks = jax.vmap(one_block)(jax.random.split(key_rows, DEVICES))
    return blocks.reshape(TRACES, 1).astype(jnp.int32)


def with_ends(drawn, key, smallest, high):
    longest = drawn.shape.index(max(drawn.shape))
    spots = []
    for shift in (0, 1):
        where = [jax.random.randint(jax.random.fold_in(key, axis), (), 0, length) for axis, length in enumerate(drawn.shape)]
        where[longest] = (where[longest] + shift) % drawn.shape[longest]
        spots.append(tuple(where))
    return drawn.at[spots[0]].set(smallest).at[spots[1]].set(high)


def levels(key, shape, shards, low, largest):
    level = 1.0
    for axis_at, shards_of in shards:
        heights = jax.random.uniform(jax.random.fold_in(jax.random.fold_in(key, 6), axis_at), (shards_of,), jnp.float32, low / len(shards), largest / len(shards))
        level = level * jnp.repeat(jnp.exp(heights), shape[axis_at] // shards_of).reshape((-1,) + (1,) * (len(shape) - 1 - axis_at))
    return level


def gaussian(rng, shape, deviation, bound, cuts=(), kind=jnp.bfloat16):
    loudness = levels(rng, shape, cuts, -0.22, 0.18) if cuts else 1.0
    result = jax.random.normal(rng, shape, jnp.float32) * deviation * loudness
    return jnp.minimum(jnp.maximum(result, -bound), bound).astype(kind)


def setup_inputs(seed: int = 0) -> dict:
    keys = jax.random.split(jax.random.key(seed), 7)
    return {
        "traces": gaussian(keys[0], (TRACES, NT), 1.0, 6.0, ((0, 32),)),
        "owners": draw_owners(jax.random.fold_in(keys[6], 71), 0),
        "midpoint": with_ends(jax.random.randint(keys[2], (TRACES,), 0, CMP_DEV), jax.random.fold_in(keys[2], 1), 0, CMP_DEV - 1).astype(jnp.int32),
        "offset_class": with_ends(jax.random.randint(keys[3], (TRACES,), 0, H), jax.random.fold_in(keys[3], 1), 0, H - 1).astype(jnp.int32),
        "offsets": jnp.clip(jax.random.uniform(keys[4], (H,), jnp.float32, 51.0, 1024.0), 51.0, 1024.0),
        "velocities": jnp.clip(jnp.exp(jax.random.uniform(keys[5], (VEL,), jnp.float32, math.log(1.0), math.log(4.0))), 1.0, 4.0),
    }


def window_sum(values):
    length = values.shape[-1]
    padded = jnp.pad(values, [(0, 0)] * (values.ndim - 1) + [(HALF_WIN, HALF_WIN)])
    summed = padded[..., 0:length]
    for offset in range(1, 2 * HALF_WIN + 1):
        summed = summed + padded[..., offset:offset + length]
    return summed

def neighbour_sum(values):
    padded = jnp.pad(values, ((1, 1), (0, 0)))
    return padded[0:-2] + padded[1:-1] + padded[2:]

def reference(traces, owners, midpoint, offset_class, offsets, velocities):
    classes = offsets.shape[0]
    samples = traces.shape[1]
    global_mid = owners[:, 0] * CMP_DEV + midpoint
    slot_keys = global_mid * classes + offset_class
    block_rows = TR_DEV * math.gcd(DEVICES, 16)

    def add_block(running, pieces):
        part_traces, part_keys = pieces
        return (running + jax.ops.segment_sum(part_traces.astype(jnp.float32), part_keys, NCMP * classes), None)
    start_sum = jnp.zeros((NCMP * classes, samples), jnp.float32)
    gathers, _ = lax.scan(add_block, start_sum, (traces.reshape(-1, block_rows, samples), slot_keys.reshape(-1, block_rows)))
    binned = lax.optimization_barrier(gathers.astype(jnp.bfloat16)).astype(jnp.float32).reshape(NCMP, classes, samples)
    fold_count = jax.ops.segment_sum(jnp.ones(midpoint.shape, jnp.float32), global_mid, NCMP)
    padded = jnp.pad(binned, ((0, 0), (0, 0), (0, 2)))
    sample_time = jnp.arange(samples).astype(jnp.float32)
    shaped = (NCMP, classes, samples)

    def per_velocity(velocity):
        slowness = offsets / velocity
        position = jnp.sqrt(sample_time[None, :] * sample_time[None, :] + (slowness * slowness)[:, None])
        floored = jnp.floor(position)
        fraction = position - floored
        sample_index = jnp.minimum(floored, float(samples)).astype(jnp.int32)
        low_weight = lax.optimization_barrier((1.0 - fraction).astype(jnp.bfloat16)).astype(jnp.float32)
        high_weight = lax.optimization_barrier(fraction.astype(jnp.bfloat16)).astype(jnp.float32)
        lower_val = jnp.take_along_axis(padded, jnp.broadcast_to(sample_index[None], shaped), axis=2)
        upper_val = jnp.take_along_axis(padded, jnp.broadcast_to(sample_index[None] + 1, shaped), axis=2)
        moved_out = low_weight[None] * lower_val + high_weight[None] * upper_val
        summed = lax.optimization_barrier(jnp.sum(moved_out, axis=1))
        energy = lax.optimization_barrier(jnp.sum(moved_out * moved_out, axis=1))
        stacked = (summed / jnp.maximum(fold_count, 1.0)[:, None]).astype(jnp.bfloat16)
        numerator = neighbour_sum(window_sum(summed * summed))
        denominator = neighbour_sum(window_sum(energy))
        return (stacked, numerator / jnp.maximum(classes * denominator, 1.0))
    stacked, semblance = lax.map(per_velocity, velocities)
    return (jnp.transpose(stacked, (1, 0, 2)), jnp.transpose(semblance, (1, 0, 2)))
```

```python
import functools
import math

import jax
import jax.numpy as jnp
from jax import lax
from jax.experimental import pallas as pl
from jax.experimental.pallas import tpu as pltpu
from jax.sharding import PartitionSpec as P

HALF_WIN = 4
CMP_DEV = 8
LANES = 128
F32 = jnp.float32
BF16 = jnp.bfloat16
VMEM = pl.BlockSpec(memory_space=pltpu.VMEM)
SMEM = pl.BlockSpec(memory_space=pltpu.SMEM)

LANE_GATHER = lax.GatherDimensionNumbers(
    offset_dims=(),
    collapsed_slice_dims=(1,),
    start_index_map=(1,),
    operand_batching_dims=(0,),
    start_indices_batching_dims=(0,),
)


def take_lanes(rows, index):
    return lax.gather(
        rows,
        index[..., None],
        LANE_GATHER,
        (1, 1),
        mode=lax.GatherScatterMode.PROMISE_IN_BOUNDS,
    )


def bin_kernel(kept_rows, places_ref, *refs):
    *data, kept_ref, sent_ref, member_ref = refs
    rows = member_ref.shape[0]
    per = data[0].shape[0]

    @pl.when(pl.program_id(0) == 0)
    def _():
        row = lax.broadcasted_iota(jnp.int32, member_ref.shape, 0)
        first = jnp.broadcast_to(places_ref[0:1, :], member_ref.shape)
        second = jnp.broadcast_to(places_ref[1:2, :], member_ref.shape)
        hit = (row == first) | (row == second)
        member_ref[...] = jnp.where(hit, 1.0, 0.0).astype(BF16)

    total = None
    for at, block in enumerate(data):
        part = jnp.dot(
            member_ref[:, at * per : (at + 1) * per], block[...], preferred_element_type=F32
        )
        total = part if total is None else total + part
    kept_ref[...] = total[:kept_rows]
    if kept_rows < rows:
        sent_ref[...] = total[kept_rows:].astype(BF16)
    else:
        sent_ref[...] = jnp.zeros(sent_ref.shape, BF16)


def bin_rows(places, data, starts, cols, rows, kept_rows):
    tile = math.gcd(cols, 256)
    per = data[0].shape[0]
    sent_rows = max(rows - kept_rows, 16)
    in_specs = [pl.BlockSpec(places.shape, lambda t: (0, 0))]
    for start in starts:
        in_specs.append(pl.BlockSpec((per, tile), lambda t, s=start // tile: (0, t + s)))
    return pl.pallas_call(
        functools.partial(bin_kernel, kept_rows),
        grid=(cols // tile,),
        in_specs=in_specs,
        out_specs=[
            pl.BlockSpec((kept_rows, tile), lambda t: (0, t)),
            pl.BlockSpec((sent_rows, tile), lambda t: (0, t)),
        ],
        out_shape=[
            jax.ShapeDtypeStruct((kept_rows, cols), F32),
            jax.ShapeDtypeStruct((sent_rows, cols), BF16),
        ],
        scratch_shapes=[pltpu.VMEM((rows, len(data) * per), BF16)],
        compiler_params=pltpu.CompilerParams(vmem_limit_bytes=40 * 1024 * 1024),
        cost_estimate=pl.CostEstimate(
            flops=2 * rows * len(data) * per * cols,
            bytes_accessed=2 * len(data) * per * cols + 6 * rows * cols,
            transcendentals=0,
        ),
    )(places, *data)


def exchange_rows(traces, key, classes):
    inline_count = lax.axis_size("inline")
    xline_count = lax.axis_size("xline")
    me = lax.axis_index("inline")
    me_x = lax.axis_index("xline")
    per, samples = traces.shape
    dev_rows = CMP_DEV * classes
    line_rows = xline_count * dev_rows
    block_rows = -(-(line_rows + 2 * classes) // 16) * 16
    bits = [1 << b for b in range(inline_count.bit_length() - 1)]

    def swap(value, bit):
        return lax.ppermute(value, "inline", [(i, i ^ bit) for i in range(inline_count)])

    core, others = bits[0], bits[1:]
    orders = [others, others[::-1]] if len(others) > 1 else [others]
    cols = samples // len(orders)

    pair_key = jnp.stack([key, swap(key, core)])
    mate = swap(traces, core)
    totals = []
    for part, order in enumerate(orders):
        start = part * cols
        data, starts, keys = [traces, mate], [start, start], [pair_key]
        done = core
        if order:
            first = order[0]
            done |= first
            far = swap(lax.slice_in_dim(traces, start, start + cols, axis=1), first)
            data += [far, swap(far, core)]
            starts += [0, 0]
            keys.append(swap(pair_key, first))
        rest = order[1:]
        keys = jnp.concatenate(keys).reshape(-1)
        line = keys // line_rows
        local = keys % line_rows

        def row_of(target, at):
            apart = target ^ me
            code = jnp.zeros_like(target)
            for bit in rest:
                code = code * 2 + jnp.where(apart & bit != 0, 1, 0)
            valid = (apart & done == 0) & (target >= 0) & (target < inline_count)
            return jnp.where(valid, code * block_rows + at, -1)

        own_place = row_of(line, local + classes)
        low, high = local < classes, local >= line_rows - classes
        rim_place = jnp.where(
            high,
            row_of(line + 1, local - (line_rows - classes)),
            jnp.where(low, row_of(line - 1, local + classes + line_rows), -1),
        )
        rows = block_rows << len(rest)
        half = rows // 2 if rest else rows
        kept, sent = bin_rows(jnp.stack([own_place, rim_place]), data, starts, cols, rows, half)
        for at, bit in enumerate(rest):
            if at:
                half = kept.shape[0] // 2
                sent = kept[half:].astype(BF16)
                kept = kept[:half]
            kept = kept + swap(sent, bit).astype(F32)
        totals.append(kept)
    total = jnp.concatenate(totals, axis=1) if len(totals) > 1 else totals[0]

    window = dev_rows + 2 * classes
    rounded = total.astype(BF16)
    power_of_two = xline_count & (xline_count - 1) == 0
    result = lax.dynamic_slice_in_dim(total, me_x * dev_rows, window, 0)
    for step in range(xline_count - 1, 0, -1):
        if power_of_two:
            target = me_x ^ step
            pairs = [(i, i ^ step) for i in range(xline_count)]
        else:
            target = (me_x + step) % xline_count
            pairs = [(i, (i + step) % xline_count) for i in range(xline_count)]
        block = lax.dynamic_slice_in_dim(rounded, target * dev_rows, window, 0)
        result = result + lax.ppermute(block, "xline", pairs).astype(F32)
    return result


def panel_kernel(
    classes,
    vels,
    blocks_ref,
    scale_ref,
    rows_ref,
    local_ref,
    low_ref,
    high_ref,
    stacked_ref,
    semblance_ref,
    plane_ref,
    source_ref,
    rim_source_ref,
    sum_ref,
    energy_ref,
    rim_ref,
    window_ref,
):
    count = rows_ref.shape[1] // LANES
    mids = CMP_DEV
    lane = lax.broadcasted_iota(jnp.int32, (8, LANES), 1)
    sub = lax.broadcasted_iota(jnp.int32, (8, LANES), 0)
    sub16 = lax.broadcasted_iota(jnp.int32, (16, LANES), 0)

    for at in range(count):
        block = rows_ref[:, at * LANES : (at + 1) * LANES]
        plane_ref[at] = block.astype(BF16).astype(F32)
    plane_ref[count] = jnp.zeros(plane_ref.shape[1:], F32)

    def later(here, after):
        return jnp.where(
            lane == LANES - 1,
            pltpu.roll(after, LANES - 1, 1),
            pltpu.roll(here, LANES - 1, 1),
        )

    def rim_rows(at):
        return jnp.where(
            sub < classes, plane_ref[at, 0:8, :], plane_ref[at, mids * classes : mids * classes + 8, :]
        )

    zeros = jnp.zeros((16, LANES), BF16)
    for at in range(count):
        for h in range(classes):
            here = plane_ref[at, pl.ds(classes + h, mids, stride=classes), :]
            after = plane_ref[at + 1, pl.ds(classes + h, mids, stride=classes), :]
            source_ref[h, at] = jnp.concatenate([here, later(here, after)], axis=0).astype(BF16)
        here, after = rim_rows(at), rim_rows(at + 1)
        rim_source_ref[at] = jnp.concatenate([here, later(here, after)], axis=0).astype(BF16)
    for at in (count, count + 1):
        for h in range(classes):
            source_ref[h, at] = zeros
        rim_source_ref[at] = zeros

    own_class = [sub16 % classes == h for h in range(classes)]

    def per_velocity(j, _):
        for at in range(count):
            base = [blocks_ref[(j * count + at) * classes + h] for h in range(classes)]
            total = energy = None
            for h in range(classes):
                index = jnp.broadcast_to(local_ref[j, at, h : h + 1, :], (16, LANES)).astype(
                    jnp.int16
                )
                low = jnp.broadcast_to(low_ref[j, at, h : h + 1, :], (8, LANES))
                high = jnp.broadcast_to(high_ref[j, at, h : h + 1, :], (8, LANES))
                inner = index & (LANES - 1)
                got = jnp.where(
                    index < LANES,
                    take_lanes(source_ref[h, base[h]], inner),
                    take_lanes(source_ref[h, base[h] + 1], inner),
                ).astype(F32)
                moved = low * got[:8] + high * got[8:]
                total = moved if total is None else total + moved
                energy = moved * moved if energy is None else energy + moved * moved
            sum_ref[at, pl.ds(j, mids, stride=vels), :] = total
            energy_ref[at, pl.ds(j, mids, stride=vels), :] = energy
            near = rim_source_ref[base[0]]
            far = rim_source_ref[base[0] + 1]
            for h in range(1, classes):
                near = jnp.where(own_class[h], rim_source_ref[base[h]], near)
                far = jnp.where(own_class[h], rim_source_ref[base[h] + 1], far)
            local = local_ref[j, at]
            index = jnp.concatenate([local, local], axis=0).astype(jnp.int16)
            inner = index & (LANES - 1)
            got = jnp.where(
                index < LANES, take_lanes(near, inner), take_lanes(far, inner)
            ).astype(F32)
            rim_ref[at, pl.ds(j, 8, stride=vels), :] = (
                low_ref[j, at] * got[:8] + high_ref[j, at] * got[8:]
            )
        return 0

    lax.fori_loop(0, vels, per_velocity, 0)

    shape = (mids, vels, LANES)
    rows = mids * vels
    edge = jnp.zeros(window_ref.shape[1:], BF16)
    window_ref[0] = edge
    window_ref[count + 1] = edge

    def three(low, mid, high):
        return jnp.concatenate([low, mid[:-1]], axis=0) + mid + jnp.concatenate([mid[1:], high], axis=0)

    def per_block(at, _):
        total = sum_ref[at].reshape(shape)
        rim = rim_ref[at].reshape(2, classes, vels, LANES)
        rim_sum = jnp.sum(rim, axis=1)
        rim_power = rim_sum * rim_sum
        rim_energy = jnp.sum(rim * rim, axis=1)
        power = three(rim_power[0:1], total * total, rim_power[1:2])
        energy = three(rim_energy[0:1], energy_ref[at].reshape(shape), rim_energy[1:2])
        both = jnp.concatenate([power.reshape(rows, LANES), energy.reshape(rows, LANES)], axis=0)
        top = both.astype(BF16)
        window_ref[at + 1, : 2 * rows] = top
        window_ref[at + 1, 2 * rows :] = (both - top.astype(F32)).astype(BF16)
        where = pl.ds(pl.multiple_of(at * LANES, LANES), LANES)
        for m in range(mids):
            stacked_ref[m, :, where] = (total[m] * scale_ref[m]).astype(BF16)
        return 0

    lax.fori_loop(0, count, per_block, 0)

    source = lax.broadcasted_iota(jnp.int32, (3 * LANES, LANES), 0) - LANES
    target = lax.broadcasted_iota(jnp.int32, (3 * LANES, LANES), 1)
    band = jnp.where(jnp.abs(source - target) <= HALF_WIN, 1.0, 0.0).astype(BF16)

    def per_window(at, _):
        wide = jnp.concatenate([window_ref[at], window_ref[at + 1], window_ref[at + 2]], axis=1)
        summed = jnp.dot(wide, band, preferred_element_type=F32)
        summed = summed[: 2 * rows] + summed[2 * rows :]
        numerator, denominator = summed[:rows], summed[rows:]
        where = pl.ds(pl.multiple_of(at * LANES, LANES), LANES)
        semblance = numerator / jnp.maximum(classes * denominator, 1.0)
        semblance_ref[:, :, where] = semblance.reshape(shape)
        return 0

    lax.fori_loop(0, count, per_window, 0)


def panels(rows, scale, blocks, local, low, high):
    vels, count, _, _ = local.shape
    classes = local.shape[2] // 2
    samples = rows.shape[1]
    rim = 2 * classes
    return pl.pallas_call(
        functools.partial(panel_kernel, classes, vels),
        in_specs=[SMEM, SMEM, VMEM, VMEM, VMEM, VMEM],
        out_specs=[VMEM, VMEM],
        out_shape=[
            jax.ShapeDtypeStruct((CMP_DEV, vels, samples), BF16),
            jax.ShapeDtypeStruct((CMP_DEV, vels, samples), F32),
        ],
        scratch_shapes=[
            pltpu.VMEM((count + 1, rows.shape[0], LANES), F32),
            pltpu.VMEM((classes, count + 2, 16, LANES), BF16),
            pltpu.VMEM((count + 2, 16, LANES), BF16),
            pltpu.VMEM((count, CMP_DEV * vels, LANES), F32),
            pltpu.VMEM((count, CMP_DEV * vels, LANES), F32),
            pltpu.VMEM((count, rim * vels, LANES), F32),
            pltpu.VMEM((count + 2, 4 * CMP_DEV * vels, LANES), BF16),
        ],
        compiler_params=pltpu.CompilerParams(vmem_limit_bytes=40 * 1024 * 1024),
        cost_estimate=pl.CostEstimate(
            flops=40 * CMP_DEV * vels * classes * samples,
            bytes_accessed=8 * 1024 * 1024,
            transcendentals=0,
        ),
    )(blocks, scale, rows, local, low, high)


def moveout(offsets, velocities, samples):
    count = samples // LANES
    slowness = offsets[None, :] / velocities[:, None]
    sample_time = jnp.arange(samples).astype(F32).reshape(1, count, 1, LANES)
    position = jnp.sqrt(sample_time * sample_time + (slowness * slowness)[:, None, :, None])
    floored = jnp.floor(position)
    fraction = position - floored
    sample_index = jnp.minimum(floored, float(samples)).astype(jnp.int32)
    blocks = jnp.min(sample_index, axis=-1) // LANES
    local = sample_index - (blocks * LANES)[..., None]
    low = lax.reduce_precision(1.0 - fraction, 8, 7)
    high = lax.reduce_precision(fraction, 8, 7)
    twice = [jnp.concatenate([v, v], axis=2) for v in (local, low, high)]
    return (blocks.reshape(-1), *twice)


def per_device(traces, owners, midpoint, offset_class, offsets, velocities):
    devices = lax.axis_size("inline") * lax.axis_size("xline")
    samples = traces.shape[1]
    classes = offsets.shape[0]
    key = (owners[:, 0] * CMP_DEV + midpoint) * classes + offset_class
    slots = jnp.arange(devices * CMP_DEV)
    counts = jnp.sum((key[:, None] // classes == slots[None, :]).astype(F32), axis=0)
    counts = lax.all_to_all(
        counts.reshape(devices, CMP_DEV), ("inline", "xline"), split_axis=0, concat_axis=0, tiled=True
    )
    scale = 1.0 / jnp.maximum(jnp.sum(counts, axis=0), 1.0)
    tables = moveout(offsets, velocities, samples)
    rows = exchange_rows(traces, key, classes)
    stacked, semblance = panels(rows, scale, *tables)
    return (stacked, semblance)


def solution(mesh):
    in_specs = (
        P(("inline", "xline"), None),
        P(("inline", "xline"), None),
        P(("inline", "xline")),
        P(("inline", "xline")),
        P(),
        P(),
    )
    out_specs = (P(("inline", "xline"), None, None), P(("inline", "xline"), None, None))
    return jax.shard_map(
        per_device, mesh=mesh, in_specs=in_specs, out_specs=out_specs, check_vma=False
    )
```

```python
import functools
import math

import jax
import jax.numpy as jnp
from jax import lax
from jax.experimental import pallas as pl
from jax.experimental.pallas import tpu as pltpu
from jax.sharding import PartitionSpec as P

HALF_WIN = 4
CMP_DEV = 8
LANES = 128
F32 = jnp.float32
BF16 = jnp.bfloat16
VMEM = pl.BlockSpec(memory_space=pltpu.VMEM)
SMEM = pl.BlockSpec(memory_space=pltpu.SMEM)

LANE_GATHER = lax.GatherDimensionNumbers(
    offset_dims=(),
    collapsed_slice_dims=(1,),
    start_index_map=(1,),
    operand_batching_dims=(0,),
    start_indices_batching_dims=(0,),
)


def take_lanes(rows, index):
    return lax.gather(
        rows,
        index[..., None],
        LANE_GATHER,
        (1, 1),
        mode=lax.GatherScatterMode.PROMISE_IN_BOUNDS,
    )


def bin_kernel(kept_rows, member_ref, *refs):
    *data, kept_ref, sent_ref = refs
    per, cols = data[0].shape
    tile = math.gcd(cols, 256)
    for start in range(0, cols, tile):
        where = slice(start, start + tile)
        total = None
        for at, block in enumerate(data):
            part = jnp.dot(
                member_ref[:, at * per : (at + 1) * per],
                block[:, where],
                preferred_element_type=F32,
            )
            total = part if total is None else total + part
        kept_ref[:, where] = total[:kept_rows]
        if kept_rows < total.shape[0]:
            sent_ref[:, where] = total[kept_rows:].astype(BF16)
        else:
            sent_ref[:, where] = jnp.zeros((sent_ref.shape[0], tile), BF16)


def bin_rows(member, data, starts, cols, kept_rows):
    rows = member.shape[0]
    per = data[0].shape[0]
    sent_rows = max(rows - kept_rows, 16)
    in_specs = [pl.BlockSpec(member.shape, lambda t: (0, 0))]
    for start in starts:
        in_specs.append(pl.BlockSpec((per, cols), lambda t, s=start // cols: (0, s)))
    return pl.pallas_call(
        functools.partial(bin_kernel, kept_rows),
        grid=(1,),
        in_specs=in_specs,
        out_specs=[
            pl.BlockSpec((kept_rows, cols), lambda t: (0, 0)),
            pl.BlockSpec((sent_rows, cols), lambda t: (0, 0)),
        ],
        out_shape=[
            jax.ShapeDtypeStruct((kept_rows, cols), F32),
            jax.ShapeDtypeStruct((sent_rows, cols), BF16),
        ],
        compiler_params=pltpu.CompilerParams(vmem_limit_bytes=40 * 1024 * 1024),
        cost_estimate=pl.CostEstimate(
            flops=2 * rows * len(data) * per * cols,
            bytes_accessed=2 * len(data) * per * cols + 6 * rows * cols,
            transcendentals=0,
        ),
    )(member, *data)


class Plan:
    def __init__(self, traces, key, classes):
        self.inline = lax.axis_size("inline")
        self.xline = lax.axis_size("xline")
        self.me = lax.axis_index("inline")
        self.me_x = lax.axis_index("xline")
        self.classes = classes
        self.traces = traces
        self.dev_rows = CMP_DEV * classes
        self.line_rows = self.xline * self.dev_rows
        self.block_rows = -(-(self.line_rows + 2 * classes) // 16) * 16
        bits = [1 << b for b in range(self.inline.bit_length() - 1)]
        self.core, others = bits[0], bits[1:]
        self.orders = [others, others[::-1]] if len(others) > 1 else [others]
        self.mate = self.swap(traces, self.core)
        pair = jnp.stack([key, self.swap(key, self.core)])
        self.keys = []
        for order in self.orders:
            keys = [pair] + [self.swap(pair, bit) for bit in order[:1]]
            self.keys.append(jnp.concatenate(keys).reshape(-1))
        self.members = [self.member(at) for at in range(len(self.orders))]

    def swap(self, value, bit):
        return lax.ppermute(value, "inline", [(i, i ^ bit) for i in range(self.inline)])

    def code_of(self, at, target):
        order = self.orders[at]
        apart = target ^ self.me
        code = jnp.zeros_like(target)
        done = self.core
        for place, bit in enumerate(order):
            if place:
                code = code * 2 + jnp.where(apart & bit != 0, 1, 0)
            else:
                done |= bit
        valid = (apart & done == 0) & (target >= 0) & (target < self.inline)
        return jnp.where(valid, code, -1)

    def codes(self, at):
        return 1 << max(len(self.orders[at]) - 1, 0)

    def member(self, at):
        keys = self.keys[at]
        classes, line_rows = self.classes, self.line_rows
        line, local = keys // line_rows, keys % line_rows

        def row_of(target, row):
            code = self.code_of(at, target)
            return jnp.where(code >= 0, code * self.block_rows + row, -1)

        own = row_of(line, local + classes)
        rim = jnp.where(
            local >= line_rows - classes,
            row_of(line + 1, local - (line_rows - classes)),
            jnp.where(local < classes, row_of(line - 1, local + classes + line_rows), -1),
        )
        row = jnp.arange(self.codes(at) * self.block_rows)[:, None]
        return ((row == own[None, :]) | (row == rim[None, :])).astype(BF16)

    def reduce_lines(self, at, kept, sent):
        for place, bit in enumerate(self.orders[at][1:]):
            if place:
                half = kept.shape[0] // 2
                kept, sent = kept[:half], kept[half:].astype(sent.dtype)
            kept = kept + self.swap(sent, bit).astype(F32)
        return kept

    def reduce_xline(self, total, sent, stride, window):
        power_of_two = self.xline & (self.xline - 1) == 0
        result = lax.dynamic_slice_in_dim(total, self.me_x * stride, window, 0)
        for step in range(self.xline - 1, 0, -1):
            if power_of_two:
                target = self.me_x ^ step
                pairs = [(i, i ^ step) for i in range(self.xline)]
            else:
                target = (self.me_x + step) % self.xline
                pairs = [(i, (i + step) % self.xline) for i in range(self.xline)]
            block = lax.dynamic_slice_in_dim(sent, target * stride, window, 0)
            result = result + lax.ppermute(block, "xline", pairs).astype(F32)
        return result

    def raw(self, start, cols):
        width = cols // len(self.orders)
        parts = []
        for at, order in enumerate(self.orders):
            begin = start + at * width
            data, starts = [self.traces, self.mate], [begin, begin]
            if order:
                far = self.swap(lax.slice_in_dim(self.traces, begin, begin + width, axis=1), order[0])
                data += [far, self.swap(far, self.core)]
                starts += [0, 0]
            parts.append((data, starts, width))
        return parts

    def rows(self, parts):
        totals = []
        for at, (data, starts, width) in enumerate(parts):
            rows = self.members[at].shape[0]
            kept_rows = rows // 2 if len(self.orders[at]) > 1 else rows
            kept, sent = bin_rows(self.members[at], data, starts, width, kept_rows)
            totals.append(self.reduce_lines(at, kept, sent))
        total = jnp.concatenate(totals, axis=1) if len(totals) > 1 else totals[0]
        window = self.dev_rows + 2 * self.classes
        return self.reduce_xline(total, total.astype(BF16), self.dev_rows, window)

    def fold(self):
        keys = self.keys[0]
        line, local = keys // self.line_rows, keys % self.line_rows
        slots = self.xline * CMP_DEV
        code = self.code_of(0, line)
        slot = jnp.where(code >= 0, code * slots + local // self.classes, -1)
        every = jnp.arange(self.codes(0) * slots)
        counts = jnp.sum((slot[None, :] == every[:, None]).astype(F32), axis=1)
        half = counts.shape[0] // 2 if self.codes(0) > 1 else counts.shape[0]
        counts = self.reduce_lines(0, counts[:half], counts[half:])
        return self.reduce_xline(counts, counts, CMP_DEV, CMP_DEV)


def panel_kernel(classes, vels, first, last, count, chunks, *refs):
    blocks_ref, scale_ref = refs[:2]
    rows_refs = refs[2 : 2 + chunks]
    local_ref, low_ref, high_ref = refs[2 + chunks : 5 + chunks]
    at = 5 + chunks
    if last < count:
        later_ref = refs[at]
        at += 3
    stacked_out, semblance_out = refs[at : at + 2]
    at += 2
    if first > 0:
        carry_ref = refs[at]
        at += 1
    (
        plane_ref,
        source_ref,
        rim_source_ref,
        sum_ref,
        energy_ref,
        rim_ref,
        window_ref,
        stacked_ref,
        semblance_ref,
        copies,
    ) = refs[at:]
    mids = CMP_DEV
    span = last - first
    held = count - first
    lane = lax.broadcasted_iota(jnp.int32, (8, LANES), 1)
    sub = lax.broadcasted_iota(jnp.int32, (8, LANES), 0)
    sub16 = lax.broadcasted_iota(jnp.int32, (16, LANES), 0)

    block_at = 0
    for rows_ref in rows_refs:
        for inner in range(rows_ref.shape[1] // LANES):
            block = rows_ref[:, inner * LANES : (inner + 1) * LANES]
            plane_ref[block_at] = block.astype(BF16).astype(F32)
            block_at += 1
    plane_ref[held] = jnp.zeros(plane_ref.shape[1:], F32)

    def later(here, after):
        return jnp.where(
            lane == LANES - 1,
            pltpu.roll(after, LANES - 1, 1),
            pltpu.roll(here, LANES - 1, 1),
        )

    def rim_rows(at):
        return jnp.where(
            sub < classes, plane_ref[at, 0:8, :], plane_ref[at, mids * classes : mids * classes + 8, :]
        )

    zeros = jnp.zeros((16, LANES), BF16)
    for at in range(held):
        for h in range(classes):
            here = plane_ref[at, pl.ds(classes + h, mids, stride=classes), :]
            after = plane_ref[at + 1, pl.ds(classes + h, mids, stride=classes), :]
            source_ref[h, at] = jnp.concatenate([here, later(here, after)], axis=0).astype(BF16)
        here, after = rim_rows(at), rim_rows(at + 1)
        rim_source_ref[at] = jnp.concatenate([here, later(here, after)], axis=0).astype(BF16)
    for at in (held, held + 1):
        for h in range(classes):
            source_ref[h, at] = zeros
        rim_source_ref[at] = zeros

    own_class = [sub16 % classes == h for h in range(classes)]
    group = 2 * classes

    def per_velocity(j, _):
        for at in range(span):
            where = slice(at * LANES, (at + 1) * LANES)
            base = [blocks_ref[(j * classes + h) * count + first + at] - first for h in range(classes)]
            total = energy = None
            for h in range(classes):
                row = slice(h, h + 1)
                index = jnp.broadcast_to(local_ref[j, row, where], (16, LANES)).astype(jnp.int16)
                low = jnp.broadcast_to(low_ref[j, row, where], (8, LANES))
                high = jnp.broadcast_to(high_ref[j, row, where], (8, LANES))
                inner = index & (LANES - 1)
                got = jnp.where(
                    index < LANES,
                    take_lanes(source_ref[h, base[h]], inner),
                    take_lanes(source_ref[h, base[h] + 1], inner),
                ).astype(F32)
                moved = low * got[:8] + high * got[8:]
                total = moved if total is None else total + moved
                energy = moved * moved if energy is None else energy + moved * moved
            sum_ref[at, pl.ds(j, mids, stride=vels), :] = total
            energy_ref[at, pl.ds(j, mids, stride=vels), :] = energy
            near = rim_source_ref[base[0]]
            far = rim_source_ref[base[0] + 1]
            for h in range(1, classes):
                near = jnp.where(own_class[h], rim_source_ref[base[h]], near)
                far = jnp.where(own_class[h], rim_source_ref[base[h] + 1], far)
            local = local_ref[j, :, where]
            index = jnp.concatenate([local, local], axis=0).astype(jnp.int16)
            inner = index & (LANES - 1)
            got = jnp.where(
                index < LANES, take_lanes(near, inner), take_lanes(far, inner)
            ).astype(F32)
            rim_ref[at, pl.ds(j, group, stride=vels), :] = (
                low_ref[j, :, where] * got[:8] + high_ref[j, :, where] * got[8:]
            )
        return 0

    lax.fori_loop(0, vels, per_velocity, 0)

    shape = (mids, vels, LANES)
    rows = mids * vels
    edge = jnp.zeros(window_ref.shape[1:], BF16)
    window_ref[0] = edge
    if last < count:
        window_ref[span + 1] = later_ref[0]
        window_ref[span + 2] = later_ref[1]
    else:
        window_ref[span + 1] = edge

    def three(low, mid, high):
        return jnp.concatenate([low, mid[:-1]], axis=0) + mid + jnp.concatenate([mid[1:], high], axis=0)

    def per_block(at, _):
        total = sum_ref[at].reshape(shape)
        rim = rim_ref[at].reshape(2, classes, vels, LANES)
        rim_sum = jnp.sum(rim, axis=1)
        rim_power = rim_sum * rim_sum
        rim_energy = jnp.sum(rim * rim, axis=1)
        power = three(rim_power[0:1], total * total, rim_power[1:2])
        energy = three(rim_energy[0:1], energy_ref[at].reshape(shape), rim_energy[1:2])
        window_ref[at + 1, :rows] = power.reshape(rows, LANES).astype(BF16)
        window_ref[at + 1, rows:] = energy.reshape(rows, LANES).astype(BF16)
        where = pl.ds(pl.multiple_of(at * LANES, LANES), LANES)
        for m in range(mids):
            stacked_ref[m, :, where] = (total[m] * scale_ref[m]).astype(BF16)
        return 0

    lax.fori_loop(0, span, per_block, 0)
    stacked_copy = pltpu.make_async_copy(
        stacked_ref, stacked_out.at[:, :, first * LANES : last * LANES], copies.at[0]
    )
    stacked_copy.start()

    def band(blocks):
        shape = ((blocks + 2) * LANES, blocks * LANES)
        source = lax.broadcasted_iota(jnp.int32, shape, 0) - LANES
        target = lax.broadcasted_iota(jnp.int32, shape, 1)
        return jnp.where(jnp.abs(source - target) <= HALF_WIN, 1.0, 0.0).astype(BF16)

    begin = 0 if first == 0 else 1
    end = span + 1 if last < count else span
    wide = band(2)
    narrow = band(1)
    at = begin
    while at < end:
        blocks = min(2, end - at)
        values = jnp.concatenate([window_ref[at + i] for i in range(blocks + 2)], axis=1)
        summed = jnp.dot(values, wide if blocks == 2 else narrow, preferred_element_type=F32)
        semblance = summed[:rows] / jnp.maximum(classes * summed[rows:], 1.0)
        semblance_ref[:, :, (at - begin) * LANES : (at - begin + blocks) * LANES] = semblance.reshape(
            mids, vels, blocks * LANES
        )
        at += blocks
    semblance_copy = pltpu.make_async_copy(
        semblance_ref,
        semblance_out.at[:, :, (first + begin) * LANES : (first + end) * LANES],
        copies.at[1],
    )
    semblance_copy.start()
    if first > 0:
        carry_ref[0] = window_ref[1]
        carry_ref[1] = window_ref[2]
    stacked_copy.wait()
    semblance_copy.wait()


def panels(first, last, count, classes, vels, scale, blocks, tables, rows, later):
    span = last - first
    held = count - first
    samples = count * LANES
    group = 2 * classes
    window_rows = 2 * CMP_DEV * vels
    done = span - (first > 0) + (last < count)
    outs = [
        jax.ShapeDtypeStruct((CMP_DEV, vels, samples), BF16),
        jax.ShapeDtypeStruct((CMP_DEV, vels, samples), F32),
    ]
    specs = [pl.BlockSpec(memory_space=pl.ANY)] * 2
    if first > 0:
        outs.append(jax.ShapeDtypeStruct((2, window_rows, LANES), BF16))
        specs.append(VMEM)
    operands = [blocks, scale, *rows, *tables]
    in_specs = [SMEM, SMEM] + [VMEM] * (len(rows) + len(tables))
    aliases = {}
    if later is not None:
        stacked, semblance, carry = later
        aliases = {len(operands) + 1: 0, len(operands) + 2: 1}
        operands += [carry, stacked, semblance]
        in_specs += [VMEM, pl.BlockSpec(memory_space=pl.ANY), pl.BlockSpec(memory_space=pl.ANY)]
    return pl.pallas_call(
        functools.partial(panel_kernel, classes, vels, first, last, count, len(rows)),
        in_specs=in_specs,
        out_specs=specs,
        out_shape=outs,
        input_output_aliases=aliases,
        scratch_shapes=[
            pltpu.VMEM((held + 1, rows[0].shape[0], LANES), F32),
            pltpu.VMEM((classes, held + 2, 16, LANES), BF16),
            pltpu.VMEM((held + 2, 16, LANES), BF16),
            pltpu.VMEM((span, CMP_DEV * vels, LANES), F32),
            pltpu.VMEM((span, CMP_DEV * vels, LANES), F32),
            pltpu.VMEM((span, group * vels, LANES), F32),
            pltpu.VMEM((span + 3, window_rows, LANES), BF16),
            pltpu.VMEM((CMP_DEV, vels, span * LANES), BF16),
            pltpu.VMEM((CMP_DEV, vels, done * LANES), F32),
            pltpu.SemaphoreType.DMA((2,)),
        ],
        compiler_params=pltpu.CompilerParams(vmem_limit_bytes=40 * 1024 * 1024),
        cost_estimate=pl.CostEstimate(
            flops=40 * CMP_DEV * vels * classes * span * LANES,
            bytes_accessed=(1 + span) * 512 * 1024,
            transcendentals=0,
        ),
    )(*operands)


def first_blocks(offsets, velocities, count):
    slowness = (offsets[None, :] / velocities[:, None]).reshape(-1, 1)
    sample_time = (jnp.arange(count) * LANES).astype(F32)[None, :]
    position = jnp.sqrt(sample_time * sample_time + slowness * slowness)
    index = jnp.floor(position - 0.01).astype(jnp.int32)
    return jnp.minimum(index, count * LANES) // LANES


def moveout(offsets, velocities, blocks, samples, start, stop):
    vels, classes = velocities.shape[0], offsets.shape[0]
    slowness = offsets[None, :] / velocities[:, None]
    slowness = jnp.concatenate([slowness, slowness], axis=1).reshape(-1, 1)
    sample_time = jnp.arange(start, stop).astype(F32)[None, :]
    position = jnp.sqrt(sample_time * sample_time + slowness * slowness)
    floored = jnp.floor(position)
    fraction = position - floored
    sample_index = jnp.minimum(floored, float(samples)).astype(jnp.int32)
    base = blocks.reshape(vels, classes, -1)[:, :, start // LANES : stop // LANES] * LANES
    base = jnp.concatenate([base, base], axis=1).reshape(vels * 2 * classes, -1)
    local = sample_index - jnp.repeat(base, LANES, axis=1)
    low = lax.reduce_precision(1.0 - fraction, 8, 7)
    high = lax.reduce_precision(fraction, 8, 7)
    return [v.reshape(vels, 2 * classes, stop - start) for v in (local, low, high)]


def per_device(traces, owners, midpoint, offset_class, offsets, velocities):
    samples = traces.shape[1]
    classes, vels = offsets.shape[0], velocities.shape[0]
    count = samples // LANES
    key = (owners[:, 0] * CMP_DEV + midpoint) * classes + offset_class
    plan = Plan(traces, key, classes)
    cuts = [0, samples // 2, samples]
    chunks = list(zip(cuts[:-1], cuts[1:]))[::-1]
    raw = [plan.raw(start, stop - start) for start, stop in chunks]
    scale = 1.0 / jnp.maximum(plan.fold(), 1.0)
    blocks = first_blocks(offsets, velocities, count)
    rows = []
    out = None
    for (start, stop), parts in zip(chunks, raw):
        tables = moveout(offsets, velocities, blocks, samples, start, stop)
        rows.insert(0, plan.rows(parts))
        out = panels(
            start // LANES,
            stop // LANES,
            count,
            classes,
            vels,
            scale,
            blocks.reshape(-1),
            tables,
            rows,
            out,
        )
    return (out[0], out[1])


def solution(mesh):
    in_specs = (
        P(("inline", "xline"), None),
        P(("inline", "xline"), None),
        P(("inline", "xline")),
        P(("inline", "xline")),
        P(),
        P(),
    )
    out_specs = (P(("inline", "xline"), None, None), P(("inline", "xline"), None, None))
    return jax.shard_map(
        per_device, mesh=mesh, in_specs=in_specs, out_specs=out_specs, check_vma=False
    )
```

```python
import functools
import math

import jax
import jax.numpy as jnp
from jax import lax
from jax.experimental import pallas as pl
from jax.experimental.pallas import tpu as pltpu
from jax.sharding import PartitionSpec as P

HALF_WIN = 4
CMP_DEV = 8
LANES = 128
VMEM_BYTES = 16 * 1024 * 1024
F32 = jnp.float32
BF16 = jnp.bfloat16
VMEM = pl.BlockSpec(memory_space=pltpu.VMEM)
SMEM = pl.BlockSpec(memory_space=pltpu.SMEM)
ANY = pl.BlockSpec(memory_space=pl.ANY)
TOKEN = jax.ShapeDtypeStruct((8, LANES), F32)

LANE_GATHER = lax.GatherDimensionNumbers(
    offset_dims=(),
    collapsed_slice_dims=(1,),
    start_index_map=(1,),
    operand_batching_dims=(0,),
    start_indices_batching_dims=(0,),
)


def take_lanes(rows, index):
    return lax.gather(
        rows,
        index[..., None],
        LANE_GATHER,
        (1, 1),
        mode=lax.GatherScatterMode.PROMISE_IN_BOUNDS,
    )


def bin_kernel(kept_rows, width, count, member_ref, *refs):
    data, (kept_ref, sent_ref, token_ref) = refs[:count], refs[-3:]
    token_ref[...] = jnp.zeros(token_ref.shape, F32)
    per = data[0].shape[0]
    cols = kept_ref.shape[1]
    tile = math.gcd(width, 256)
    for start in range(0, cols, tile):
        where = slice(start, min(start + tile, cols))
        total = None
        for at, block in enumerate(data):
            values = block[:, where] if start < width else jnp.ones((per, cols - width), BF16)
            part = jnp.dot(
                member_ref[:, at * per : (at + 1) * per], values, preferred_element_type=F32
            )
            total = part if total is None else total + part
        kept_ref[:, where] = total[:kept_rows]
        if kept_rows < total.shape[0]:
            sent_ref[:, where] = total[kept_rows:].astype(BF16)
        else:
            sent_ref[:, where] = jnp.zeros((sent_ref.shape[0], total.shape[1]), BF16)


def bin_rows(member, data, start, width, counted, kept_rows, after):
    rows = member.shape[0]
    per = data[0].shape[0]
    cols = width + (LANES if counted else 0)
    sent_rows = max(rows - kept_rows, 16)
    in_specs = [pl.BlockSpec(member.shape, lambda t: (0, 0))]
    in_specs += [pl.BlockSpec((per, width), lambda t: (0, start // width))] * len(data)
    in_specs += [ANY] * len(after)
    return pl.pallas_call(
        functools.partial(bin_kernel, kept_rows, width, len(data)),
        grid=(1,),
        in_specs=in_specs,
        out_specs=[
            pl.BlockSpec((kept_rows, cols), lambda t: (0, 0)),
            pl.BlockSpec((sent_rows, cols), lambda t: (0, 0)),
            pl.BlockSpec(TOKEN.shape, lambda t: (0, 0)),
        ],
        out_shape=[
            jax.ShapeDtypeStruct((kept_rows, cols), F32),
            jax.ShapeDtypeStruct((sent_rows, cols), BF16),
            TOKEN,
        ],
        compiler_params=pltpu.CompilerParams(vmem_limit_bytes=VMEM_BYTES),
        cost_estimate=pl.CostEstimate(
            flops=2 * rows * len(data) * per * cols,
            bytes_accessed=2 * len(data) * per * cols + 6 * rows * cols,
            transcendentals=0,
        ),
    )(member, *data, *after)


class Plan:
    def __init__(self, traces, key, classes):
        self.inline = lax.axis_size("inline")
        self.xline = lax.axis_size("xline")
        self.me = lax.axis_index("inline")
        self.me_x = lax.axis_index("xline")
        self.classes = classes
        self.dev_rows = CMP_DEV * classes
        self.line_rows = self.xline * self.dev_rows
        bits = [1 << b for b in range(self.inline.bit_length() - 1)]
        self.core, others = bits[0], bits[1:]
        self.orders = [others, others[::-1]] if len(others) > 1 else [others]
        self.codes = 1 << len(others)
        unit = 8 if self.codes % 4 == 0 else 16
        self.block_rows = -(-(self.line_rows + 2 * classes) // unit) * unit
        self.data = [traces, self.swap(traces, self.core)]
        self.keys = jnp.concatenate([key, self.swap(key, self.core)])
        self.members = [self.member(order) for order in self.orders]
        places = [self.me_x] + [target for target, _ in self.targets()]
        self.places = jnp.stack(places) * self.dev_rows

    def swap(self, value, bit):
        return lax.ppermute(value, "inline", [(i, i ^ bit) for i in range(self.inline)])

    def member(self, order):
        classes, line_rows = self.classes, self.line_rows
        line, local = self.keys // line_rows, self.keys % line_rows

        def row_of(target, row):
            apart = target ^ self.me
            code = jnp.zeros_like(target)
            for bit in order:
                code = code * 2 + jnp.where(apart & bit != 0, 1, 0)
            valid = (apart & self.core == 0) & (target >= 0) & (target < self.inline)
            return jnp.where(valid, code * self.block_rows + row, -1)

        own = row_of(line, local + classes)
        rim = jnp.where(
            local >= line_rows - classes,
            row_of(line + 1, local - (line_rows - classes)),
            jnp.where(local < classes, row_of(line - 1, local + classes + line_rows), -1),
        )
        row = jnp.arange(self.codes * self.block_rows)[:, None]
        return ((row == own[None, :]) | (row == rim[None, :])).astype(BF16)

    def bin(self, start, cols, counted, after):
        width = cols // len(self.orders)
        rows = self.codes * self.block_rows
        parts = []
        for at, order in enumerate(self.orders):
            count_here = counted and at == len(self.orders) - 1
            parts.append(
                bin_rows(
                    self.members[at],
                    self.data,
                    start + at * width,
                    width,
                    count_here,
                    rows // 2 if order else rows,
                    after,
                )
            )
        return parts

    def exchange(self, place, parts):
        return [
            (kept, self.swap(sent, order[place])) for order, (kept, sent, *_) in zip(self.orders, parts)
        ]

    def targets(self):
        steps = []
        for step in range(self.xline - 1, 0, -1):
            if self.xline & (self.xline - 1) == 0:
                target = self.me_x ^ step
                pairs = [(i, i ^ step) for i in range(self.xline)]
            else:
                target = (self.me_x + step) % self.xline
                pairs = [(i, (i + step) % self.xline) for i in range(self.xline)]
            steps.append((target, pairs))
        return steps

    def merge(self, parts, after):
        half = parts[0][0].shape[0] // 2
        shapes = []
        for kept, _ in parts:
            shapes.append(jax.ShapeDtypeStruct((half, kept.shape[1]), F32))
            shapes.append(jax.ShapeDtypeStruct((half, kept.shape[1]), BF16))
        flat = [value for part in parts for value in part]
        outs = pl.pallas_call(
            functools.partial(merge_kernel, len(parts)),
            in_specs=[VMEM] * len(flat) + [ANY] * len(after),
            out_specs=[VMEM] * (len(shapes) + 1),
            out_shape=shapes + [TOKEN],
            compiler_params=pltpu.CompilerParams(vmem_limit_bytes=VMEM_BYTES),
            cost_estimate=cost_of(flat),
        )(*flat, *after)
        return list(zip(outs[0:-1:2], outs[1:-1:2])), outs[-1]

    def spread(self, parts, after):
        window = self.dev_rows + 2 * self.classes
        cols = sum(kept.shape[1] for kept, _ in parts)
        flat = [value for part in parts for value in part]
        kinds = [F32] + [BF16] * (self.xline - 1)
        return pl.pallas_call(
            functools.partial(spread_kernel, len(parts), len(kinds)),
            in_specs=[SMEM] + [VMEM] * len(flat) + [ANY] * len(after),
            out_specs=[VMEM] * (len(kinds) + 1),
            out_shape=[jax.ShapeDtypeStruct((window, cols), kind) for kind in kinds] + [TOKEN],
            scratch_shapes=[pltpu.VMEM((parts[0][0].shape[0], cols), F32)],
            compiler_params=pltpu.CompilerParams(vmem_limit_bytes=VMEM_BYTES),
            cost_estimate=cost_of(flat),
        )(self.places, *flat, *after)

    def across(self, blocks):
        own, *sent = blocks
        return [own] + [
            lax.ppermute(block, "xline", pairs) for block, (_, pairs) in zip(sent, self.targets())
        ]


def cost_of(values):
    size = sum(value.size * value.dtype.itemsize for value in values)
    return pl.CostEstimate(flops=0, bytes_accessed=2 * size, transcendentals=0)


def merge_kernel(count, *refs):
    ins, outs, token_ref = refs[: 2 * count], refs[-2 * count - 1 : -1], refs[-1]
    token_ref[...] = jnp.zeros(token_ref.shape, F32)
    for at in range(count):
        kept, sent = ins[2 * at : 2 * at + 2]
        half = kept.shape[0] // 2
        total = kept[...] + sent[...].astype(F32)
        outs[2 * at][...] = total[:half]
        outs[2 * at + 1][...] = total[half:].astype(BF16)


def spread_kernel(count, blocks, places_ref, *refs):
    ins, outs, token_ref, total_ref = refs[: 2 * count], refs[-blocks - 2 : -2], refs[-2], refs[-1]
    token_ref[...] = jnp.zeros(token_ref.shape, F32)
    start = 0
    for at in range(count):
        kept, sent = ins[2 * at : 2 * at + 2]
        stop = start + kept.shape[1]
        total_ref[:, start:stop] = kept[...] + sent[...].astype(F32)
        start = stop
    for at, out in enumerate(outs):
        place = pl.multiple_of(places_ref[at], 8)
        out[...] = total_ref[pl.ds(place, out.shape[0]), :].astype(out.dtype)


def panel_kernel(classes, vels, first, last, count, pieces, waits, *refs):
    blocks_ref = refs[0]
    at = 1
    chunk_refs = []
    for number in pieces:
        chunk_refs.append(refs[at : at + number])
        at += number
    local_ref, low_ref, high_ref = refs[at : at + 3]
    at += 3 + waits
    if last < count:
        later_ref = refs[at]
        at += 3
    stacked_out, semblance_out = refs[at : at + 2]
    at += 2
    if first > 0:
        carry_ref = refs[at]
        at += 1
    (
        plane_ref,
        source_ref,
        rim_source_ref,
        sum_ref,
        energy_ref,
        rim_ref,
        window_ref,
        scale_ref,
        stacked_ref,
        semblance_ref,
        copies,
    ) = refs[at:]
    mids = CMP_DEV
    span = last - first
    held = count - first
    lane = lax.broadcasted_iota(jnp.int32, (8, LANES), 1)
    sub = lax.broadcasted_iota(jnp.int32, (8, LANES), 0)
    sub16 = lax.broadcasted_iota(jnp.int32, (16, LANES), 0)

    block_at = 0
    for piece_refs in chunk_refs:
        for inner in range(piece_refs[0].shape[1] // LANES):
            where = slice(inner * LANES, (inner + 1) * LANES)
            block = piece_refs[0][:, where]
            for piece_ref in piece_refs[1:]:
                block = block + piece_ref[:, where].astype(F32)
            plane_ref[block_at] = block.astype(BF16).astype(F32) if block_at < held else block
            block_at += 1
    fold = None
    for h in range(classes):
        counts = plane_ref[held, pl.ds(classes + h, mids, stride=classes), :]
        fold = counts if fold is None else fold + counts
    scale_ref[...] = 1.0 / jnp.maximum(fold, 1.0)
    plane_ref[held] = jnp.zeros(plane_ref.shape[1:], F32)

    def later(here, after):
        return jnp.where(
            lane == LANES - 1,
            pltpu.roll(after, LANES - 1, 1),
            pltpu.roll(here, LANES - 1, 1),
        )

    def rim_rows(at):
        return jnp.where(
            sub < classes, plane_ref[at, 0:8, :], plane_ref[at, mids * classes : mids * classes + 8, :]
        )

    zeros = jnp.zeros((16, LANES), BF16)
    for at in range(held):
        for h in range(classes):
            here = plane_ref[at, pl.ds(classes + h, mids, stride=classes), :]
            after = plane_ref[at + 1, pl.ds(classes + h, mids, stride=classes), :]
            source_ref[h, at] = jnp.concatenate([here, later(here, after)], axis=0).astype(BF16)
        here, after = rim_rows(at), rim_rows(at + 1)
        rim_source_ref[at] = jnp.concatenate([here, later(here, after)], axis=0).astype(BF16)
    for at in (held, held + 1):
        for h in range(classes):
            source_ref[h, at] = zeros
        rim_source_ref[at] = zeros

    own_class = [sub16 % classes == h for h in range(classes)]
    group = 2 * classes

    def per_velocity(j, _):
        for at in range(span):
            where = slice(at * LANES, (at + 1) * LANES)
            base = [blocks_ref[h, j * span + at] - first for h in range(classes)]
            total = energy = None
            for h in range(classes):
                row = slice(h, h + 1)
                index = jnp.broadcast_to(local_ref[j, row, where], (16, LANES)).astype(jnp.int16)
                low = jnp.broadcast_to(low_ref[j, row, where], (8, LANES))
                high = jnp.broadcast_to(high_ref[j, row, where], (8, LANES))
                inner = index & (LANES - 1)
                got = jnp.where(
                    index < LANES,
                    take_lanes(source_ref[h, base[h]], inner),
                    take_lanes(source_ref[h, base[h] + 1], inner),
                ).astype(F32)
                moved = low * got[:8] + high * got[8:]
                total = moved if total is None else total + moved
                energy = moved * moved if energy is None else energy + moved * moved
            sum_ref[at, pl.ds(j, mids, stride=vels), :] = total
            energy_ref[at, pl.ds(j, mids, stride=vels), :] = energy
            near = rim_source_ref[base[0]]
            far = rim_source_ref[base[0] + 1]
            for h in range(1, classes):
                near = jnp.where(own_class[h], rim_source_ref[base[h]], near)
                far = jnp.where(own_class[h], rim_source_ref[base[h] + 1], far)
            local = local_ref[j, :, where]
            index = jnp.concatenate([local, local], axis=0).astype(jnp.int16)
            inner = index & (LANES - 1)
            got = jnp.where(
                index < LANES, take_lanes(near, inner), take_lanes(far, inner)
            ).astype(F32)
            rim_ref[at, pl.ds(j, group, stride=vels), :] = (
                low_ref[j, :, where] * got[:8] + high_ref[j, :, where] * got[8:]
            )
        return 0

    lax.fori_loop(0, vels, per_velocity, 0, unroll=2)

    shape = (mids, vels, LANES)
    rows = mids * vels
    edge = jnp.zeros(window_ref.shape[1:], BF16)
    window_ref[0] = edge
    if last < count:
        window_ref[span + 1] = later_ref[0]
        window_ref[span + 2] = later_ref[1]
    else:
        window_ref[span + 1] = edge

    def three(low, mid, high):
        return jnp.concatenate([low, mid[:-1]], axis=0) + mid + jnp.concatenate([mid[1:], high], axis=0)

    def per_block(at, _):
        total = sum_ref[at].reshape(shape)
        rim = rim_ref[at].reshape(2, classes, vels, LANES)
        rim_sum = jnp.sum(rim, axis=1)
        rim_power = rim_sum * rim_sum
        rim_energy = jnp.sum(rim * rim, axis=1)
        power = three(rim_power[0:1], total * total, rim_power[1:2])
        energy = three(rim_energy[0:1], energy_ref[at].reshape(shape), rim_energy[1:2])
        window_ref[at + 1, :rows] = power.reshape(rows, LANES).astype(BF16)
        window_ref[at + 1, rows:] = energy.reshape(rows, LANES).astype(BF16)
        where = pl.ds(pl.multiple_of(at * LANES, LANES), LANES)
        for m in range(mids):
            stacked_ref[m, :, where] = (total[m] * scale_ref[m : m + 1, :]).astype(BF16)
        return 0

    lax.fori_loop(0, span, per_block, 0)
    stacked_copy = pltpu.make_async_copy(
        stacked_ref, stacked_out.at[:, :, first * LANES : last * LANES], copies.at[0]
    )
    stacked_copy.start()

    def band(blocks):
        shape = ((blocks + 2) * LANES, blocks * LANES)
        source = lax.broadcasted_iota(jnp.int32, shape, 0) - LANES
        target = lax.broadcasted_iota(jnp.int32, shape, 1)
        return jnp.where(jnp.abs(source - target) <= HALF_WIN, 1.0, 0.0).astype(BF16)

    begin = 0 if first == 0 else 1
    end = span + 1 if last < count else span
    wide = band(2)
    narrow = band(1)
    at = begin
    while at < end:
        blocks = min(2, end - at)
        values = jnp.concatenate([window_ref[at + i] for i in range(blocks + 2)], axis=1)
        summed = jnp.dot(values, wide if blocks == 2 else narrow, preferred_element_type=F32)
        semblance = summed[:rows] / jnp.maximum(classes * summed[rows:], 1.0)
        semblance_ref[:, :, (at - begin) * LANES : (at - begin + blocks) * LANES] = semblance.reshape(
            mids, vels, blocks * LANES
        )
        at += blocks
    semblance_copy = pltpu.make_async_copy(
        semblance_ref,
        semblance_out.at[:, :, (first + begin) * LANES : (first + end) * LANES],
        copies.at[1],
    )
    semblance_copy.start()
    if first > 0:
        carry_ref[0] = window_ref[1]
        carry_ref[1] = window_ref[2]
    stacked_copy.wait()
    semblance_copy.wait()


def panels(first, last, count, classes, vels, tables, rows, after, later):
    span = last - first
    held = count - first
    samples = count * LANES
    group = 2 * classes
    window_rows = 2 * CMP_DEV * vels
    done = span - (first > 0) + (last < count)
    outs = [
        jax.ShapeDtypeStruct((CMP_DEV, vels, samples), BF16),
        jax.ShapeDtypeStruct((CMP_DEV, vels, samples), F32),
    ]
    specs = [ANY] * 2
    if first > 0:
        outs.append(jax.ShapeDtypeStruct((2, window_rows, LANES), BF16))
        specs.append(VMEM)
    flat = [piece for chunk in rows for piece in chunk]
    *tables, blocks = tables
    operands = [blocks, *flat, *tables, *after]
    in_specs = [SMEM] + [VMEM] * (len(flat) + len(tables)) + [ANY] * len(after)
    aliases = {}
    if later is not None:
        stacked, semblance, carry = later
        aliases = {len(operands) + 1: 0, len(operands) + 2: 1}
        operands += [carry, stacked, semblance]
        in_specs += [VMEM, ANY, ANY]
    return pl.pallas_call(
        functools.partial(panel_kernel, classes, vels, first, last, count, [len(c) for c in rows], len(after)),
        in_specs=in_specs,
        out_specs=specs,
        out_shape=outs,
        input_output_aliases=aliases,
        scratch_shapes=[
            pltpu.VMEM((held + 1, flat[0].shape[0], LANES), F32),
            pltpu.VMEM((classes, held + 2, 16, LANES), BF16),
            pltpu.VMEM((held + 2, 16, LANES), BF16),
            pltpu.VMEM((span, CMP_DEV * vels, LANES), F32),
            pltpu.VMEM((span, CMP_DEV * vels, LANES), F32),
            pltpu.VMEM((span, group * vels, LANES), F32),
            pltpu.VMEM((span + 3, window_rows, LANES), BF16),
            pltpu.VMEM((CMP_DEV, LANES), F32),
            pltpu.VMEM((CMP_DEV, vels, span * LANES), BF16),
            pltpu.VMEM((CMP_DEV, vels, done * LANES), F32),
            pltpu.SemaphoreType.DMA((2,)),
        ],
        compiler_params=pltpu.CompilerParams(vmem_limit_bytes=VMEM_BYTES),
        cost_estimate=pl.CostEstimate(
            flops=14000 * CMP_DEV * vels * classes * span * LANES,
            bytes_accessed=(1 + span) * 512 * 1024,
            transcendentals=0,
        ),
    )(*operands)


def table_kernel(classes, start, samples, offsets_ref, velocities_ref, *refs):
    local_ref, low_ref, high_ref, blocks_ref = refs[-4:]
    vels, rows, cols = local_ref.shape
    lane = lax.broadcasted_iota(jnp.int32, (rows, LANES), 1)
    sub = lax.broadcasted_iota(jnp.int32, (rows, LANES), 0)
    offset = jnp.full((rows, LANES), offsets_ref[0], F32)
    for h in range(1, classes):
        offset = jnp.where(sub % classes == h, offsets_ref[h], offset)

    def per_velocity(j, blocks):
        blocks = list(blocks)
        slowness = offset / jnp.full((rows, LANES), velocities_ref[j], F32)
        square = slowness * slowness
        for at in range(cols // LANES):
            begin = start + at * LANES
            first = jnp.sqrt(square + float(begin) * float(begin)) - 0.01
            first = jnp.minimum(jnp.maximum(first, float(begin)), float(samples)).astype(jnp.int32)
            base = first // LANES
            flat = j * (cols // LANES) + at
            for wide in range(len(blocks)):
                blocks[wide] = jnp.where(lane == flat - wide * LANES, base, blocks[wide])
            time = (lane + begin).astype(F32)
            position = jnp.sqrt(time * time + square)
            floored = jnp.floor(position)
            fraction = position - floored
            index = jnp.minimum(floored, float(samples)).astype(jnp.int32)
            where = slice(at * LANES, (at + 1) * LANES)
            local_ref[j, :, where] = index - base * LANES
            low_ref[j, :, where] = (1.0 - fraction).astype(BF16).astype(F32)
            high_ref[j, :, where] = fraction.astype(BF16).astype(F32)
        return tuple(blocks)

    width = blocks_ref.shape[1] // LANES
    blocks = lax.fori_loop(
        0,
        vels,
        per_velocity,
        tuple(jnp.zeros((rows, LANES), jnp.int32) for _ in range(width)),
        unroll=math.gcd(vels, 4),
    )
    for wide in range(width):
        blocks_ref[:, wide * LANES : (wide + 1) * LANES] = blocks[wide]


def moveout(offsets, velocities, samples, start, stop, after):
    vels, classes = velocities.shape[0], offsets.shape[0]
    shape = (vels, 2 * classes, stop - start)
    width = pl.cdiv(vels * (stop - start) // LANES, LANES) * LANES
    return pl.pallas_call(
        functools.partial(table_kernel, classes, start, samples),
        in_specs=[SMEM, SMEM] + [ANY] * len(after),
        out_specs=[VMEM] * 4,
        out_shape=[
            jax.ShapeDtypeStruct(shape, jnp.int32),
            jax.ShapeDtypeStruct(shape, F32),
            jax.ShapeDtypeStruct(shape, F32),
            jax.ShapeDtypeStruct((2 * classes, width), jnp.int32),
        ],
        compiler_params=pltpu.CompilerParams(vmem_limit_bytes=VMEM_BYTES),
        cost_estimate=pl.CostEstimate(
            flops=14000 * math.prod(shape), bytes_accessed=12 * math.prod(shape), transcendentals=0
        ),
    )(offsets, velocities, *after)


def per_device(traces, owners, midpoint, offset_class, offsets, velocities):
    samples = traces.shape[1]
    classes, vels = offsets.shape[0], velocities.shape[0]
    count = samples // LANES
    key = (owners[:, 0] * CMP_DEV + midpoint) * classes + offset_class
    plan = Plan(traces, key, classes)
    cuts = [0, samples // 2, samples]
    chunks = list(zip(cuts[:-1], cuts[1:]))[::-1]
    parts, after = [], [plan.places]
    for start, stop in chunks:
        parts.append(plan.bin(start, stop - start, stop == samples, after))
        after = [parts[-1][-1][2]]
    steps = len(plan.orders[0])
    tables, rows, tokens = [], [], []
    for at, chunk in enumerate(chunks):
        tables.append(moveout(offsets, velocities, samples, *chunk, after))
        part = plan.exchange(0, parts[at])
        for place in range(1, steps):
            part, token = plan.merge(part, after)
            part = plan.exchange(place, part)
        *spread, token = plan.spread(part, [rows[-1][1]] if rows else [])
        rows.append(plan.across(spread))
        tokens.append(token)
        after = [token]
    out = None
    for at, (start, stop) in enumerate(chunks):
        out = panels(
            start // LANES,
            stop // LANES,
            count,
            classes,
            vels,
            tables[at],
            rows[: at + 1][::-1],
            tokens[at + 1 : at + 2],
            out,
        )
    return (out[0], out[1])


def solution(mesh):
    in_specs = (
        P(("inline", "xline"), None),
        P(("inline", "xline"), None),
        P(("inline", "xline")),
        P(("inline", "xline")),
        P(),
        P(),
    )
    out_specs = (P(("inline", "xline"), None, None), P(("inline", "xline"), None, None))
    return jax.shard_map(
        per_device, mesh=mesh, in_specs=in_specs, out_specs=out_specs, check_vma=False
    )
```

```python
import functools
import math

import jax
import jax.numpy as jnp
from jax import lax
from jax.experimental import pallas as pl
from jax.experimental.pallas import tpu as pltpu
from jax.sharding import PartitionSpec as P

HALF_WIN = 4
CMP_DEV = 8
LANES = 128
UNROLL = 8
PIECES = 2
VMEM_BYTES = 16 * 1024 * 1024
F32 = jnp.float32
BF16 = jnp.bfloat16
VMEM = pl.BlockSpec(memory_space=pltpu.VMEM)
SMEM = pl.BlockSpec(memory_space=pltpu.SMEM)
ANY = pl.BlockSpec(memory_space=pl.ANY)
TOKEN = jax.ShapeDtypeStruct((8, LANES), F32)

LANE_GATHER = lax.GatherDimensionNumbers(
    offset_dims=(),
    collapsed_slice_dims=(1,),
    start_index_map=(1,),
    operand_batching_dims=(0,),
    start_indices_batching_dims=(0,),
)


def take_lanes(rows, index):
    return lax.gather(
        rows,
        index[..., None],
        LANE_GATHER,
        (1, 1),
        mode=lax.GatherScatterMode.PROMISE_IN_BOUNDS,
    )


def bin_kernel(orders, count, kept_rows, *refs):
    members, data = refs[:orders], refs[orders : orders + count]
    outs, token_ref = refs[-2 * orders - 1 : -1], refs[-1]
    token_ref[...] = jnp.zeros(token_ref.shape, F32)
    per, cols = data[0].shape
    width = cols // orders
    tile = math.gcd(width, 256)
    for order in range(orders):
        member_ref = members[order]
        kept_ref, sent_ref = outs[2 * order : 2 * order + 2]
        rows = member_ref.shape[0]
        for start in range(0, kept_ref.shape[1], tile):
            stop = min(start + tile, kept_ref.shape[1])
            total = None
            for at, block in enumerate(data):
                if start < width:
                    values = block[:, order * width + start : order * width + stop]
                else:
                    values = jnp.ones((per, stop - start), BF16)
                part = jnp.dot(
                    member_ref[:, at * per : (at + 1) * per], values, preferred_element_type=F32
                )
                total = part if total is None else total + part
            kept_ref[:, start:stop] = total[:kept_rows]
            if kept_rows < rows:
                sent_ref[:, start:stop] = total[kept_rows:].astype(BF16)
            else:
                sent_ref[:, start:stop] = jnp.zeros((sent_ref.shape[0], stop - start), BF16)


def bin_rows(members, data, start, cols, counted, kept_rows, after):
    rows = members[0].shape[0]
    per = data[0].shape[0]
    sent_rows = max(rows - kept_rows, 16)
    in_specs = [pl.BlockSpec(member.shape, lambda t: (0, 0)) for member in members]
    in_specs += [pl.BlockSpec((per, cols), lambda t: (0, start // cols))] * len(data)
    in_specs += [ANY] * len(after)
    shapes = []
    for at in range(len(members)):
        width = cols // len(members) + (LANES if counted and at == len(members) - 1 else 0)
        shapes.append(jax.ShapeDtypeStruct((kept_rows, width), F32))
        shapes.append(jax.ShapeDtypeStruct((sent_rows, width), BF16))
    shapes.append(TOKEN)
    outs = pl.pallas_call(
        functools.partial(bin_kernel, len(members), len(data), kept_rows),
        grid=(1,),
        in_specs=in_specs,
        out_specs=[pl.BlockSpec(shape.shape, lambda t: (0, 0)) for shape in shapes],
        out_shape=shapes,
        compiler_params=pltpu.CompilerParams(vmem_limit_bytes=VMEM_BYTES),
        cost_estimate=pl.CostEstimate(
            flops=2 * rows * len(data) * per * cols,
            bytes_accessed=0,
            transcendentals=0,
        ),
    )(*members, *data, *after)
    return list(zip(outs[0:-1:2], outs[1:-1:2])), outs[-1]


class Plan:
    def __init__(self, traces, key, classes):
        self.inline = lax.axis_size("inline")
        self.xline = lax.axis_size("xline")
        self.me = lax.axis_index("inline")
        self.me_x = lax.axis_index("xline")
        self.classes = classes
        self.dev_rows = CMP_DEV * classes
        self.line_rows = self.xline * self.dev_rows
        bits = [1 << b for b in range(self.inline.bit_length() - 1)]
        self.core, others = bits[0], bits[1:]
        self.orders = [others, others[::-1]] if len(others) > 1 else [others]
        self.codes = 1 << len(others)
        unit = 8 if self.codes % 4 == 0 else 16
        self.block_rows = -(-(self.line_rows + 2 * classes) // unit) * unit
        self.data = [traces, self.swap(traces, self.core)]
        self.keys = jnp.concatenate([key, self.swap(key, self.core)])
        self.members = [self.member(order) for order in self.orders]
        places = [self.me_x] + [target for target, _ in self.targets()]
        self.places = jnp.stack(places) * self.dev_rows

    def swap(self, value, bit):
        return lax.ppermute(value, "inline", [(i, i ^ bit) for i in range(self.inline)])

    def member(self, order):
        classes, line_rows = self.classes, self.line_rows
        line, local = self.keys // line_rows, self.keys % line_rows

        def row_of(target, row):
            apart = target ^ self.me
            code = jnp.zeros_like(target)
            for bit in order:
                code = code * 2 + jnp.where(apart & bit != 0, 1, 0)
            valid = (apart & self.core == 0) & (target >= 0) & (target < self.inline)
            return jnp.where(valid, code * self.block_rows + row, -1)

        own = row_of(line, local + classes)
        rim = jnp.where(
            local >= line_rows - classes,
            row_of(line + 1, local - (line_rows - classes)),
            jnp.where(local < classes, row_of(line - 1, local + classes + line_rows), -1),
        )
        row = jnp.arange(self.codes * self.block_rows)[:, None]
        return ((row == own[None, :]) | (row == rim[None, :])).astype(BF16)

    def bin(self, start, cols, counted, after):
        rows = self.codes * self.block_rows
        kept_rows = rows // 2 if self.orders[0] else rows
        return bin_rows(self.members, self.data, start, cols, counted, kept_rows, after)

    def exchange(self, place, parts):
        return [
            (kept, self.swap(sent, order[place])) for order, (kept, sent) in zip(self.orders, parts)
        ]

    def targets(self):
        steps = []
        for step in range(self.xline - 1, 0, -1):
            if self.xline & (self.xline - 1) == 0:
                target = self.me_x ^ step
                pairs = [(i, i ^ step) for i in range(self.xline)]
            else:
                target = (self.me_x + step) % self.xline
                pairs = [(i, (i + step) % self.xline) for i in range(self.xline)]
            steps.append((target, pairs))
        return steps

    def merge(self, parts, after):
        half = parts[0][0].shape[0] // 2
        shapes = []
        for kept, _ in parts:
            shapes.append(jax.ShapeDtypeStruct((half, kept.shape[1]), F32))
            shapes.append(jax.ShapeDtypeStruct((half, kept.shape[1]), BF16))
        flat = [value for part in parts for value in part]
        outs = pl.pallas_call(
            functools.partial(merge_kernel, len(parts)),
            in_specs=[VMEM] * len(flat) + [ANY] * len(after),
            out_specs=[VMEM] * (len(shapes) + 1),
            out_shape=shapes + [TOKEN],
            compiler_params=pltpu.CompilerParams(vmem_limit_bytes=VMEM_BYTES),
            cost_estimate=cost_of(flat),
        )(*flat, *after)
        return list(zip(outs[0:-1:2], outs[1:-1:2])), outs[-1]

    def spread(self, parts, after):
        window = self.dev_rows + 2 * self.classes
        cols = sum(kept.shape[1] for kept, _ in parts)
        flat = [value for part in parts for value in part]
        kinds = [F32] + [BF16] * (self.xline - 1)
        return pl.pallas_call(
            functools.partial(spread_kernel, len(parts), len(kinds)),
            in_specs=[SMEM] + [VMEM] * len(flat) + [ANY] * len(after),
            out_specs=[VMEM] * (len(kinds) + 1),
            out_shape=[jax.ShapeDtypeStruct((window, cols), kind) for kind in kinds] + [TOKEN],
            scratch_shapes=[pltpu.VMEM((parts[0][0].shape[0], cols), F32)],
            compiler_params=pltpu.CompilerParams(vmem_limit_bytes=VMEM_BYTES),
            cost_estimate=cost_of(flat),
        )(self.places, *flat, *after)

    def across(self, blocks):
        own, *sent = blocks
        return [own] + [
            lax.ppermute(block, "xline", pairs) for block, (_, pairs) in zip(sent, self.targets())
        ]


def cost_of(values):
    size = sum(value.size * value.dtype.itemsize for value in values)
    return pl.CostEstimate(flops=0, bytes_accessed=2 * size, transcendentals=0)


def merge_kernel(count, *refs):
    ins, outs, token_ref = refs[: 2 * count], refs[-2 * count - 1 : -1], refs[-1]
    token_ref[...] = jnp.zeros(token_ref.shape, F32)
    for at in range(count):
        kept, sent = ins[2 * at : 2 * at + 2]
        half = kept.shape[0] // 2
        total = kept[...] + sent[...].astype(F32)
        outs[2 * at][...] = total[:half]
        outs[2 * at + 1][...] = total[half:].astype(BF16)


def spread_kernel(count, blocks, places_ref, *refs):
    ins, outs, token_ref, total_ref = refs[: 2 * count], refs[-blocks - 2 : -2], refs[-2], refs[-1]
    token_ref[...] = jnp.zeros(token_ref.shape, F32)
    start = 0
    for at in range(count):
        kept, sent = ins[2 * at : 2 * at + 2]
        stop = start + kept.shape[1]
        total_ref[:, start:stop] = kept[...] + sent[...].astype(F32)
        start = stop
    for at, out in enumerate(outs):
        place = pl.multiple_of(places_ref[at], 8)
        out[...] = total_ref[pl.ds(place, out.shape[0]), :].astype(out.dtype)


def panel_kernel(classes, vels, first, last, count, pieces, waits, *refs):
    blocks_ref = refs[0]
    at = 1
    chunk_refs = []
    for number in pieces:
        chunk_refs.append(refs[at : at + number])
        at += number
    index_ref, low_ref, high_ref = refs[at : at + 3]
    at += 3 + waits
    if last < count:
        later_ref, stacked_later, semblance_later = refs[at : at + 3]
        at += 3
    stacked_out, semblance_out = refs[at : at + 2]
    at += 2
    if first > 0:
        carry_ref = refs[at]
        at += 1
    (
        plane_ref,
        source_ref,
        rim_source_ref,
        sum_ref,
        energy_ref,
        rim_ref,
        window_ref,
        scale_ref,
        band_ref,
        *staged,
    ) = refs[at:]
    mids = CMP_DEV
    span = last - first
    held = count - first
    lane = lax.broadcasted_iota(jnp.int32, (8, LANES), 1)
    sub = lax.broadcasted_iota(jnp.int32, (8, LANES), 0)
    sub16 = lax.broadcasted_iota(jnp.int32, (16, LANES), 0)

    block_at = 0
    for piece_refs in chunk_refs:
        for inner in range(piece_refs[0].shape[1] // LANES):
            where = slice(inner * LANES, (inner + 1) * LANES)
            block = piece_refs[0][:, where]
            for piece_ref in piece_refs[1:]:
                block = block + piece_ref[:, where].astype(F32)
            plane_ref[block_at] = block.astype(BF16).astype(F32) if block_at < held else block
            block_at += 1
    fold = None
    for h in range(classes):
        counts = plane_ref[held, pl.ds(classes + h, mids, stride=classes), :]
        fold = counts if fold is None else fold + counts
    scale_ref[...] = 1.0 / jnp.maximum(fold, 1.0)
    plane_ref[held] = jnp.zeros(plane_ref.shape[1:], F32)

    def later(here, after):
        return jnp.where(
            lane == LANES - 1,
            pltpu.roll(after, LANES - 1, 1),
            pltpu.roll(here, LANES - 1, 1),
        )

    def rim_rows(at):
        return jnp.where(
            sub < classes, plane_ref[at, 0:8, :], plane_ref[at, mids * classes : mids * classes + 8, :]
        )

    zeros = jnp.zeros((16, LANES), BF16)
    for at in range(held):
        for h in range(classes):
            here = plane_ref[at, pl.ds(classes + h, mids, stride=classes), :]
            after = plane_ref[at + 1, pl.ds(classes + h, mids, stride=classes), :]
            source_ref[h, at] = jnp.concatenate([here, later(here, after)], axis=0).astype(BF16)
        here, after = rim_rows(at), rim_rows(at + 1)
        rim_source_ref[at] = jnp.concatenate([here, later(here, after)], axis=0).astype(BF16)
    for at in (held, held + 1):
        for h in range(classes):
            source_ref[h, at] = zeros
        rim_source_ref[at] = zeros

    own_class = [sub16 % classes == h for h in range(classes)]
    group = 2 * classes
    shape = (mids, vels, LANES)
    rows = mids * vels
    source = lax.broadcasted_iota(jnp.int32, band_ref.shape, 0) - LANES
    target = lax.broadcasted_iota(jnp.int32, band_ref.shape, 1)
    band_ref[...] = jnp.where(jnp.abs(source - target) <= HALF_WIN, 1.0, 0.0).astype(BF16)
    edge = jnp.zeros(window_ref.shape[1:], BF16)
    window_ref[0] = edge
    if last < count:
        window_ref[span + 1] = later_ref[0]
        window_ref[span + 2] = later_ref[1]
    else:
        window_ref[span + 1] = edge

    def moved_out(j, at, where):
        base = [blocks_ref[h, j * span + at] - first for h in range(classes)]
        total = energy = None
        for h in range(classes):
            row = slice(h, h + 1)
            local = jnp.broadcast_to(index_ref[j, row, where], (8, LANES))
            index = jnp.concatenate([local, local], axis=0).astype(jnp.int16)
            low = jnp.broadcast_to(low_ref[j, row, where], (8, LANES))
            high = jnp.broadcast_to(high_ref[j, row, where], (8, LANES))
            inner = index & (LANES - 1)
            got = jnp.where(
                index < LANES,
                take_lanes(source_ref[h, base[h]], inner),
                take_lanes(source_ref[h, base[h] + 1], inner),
            ).astype(F32)
            moved = low * got[:8] + high * got[8:]
            total = moved if total is None else total + moved
            energy = moved * moved if energy is None else energy + moved * moved
        sum_ref[at, pl.ds(j, mids, stride=vels), :] = total
        energy_ref[at, pl.ds(j, mids, stride=vels), :] = energy
        near = rim_source_ref[base[0]]
        far = rim_source_ref[base[0] + 1]
        for h in range(1, classes):
            near = jnp.where(own_class[h], rim_source_ref[base[h]], near)
            far = jnp.where(own_class[h], rim_source_ref[base[h] + 1], far)
        local = index_ref[j, :, where]
        index = jnp.concatenate([local, local], axis=0).astype(jnp.int16)
        inner = index & (LANES - 1)
        got = jnp.where(index < LANES, take_lanes(near, inner), take_lanes(far, inner)).astype(F32)
        rim_ref[at, pl.ds(j, group, stride=vels), :] = (
            low_ref[j, :, where] * got[:8] + high_ref[j, :, where] * got[8:]
        )

    def three(low, mid, high):
        return jnp.concatenate([low, mid[:-1]], axis=0) + mid + jnp.concatenate([mid[1:], high], axis=0)

    begin = 0 if first == 0 else 1
    end = span + 1 if last < count else span
    copies = []
    if first > 0:
        stacked_ref, semblance_ref = stacked_out, semblance_out
    else:
        stacked_ref, semblance_ref, semaphores = staged

        def leave(source, out, begin, end):
            place = out.at[:, :, begin * LANES : end * LANES]
            copies.append(pltpu.make_async_copy(source, place, semaphores.at[len(copies)]))
            copies[-1].start()

        if last < count:
            leave(stacked_later, stacked_out, last, count)
            leave(semblance_later, semblance_out, last + 1, count)

    def per_block(at, _):
        where = pl.ds(pl.multiple_of(at * LANES, LANES), LANES)
        total = sum_ref[at].reshape(shape)
        rim = rim_ref[at].reshape(2, classes, vels, LANES)
        rim_sum = jnp.sum(rim, axis=1)
        rim_power = rim_sum * rim_sum
        rim_energy = jnp.sum(rim * rim, axis=1)
        power = three(rim_power[0:1], total * total, rim_power[1:2])
        energy = three(rim_energy[0:1], energy_ref[at].reshape(shape), rim_energy[1:2])
        window_ref[at + 1, :rows] = power.reshape(rows, LANES).astype(BF16)
        window_ref[at + 1, rows:] = energy.reshape(rows, LANES).astype(BF16)
        for m in range(mids):
            stacked_ref[m, :, where] = (total[m] * scale_ref[m : m + 1, :]).astype(BF16)
        return 0

    def per_window(at, blocks):
        values = jnp.concatenate([window_ref[at + i] for i in range(blocks + 2)], axis=1)
        band = band_ref[: (blocks + 2) * LANES, : blocks * LANES]
        summed = jnp.dot(values, band, preferred_element_type=F32)
        semblance = summed[:rows] / jnp.maximum(classes * summed[rows:], 1.0)
        semblance_ref[:, :, (at - begin) * LANES : (at - begin + blocks) * LANES] = semblance.reshape(
            mids, vels, blocks * LANES
        )

    pieces = PIECES if first == 0 and span % PIECES == 0 else 1
    top, finished = span, end
    for piece in range(pieces):
        low = top - span // pieces

        def per_velocity(j, _, blocks=range(low, top)):
            for at in blocks:
                moved_out(j, at, slice(at * LANES, (at + 1) * LANES))
            return 0

        lax.fori_loop(0, vels, per_velocity, 0, unroll=math.gcd(vels, UNROLL * pieces))
        lax.fori_loop(low, top, per_block, 0)
        if first == 0:
            leave(stacked_ref.at[:, :, low * LANES : top * LANES], stacked_out, low, top)
        ready = low + 1 if low else begin
        for at in range(ready, finished, 2):
            per_window(at, min(2, finished - at))
        if first == 0:
            leave(semblance_ref.at[:, :, ready * LANES : finished * LANES], semblance_out, ready, finished)
        top, finished = low, ready
    if first > 0:
        carry_ref[0] = window_ref[1]
        carry_ref[1] = window_ref[2]
    for copy in copies:
        copy.wait()


def panels(first, last, count, classes, vels, tables, rows, after, later):
    span = last - first
    held = count - first
    group = 2 * classes
    window_rows = 2 * CMP_DEV * vels
    flat = [piece for chunk in rows for piece in chunk]
    *tables, blocks = tables
    operands = [blocks, *flat, *tables, *after]
    in_specs = [SMEM] + [VMEM] * (len(flat) + len(tables)) + [ANY] * len(after)
    if later is not None:
        stacked, semblance, carry = later
        operands += [carry, stacked, semblance]
        in_specs += [VMEM] * 3
    staged = []
    if first > 0:
        outs = [
            jax.ShapeDtypeStruct((CMP_DEV, vels, span * LANES), BF16),
            jax.ShapeDtypeStruct((CMP_DEV, vels, (span - 1) * LANES), F32),
            jax.ShapeDtypeStruct((2, window_rows, LANES), BF16),
        ]
        specs = [VMEM] * 3
    else:
        outs = [
            jax.ShapeDtypeStruct((CMP_DEV, vels, count * LANES), BF16),
            jax.ShapeDtypeStruct((CMP_DEV, vels, count * LANES), F32),
        ]
        specs = [ANY] * 2
        done = span + (last < count)
        staged = [
            pltpu.VMEM((CMP_DEV, vels, span * LANES), BF16),
            pltpu.VMEM((CMP_DEV, vels, done * LANES), F32),
            pltpu.SemaphoreType.DMA((2 + 2 * PIECES,)),
        ]
    return pl.pallas_call(
        functools.partial(
            panel_kernel, classes, vels, first, last, count, [len(c) for c in rows], len(after)
        ),
        in_specs=in_specs,
        out_specs=specs,
        out_shape=outs,
        scratch_shapes=[
            pltpu.VMEM((held + 1, flat[0].shape[0], LANES), F32),
            pltpu.VMEM((classes, held + 2, 16, LANES), BF16),
            pltpu.VMEM((held + 2, 16, LANES), BF16),
            pltpu.VMEM((span, CMP_DEV * vels, LANES), F32),
            pltpu.VMEM((span, CMP_DEV * vels, LANES), F32),
            pltpu.VMEM((span, group * vels, LANES), F32),
            pltpu.VMEM((span + 3, window_rows, LANES), BF16),
            pltpu.VMEM((CMP_DEV, LANES), F32),
            pltpu.VMEM((4 * LANES, 2 * LANES), BF16),
            *staged,
        ],
        compiler_params=pltpu.CompilerParams(vmem_limit_bytes=VMEM_BYTES),
        cost_estimate=pl.CostEstimate(
            flops=14000 * CMP_DEV * vels * classes * span * LANES,
            bytes_accessed=(1 + span) * 512 * 1024,
            transcendentals=0,
        ),
    )(*operands)


def table_kernel(classes, start, samples, offsets_ref, velocities_ref, *refs):
    index_ref, low_ref, high_ref, blocks_ref, token_ref = refs[-5:]
    token_ref[...] = jnp.zeros(token_ref.shape, F32)
    vels, rows, cols = low_ref.shape
    lane = lax.broadcasted_iota(jnp.int32, (rows, LANES), 1)
    sub = lax.broadcasted_iota(jnp.int32, (rows, LANES), 0)
    offset = jnp.full((rows, LANES), offsets_ref[0], F32)
    for h in range(1, classes):
        offset = jnp.where(sub % classes == h, offsets_ref[h], offset)

    def per_velocity(j, blocks):
        blocks = list(blocks)
        slowness = offset / jnp.full((rows, LANES), velocities_ref[j], F32)
        square = slowness * slowness
        for at in range(cols // LANES):
            begin = start + at * LANES
            first = jnp.sqrt(square + float(begin) * float(begin)) - 0.01
            first = jnp.minimum(jnp.maximum(first, float(begin)), float(samples)).astype(jnp.int32)
            base = first // LANES
            flat = j * (cols // LANES) + at
            for wide in range(len(blocks)):
                blocks[wide] = jnp.where(lane == flat - wide * LANES, base, blocks[wide])
            time = (lane + begin).astype(F32)
            position = jnp.sqrt(time * time + square)
            floored = jnp.floor(position)
            fraction = position - floored
            index = jnp.minimum(floored, float(samples)).astype(jnp.int32)
            where = slice(at * LANES, (at + 1) * LANES)
            index_ref[j, :, where] = index - base * LANES
            low_ref[j, :, where] = (1.0 - fraction).astype(BF16).astype(F32)
            high_ref[j, :, where] = fraction.astype(BF16).astype(F32)
        return tuple(blocks)

    width = blocks_ref.shape[1] // LANES
    blocks = lax.fori_loop(
        0,
        vels,
        per_velocity,
        tuple(jnp.zeros((rows, LANES), jnp.int32) for _ in range(width)),
        unroll=math.gcd(vels, 4),
    )
    for wide in range(width):
        blocks_ref[:, wide * LANES : (wide + 1) * LANES] = blocks[wide]


def moveout(offsets, velocities, samples, start, stop, after):
    vels, classes = velocities.shape[0], offsets.shape[0]
    shape = (vels, 2 * classes, stop - start)
    width = pl.cdiv(vels * (stop - start) // LANES, LANES) * LANES
    return pl.pallas_call(
        functools.partial(table_kernel, classes, start, samples),
        in_specs=[SMEM, SMEM] + [ANY] * len(after),
        out_specs=[VMEM] * 5,
        out_shape=[
            jax.ShapeDtypeStruct(shape, jnp.int32),
            jax.ShapeDtypeStruct(shape, F32),
            jax.ShapeDtypeStruct(shape, F32),
            jax.ShapeDtypeStruct((2 * classes, width), jnp.int32),
            TOKEN,
        ],
        compiler_params=pltpu.CompilerParams(vmem_limit_bytes=VMEM_BYTES),
        cost_estimate=pl.CostEstimate(
            flops=0, bytes_accessed=0, transcendentals=0
        ),
    )(offsets, velocities, *after)


def per_device(traces, owners, midpoint, offset_class, offsets, velocities):
    samples = traces.shape[1]
    classes, vels = offsets.shape[0], velocities.shape[0]
    count = samples // LANES
    key = (owners.reshape(-1) * CMP_DEV + midpoint) * classes + offset_class
    plan = Plan(traces, key, classes)
    cuts = [0, samples // 2, samples]
    chunks = list(zip(cuts[:-1], cuts[1:]))[::-1]
    parts, tokens = [], [plan.places]
    for start, stop in chunks:
        part, token = plan.bin(start, stop - start, stop == samples, tokens[-1:])
        parts.append(part)
        tokens.append(token)
    tables, spreads = [], []
    *table, token = moveout(offsets, velocities, samples, *chunks[0], tokens[-1:])
    tables.append(table)
    tokens.append(token)
    for at in range(len(chunks)):
        part = plan.exchange(0, parts[at])
        for place in range(1, len(plan.orders[0])):
            part, token = plan.merge(part, tokens[-1:])
            part = plan.exchange(place, part)
            tokens.append(token)
        spreads.append(part)
    rows, tokens = [], []
    for part in spreads:
        *spread, token = plan.spread(part, tokens[-1:])
        rows.append(plan.across(spread))
        tokens.append(token)
    for chunk in chunks[1:]:
        *table, token = moveout(offsets, velocities, samples, *chunk, tokens[-1:])
        tables.append(table)
        tokens.append(token)
    out = None
    for at, (start, stop) in enumerate(chunks):
        out = panels(
            start // LANES,
            stop // LANES,
            count,
            classes,
            vels,
            tables[at],
            rows[: at + 1][::-1],
            tokens[-1:] if not at else [],
            out,
        )
    return (out[0], out[1])


def solution(mesh):
    in_specs = (
        P(("inline", "xline"), None),
        P(("inline", "xline"), None),
        P(("inline", "xline")),
        P(("inline", "xline")),
        P(),
        P(),
    )
    out_specs = (P(("inline", "xline"), None, None), P(("inline", "xline"), None, None))
    return jax.shard_map(
        per_device, mesh=mesh, in_specs=in_specs, out_specs=out_specs, check_vma=False
    )
```

```python
import functools
import math

import jax
import jax.numpy as jnp
from jax import lax
from jax.experimental import pallas as pl
from jax.experimental.pallas import tpu as pltpu
from jax.sharding import PartitionSpec as P

HALF_WIN = 4
CMP_DEV = 8
LANES = 128
UNROLL = 8
PIECES = 2
VMEM_BYTES = 16 * 1024 * 1024
F32 = jnp.float32
BF16 = jnp.bfloat16
VMEM = pl.BlockSpec(memory_space=pltpu.VMEM)
SMEM = pl.BlockSpec(memory_space=pltpu.SMEM)
ANY = pl.BlockSpec(memory_space=pl.ANY)
TOKEN = jax.ShapeDtypeStruct((8, LANES), F32)

LANE_GATHER = lax.GatherDimensionNumbers(
    offset_dims=(),
    collapsed_slice_dims=(1,),
    start_index_map=(1,),
    operand_batching_dims=(0,),
    start_indices_batching_dims=(0,),
)


def take_lanes(rows, index):
    return lax.gather(
        rows,
        index[..., None],
        LANE_GATHER,
        (1, 1),
        mode=lax.GatherScatterMode.PROMISE_IN_BOUNDS,
    )


def bin_kernel(orders, count, kept_rows, *refs):
    members, data = refs[:orders], refs[orders : orders + count]
    outs, token_ref = refs[-2 * orders - 1 : -1], refs[-1]
    token_ref[...] = jnp.zeros(token_ref.shape, F32)
    per, cols = data[0].shape
    width = cols // orders
    tile = math.gcd(width, 256)
    for order in range(orders):
        member_ref = members[order]
        kept_ref, sent_ref = outs[2 * order : 2 * order + 2]
        rows = member_ref.shape[0]
        for start in range(0, kept_ref.shape[1], tile):
            stop = min(start + tile, kept_ref.shape[1])
            total = None
            for at, block in enumerate(data):
                if start < width:
                    values = block[:, order * width + start : order * width + stop]
                else:
                    values = jnp.ones((per, stop - start), BF16)
                part = jnp.dot(
                    member_ref[:, at * per : (at + 1) * per], values, preferred_element_type=F32
                )
                total = part if total is None else total + part
            kept_ref[:, start:stop] = total[:kept_rows]
            if kept_rows < rows:
                sent_ref[:, start:stop] = total[kept_rows:].astype(BF16)
            else:
                sent_ref[:, start:stop] = jnp.zeros((sent_ref.shape[0], stop - start), BF16)


def bin_rows(members, data, start, cols, counted, kept_rows, after):
    rows = members[0].shape[0]
    per = data[0].shape[0]
    sent_rows = max(rows - kept_rows, 16)
    in_specs = [pl.BlockSpec(member.shape, lambda t: (0, 0)) for member in members]
    in_specs += [pl.BlockSpec((per, cols), lambda t: (0, start // cols))] * len(data)
    in_specs += [ANY] * len(after)
    shapes = []
    for at in range(len(members)):
        width = cols // len(members) + (LANES if counted and at == len(members) - 1 else 0)
        shapes.append(jax.ShapeDtypeStruct((kept_rows, width), F32))
        shapes.append(jax.ShapeDtypeStruct((sent_rows, width), BF16))
    shapes.append(TOKEN)
    outs = pl.pallas_call(
        functools.partial(bin_kernel, len(members), len(data), kept_rows),
        grid=(1,),
        in_specs=in_specs,
        out_specs=[pl.BlockSpec(shape.shape, lambda t: (0, 0)) for shape in shapes],
        out_shape=shapes,
        compiler_params=pltpu.CompilerParams(vmem_limit_bytes=VMEM_BYTES),
        cost_estimate=pl.CostEstimate(
            flops=2 * rows * len(data) * per * cols,
            bytes_accessed=0,
            transcendentals=0,
        ),
    )(*members, *data, *after)
    return list(zip(outs[0:-1:2], outs[1:-1:2])), outs[-1]


class Plan:
    def __init__(self, traces, key, classes):
        self.inline = lax.axis_size("inline")
        self.xline = lax.axis_size("xline")
        self.me = lax.axis_index("inline")
        self.me_x = lax.axis_index("xline")
        self.classes = classes
        self.dev_rows = CMP_DEV * classes
        self.line_rows = self.xline * self.dev_rows
        bits = [1 << b for b in range(self.inline.bit_length() - 1)]
        self.core, others = bits[0], bits[1:]
        self.orders = [others, others[::-1]] if len(others) > 1 else [others]
        self.codes = 1 << len(others)
        unit = 8 if self.codes % 4 == 0 else 16
        self.block_rows = -(-(self.line_rows + 2 * classes) // unit) * unit
        self.data = [traces, self.swap(traces, self.core)]
        self.keys = jnp.concatenate([key, self.swap(key, self.core)])
        self.members = [self.member(order) for order in self.orders]
        places = [self.me_x] + [target for target, _ in self.targets()]
        self.places = jnp.stack(places) * self.dev_rows

    def swap(self, value, bit):
        return lax.ppermute(value, "inline", [(i, i ^ bit) for i in range(self.inline)])

    def member(self, order):
        classes, line_rows = self.classes, self.line_rows
        line, local = self.keys // line_rows, self.keys % line_rows

        def row_of(target, row):
            apart = target ^ self.me
            code = jnp.zeros_like(target)
            for bit in order:
                code = code * 2 + jnp.where(apart & bit != 0, 1, 0)
            valid = (apart & self.core == 0) & (target >= 0) & (target < self.inline)
            return jnp.where(valid, code * self.block_rows + row, -1)

        own = row_of(line, local + classes)
        rim = jnp.where(
            local >= line_rows - classes,
            row_of(line + 1, local - (line_rows - classes)),
            jnp.where(local < classes, row_of(line - 1, local + classes + line_rows), -1),
        )
        row = jnp.arange(self.codes * self.block_rows)[:, None]
        return ((row == own[None, :]) | (row == rim[None, :])).astype(BF16)

    def bin(self, start, cols, counted, after):
        rows = self.codes * self.block_rows
        kept_rows = rows // 2 if self.orders[0] else rows
        return bin_rows(self.members, self.data, start, cols, counted, kept_rows, after)

    def exchange(self, place, parts):
        return [
            (kept, self.swap(sent, order[place])) for order, (kept, sent) in zip(self.orders, parts)
        ]

    def targets(self):
        steps = []
        for step in range(self.xline - 1, 0, -1):
            if self.xline & (self.xline - 1) == 0:
                target = self.me_x ^ step
                pairs = [(i, i ^ step) for i in range(self.xline)]
            else:
                target = (self.me_x + step) % self.xline
                pairs = [(i, (i + step) % self.xline) for i in range(self.xline)]
            steps.append((target, pairs))
        return steps

    def merge(self, parts, after):
        half = parts[0][0].shape[0] // 2
        shapes = []
        for kept, _ in parts:
            shapes.append(jax.ShapeDtypeStruct((half, kept.shape[1]), F32))
            shapes.append(jax.ShapeDtypeStruct((half, kept.shape[1]), BF16))
        flat = [value for part in parts for value in part]
        outs = pl.pallas_call(
            functools.partial(merge_kernel, len(parts)),
            in_specs=[VMEM] * len(flat) + [ANY] * len(after),
            out_specs=[VMEM] * (len(shapes) + 1),
            out_shape=shapes + [TOKEN],
            compiler_params=pltpu.CompilerParams(vmem_limit_bytes=VMEM_BYTES),
            cost_estimate=cost_of(flat),
        )(*flat, *after)
        return list(zip(outs[0:-1:2], outs[1:-1:2])), outs[-1]

    def spread(self, parts, after):
        window = self.dev_rows + 2 * self.classes
        cols = sum(kept.shape[1] for kept, _ in parts)
        flat = [value for part in parts for value in part]
        kinds = [F32] + [BF16] * (self.xline - 1)
        return pl.pallas_call(
            functools.partial(spread_kernel, len(parts), len(kinds)),
            in_specs=[SMEM] + [VMEM] * len(flat) + [ANY] * len(after),
            out_specs=[VMEM] * (len(kinds) + 1),
            out_shape=[jax.ShapeDtypeStruct((window, cols), kind) for kind in kinds] + [TOKEN],
            scratch_shapes=[pltpu.VMEM((parts[0][0].shape[0], cols), F32)],
            compiler_params=pltpu.CompilerParams(vmem_limit_bytes=VMEM_BYTES),
            cost_estimate=cost_of(flat),
        )(self.places, *flat, *after)

    def across(self, blocks, near_first):
        own, *sent = blocks
        moves = [(block, pairs) for block, (_, pairs) in zip(sent, self.targets())]
        if near_first:
            moves = moves[::-1]
        return [own] + [lax.ppermute(block, "xline", pairs) for block, pairs in moves]


def cost_of(values):
    size = sum(value.size * value.dtype.itemsize for value in values)
    return pl.CostEstimate(flops=0, bytes_accessed=2 * size, transcendentals=0)


def merge_kernel(count, *refs):
    ins, outs, token_ref = refs[: 2 * count], refs[-2 * count - 1 : -1], refs[-1]
    token_ref[...] = jnp.zeros(token_ref.shape, F32)
    for at in range(count):
        kept, sent = ins[2 * at : 2 * at + 2]
        half = kept.shape[0] // 2
        total = kept[...] + sent[...].astype(F32)
        outs[2 * at][...] = total[:half]
        outs[2 * at + 1][...] = total[half:].astype(BF16)


def spread_kernel(count, blocks, places_ref, *refs):
    ins, outs, token_ref, total_ref = refs[: 2 * count], refs[-blocks - 2 : -2], refs[-2], refs[-1]
    token_ref[...] = jnp.zeros(token_ref.shape, F32)
    start = 0
    for at in range(count):
        kept, sent = ins[2 * at : 2 * at + 2]
        stop = start + kept.shape[1]
        total_ref[:, start:stop] = kept[...] + sent[...].astype(F32)
        start = stop
    for at, out in enumerate(outs):
        place = pl.multiple_of(places_ref[at], 8)
        out[...] = total_ref[pl.ds(place, out.shape[0]), :].astype(out.dtype)


def panel_kernel(classes, vels, first, last, count, pieces, waits, *refs):
    blocks_ref = refs[0]
    at = 1
    chunk_refs = []
    for number in pieces:
        chunk_refs.append(refs[at : at + number])
        at += number
    index_ref, low_ref, high_ref = refs[at : at + 3]
    at += 3 + waits
    if last < count:
        later_ref, stacked_later, semblance_later = refs[at : at + 3]
        at += 3
    stacked_out, semblance_out = refs[at : at + 2]
    at += 2
    if first > 0:
        carry_ref = refs[at]
        at += 1
    (
        plane_ref,
        source_ref,
        rim_source_ref,
        sum_ref,
        energy_ref,
        rim_ref,
        window_ref,
        scale_ref,
        band_ref,
        *staged,
    ) = refs[at:]
    mids = CMP_DEV
    span = last - first
    held = count - first
    lane = lax.broadcasted_iota(jnp.int32, (8, LANES), 1)
    sub = lax.broadcasted_iota(jnp.int32, (8, LANES), 0)
    sub16 = lax.broadcasted_iota(jnp.int32, (16, LANES), 0)

    block_at = 0
    for piece_refs in chunk_refs:
        for inner in range(piece_refs[0].shape[1] // LANES):
            where = slice(inner * LANES, (inner + 1) * LANES)
            block = piece_refs[0][:, where]
            for piece_ref in piece_refs[1:]:
                block = block + piece_ref[:, where].astype(F32)
            plane_ref[block_at] = block.astype(BF16).astype(F32) if block_at < held else block
            block_at += 1
    fold = None
    for h in range(classes):
        counts = plane_ref[held, pl.ds(classes + h, mids, stride=classes), :]
        fold = counts if fold is None else fold + counts
    scale_ref[...] = 1.0 / jnp.maximum(fold, 1.0)
    plane_ref[held] = jnp.zeros(plane_ref.shape[1:], F32)

    def later(here, after):
        return jnp.where(
            lane == LANES - 1,
            pltpu.roll(after, LANES - 1, 1),
            pltpu.roll(here, LANES - 1, 1),
        )

    def rim_rows(at):
        return jnp.where(
            sub < classes, plane_ref[at, 0:8, :], plane_ref[at, mids * classes : mids * classes + 8, :]
        )

    zeros = jnp.zeros((16, LANES), BF16)
    for at in range(held):
        for h in range(classes):
            here = plane_ref[at, pl.ds(classes + h, mids, stride=classes), :]
            after = plane_ref[at + 1, pl.ds(classes + h, mids, stride=classes), :]
            source_ref[h, at] = jnp.concatenate([here, later(here, after)], axis=0).astype(BF16)
        here, after = rim_rows(at), rim_rows(at + 1)
        rim_source_ref[at] = jnp.concatenate([here, later(here, after)], axis=0).astype(BF16)
    for at in (held, held + 1):
        for h in range(classes):
            source_ref[h, at] = zeros
        rim_source_ref[at] = zeros

    own_class = [sub16 % classes == h for h in range(classes)]
    group = 2 * classes
    shape = (mids, vels, LANES)
    rows = mids * vels
    source = lax.broadcasted_iota(jnp.int32, band_ref.shape, 0) - LANES
    target = lax.broadcasted_iota(jnp.int32, band_ref.shape, 1)
    band_ref[...] = jnp.where(jnp.abs(source - target) <= HALF_WIN, 1.0, 0.0).astype(BF16)
    edge = jnp.zeros(window_ref.shape[1:], BF16)
    window_ref[0] = edge
    if last < count:
        window_ref[span + 1] = later_ref[0]
        window_ref[span + 2] = later_ref[1]
    else:
        window_ref[span + 1] = edge

    def moved_out(j, at, where):
        base = [blocks_ref[h, j * span + at] - first for h in range(classes)]
        total = energy = None
        for h in range(classes):
            row = slice(h, h + 1)
            local = jnp.broadcast_to(index_ref[j, row, where], (8, LANES))
            index = jnp.concatenate([local, local], axis=0).astype(jnp.int16)
            low = jnp.broadcast_to(low_ref[j, row, where], (8, LANES))
            high = jnp.broadcast_to(high_ref[j, row, where], (8, LANES))
            inner = index & (LANES - 1)
            got = jnp.where(
                index < LANES,
                take_lanes(source_ref[h, base[h]], inner),
                take_lanes(source_ref[h, base[h] + 1], inner),
            ).astype(F32)
            moved = low * got[:8] + high * got[8:]
            total = moved if total is None else total + moved
            energy = moved * moved if energy is None else energy + moved * moved
        sum_ref[at, pl.ds(j, mids, stride=vels), :] = total
        energy_ref[at, pl.ds(j, mids, stride=vels), :] = energy
        near = rim_source_ref[base[0]]
        far = rim_source_ref[base[0] + 1]
        for h in range(1, classes):
            near = jnp.where(own_class[h], rim_source_ref[base[h]], near)
            far = jnp.where(own_class[h], rim_source_ref[base[h] + 1], far)
        local = index_ref[j, :, where]
        index = jnp.concatenate([local, local], axis=0).astype(jnp.int16)
        inner = index & (LANES - 1)
        got = jnp.where(index < LANES, take_lanes(near, inner), take_lanes(far, inner)).astype(F32)
        rim_ref[at, pl.ds(j, group, stride=vels), :] = (
            low_ref[j, :, where] * got[:8] + high_ref[j, :, where] * got[8:]
        )

    def three(low, mid, high):
        return jnp.concatenate([low, mid[:-1]], axis=0) + mid + jnp.concatenate([mid[1:], high], axis=0)

    begin = 0 if first == 0 else 1
    end = span + 1 if last < count else span
    copies = []
    if first > 0:
        stacked_ref, semblance_ref = stacked_out, semblance_out
    else:
        stacked_ref, semblance_ref, semaphores = staged

        def leave(source, out, begin, end):
            place = out.at[:, :, begin * LANES : end * LANES]
            copies.append(pltpu.make_async_copy(source, place, semaphores.at[len(copies)]))
            copies[-1].start()

        if last < count:
            leave(stacked_later, stacked_out, last, count)
            leave(semblance_later, semblance_out, last + 1, count)

    def per_block(at, _):
        where = pl.ds(pl.multiple_of(at * LANES, LANES), LANES)
        total = sum_ref[at].reshape(shape)
        rim = rim_ref[at].reshape(2, classes, vels, LANES)
        rim_sum = jnp.sum(rim, axis=1)
        rim_power = rim_sum * rim_sum
        rim_energy = jnp.sum(rim * rim, axis=1)
        power = three(rim_power[0:1], total * total, rim_power[1:2])
        energy = three(rim_energy[0:1], energy_ref[at].reshape(shape), rim_energy[1:2])
        window_ref[at + 1, :rows] = power.reshape(rows, LANES).astype(BF16)
        window_ref[at + 1, rows:] = energy.reshape(rows, LANES).astype(BF16)
        for m in range(mids):
            stacked_ref[m, :, where] = (total[m] * scale_ref[m : m + 1, :]).astype(BF16)
        return 0

    def per_window(at, blocks):
        values = jnp.concatenate([window_ref[at + i] for i in range(blocks + 2)], axis=1)
        band = band_ref[: (blocks + 2) * LANES, : blocks * LANES]
        summed = jnp.dot(values, band, preferred_element_type=F32)
        semblance = summed[:rows] / jnp.maximum(classes * summed[rows:], 1.0)
        semblance_ref[:, :, (at - begin) * LANES : (at - begin + blocks) * LANES] = semblance.reshape(
            mids, vels, blocks * LANES
        )

    pieces = PIECES if first == 0 and span % PIECES == 0 else 1
    top, finished = span, end
    for piece in range(pieces):
        low = top - span // pieces

        def per_velocity(j, _, blocks=range(low, top)):
            for at in blocks:
                moved_out(j, at, slice(at * LANES, (at + 1) * LANES))
            return 0

        lax.fori_loop(0, vels, per_velocity, 0, unroll=math.gcd(vels, UNROLL * pieces))
        lax.fori_loop(low, top, per_block, 0, unroll=math.gcd(top - low, 2 * pieces))
        if first == 0:
            leave(stacked_ref.at[:, :, low * LANES : top * LANES], stacked_out, low, top)
        ready = low + 1 if low else begin
        for at in range(ready, finished, 2):
            per_window(at, min(2, finished - at))
        if first == 0:
            leave(semblance_ref.at[:, :, ready * LANES : finished * LANES], semblance_out, ready, finished)
        top, finished = low, ready
    if first > 0:
        carry_ref[0] = window_ref[1]
        carry_ref[1] = window_ref[2]
    for copy in copies:
        copy.wait()


def panels(first, last, count, classes, vels, tables, rows, after, later):
    span = last - first
    held = count - first
    group = 2 * classes
    window_rows = 2 * CMP_DEV * vels
    flat = [piece for chunk in rows for piece in chunk]
    *tables, blocks = tables
    operands = [blocks, *flat, *tables, *after]
    in_specs = [SMEM] + [VMEM] * (len(flat) + len(tables)) + [ANY] * len(after)
    if later is not None:
        stacked, semblance, carry = later
        operands += [carry, stacked, semblance]
        in_specs += [VMEM] * 3
    staged = []
    if first > 0:
        outs = [
            jax.ShapeDtypeStruct((CMP_DEV, vels, span * LANES), BF16),
            jax.ShapeDtypeStruct((CMP_DEV, vels, (span - 1) * LANES), F32),
            jax.ShapeDtypeStruct((2, window_rows, LANES), BF16),
        ]
        specs = [VMEM] * 3
    else:
        outs = [
            jax.ShapeDtypeStruct((CMP_DEV, vels, count * LANES), BF16),
            jax.ShapeDtypeStruct((CMP_DEV, vels, count * LANES), F32),
        ]
        specs = [ANY] * 2
        done = span + (last < count)
        staged = [
            pltpu.VMEM((CMP_DEV, vels, span * LANES), BF16),
            pltpu.VMEM((CMP_DEV, vels, done * LANES), F32),
            pltpu.SemaphoreType.DMA((2 + 2 * PIECES,)),
        ]
    return pl.pallas_call(
        functools.partial(
            panel_kernel, classes, vels, first, last, count, [len(c) for c in rows], len(after)
        ),
        in_specs=in_specs,
        out_specs=specs,
        out_shape=outs,
        scratch_shapes=[
            pltpu.VMEM((held + 1, flat[0].shape[0], LANES), F32),
            pltpu.VMEM((classes, held + 2, 16, LANES), BF16),
            pltpu.VMEM((held + 2, 16, LANES), BF16),
            pltpu.VMEM((span, CMP_DEV * vels, LANES), F32),
            pltpu.VMEM((span, CMP_DEV * vels, LANES), F32),
            pltpu.VMEM((span, group * vels, LANES), F32),
            pltpu.VMEM((span + 3, window_rows, LANES), BF16),
            pltpu.VMEM((CMP_DEV, LANES), F32),
            pltpu.VMEM((4 * LANES, 2 * LANES), BF16),
            *staged,
        ],
        compiler_params=pltpu.CompilerParams(vmem_limit_bytes=VMEM_BYTES),
        cost_estimate=pl.CostEstimate(
            flops=14000 * CMP_DEV * vels * classes * span * LANES,
            bytes_accessed=(1 + span) * 512 * 1024,
            transcendentals=0,
        ),
    )(*operands)


def table_kernel(classes, start, samples, offsets_ref, velocities_ref, *refs):
    index_ref, low_ref, high_ref, blocks_ref, token_ref = refs[-5:]
    token_ref[...] = jnp.zeros(token_ref.shape, F32)
    vels, rows, cols = low_ref.shape
    lane = lax.broadcasted_iota(jnp.int32, (rows, LANES), 1)
    sub = lax.broadcasted_iota(jnp.int32, (rows, LANES), 0)
    offset = jnp.full((rows, LANES), offsets_ref[0], F32)
    for h in range(1, classes):
        offset = jnp.where(sub % classes == h, offsets_ref[h], offset)

    def per_velocity(j, blocks):
        blocks = list(blocks)
        slowness = offset / jnp.full((rows, LANES), velocities_ref[j], F32)
        square = slowness * slowness
        for at in range(cols // LANES):
            begin = start + at * LANES
            first = jnp.sqrt(square + float(begin) * float(begin)) - 0.01
            first = jnp.minimum(jnp.maximum(first, float(begin)), float(samples)).astype(jnp.int32)
            base = first // LANES
            flat = j * (cols // LANES) + at
            for wide in range(len(blocks)):
                blocks[wide] = jnp.where(lane == flat - wide * LANES, base, blocks[wide])
            time = (lane + begin).astype(F32)
            position = jnp.sqrt(time * time + square)
            floored = jnp.floor(position)
            fraction = position - floored
            index = jnp.minimum(floored, float(samples)).astype(jnp.int32)
            where = slice(at * LANES, (at + 1) * LANES)
            index_ref[j, :, where] = index - base * LANES
            low_ref[j, :, where] = (1.0 - fraction).astype(BF16).astype(F32)
            high_ref[j, :, where] = fraction.astype(BF16).astype(F32)
        return tuple(blocks)

    width = blocks_ref.shape[1] // LANES
    blocks = lax.fori_loop(
        0,
        vels,
        per_velocity,
        tuple(jnp.zeros((rows, LANES), jnp.int32) for _ in range(width)),
        unroll=math.gcd(vels, 4),
    )
    for wide in range(width):
        blocks_ref[:, wide * LANES : (wide + 1) * LANES] = blocks[wide]


def moveout(offsets, velocities, samples, start, stop, after):
    vels, classes = velocities.shape[0], offsets.shape[0]
    shape = (vels, 2 * classes, stop - start)
    width = pl.cdiv(vels * (stop - start) // LANES, LANES) * LANES
    return pl.pallas_call(
        functools.partial(table_kernel, classes, start, samples),
        in_specs=[SMEM, SMEM] + [ANY] * len(after),
        out_specs=[VMEM] * 5,
        out_shape=[
            jax.ShapeDtypeStruct(shape, jnp.int32),
            jax.ShapeDtypeStruct(shape, F32),
            jax.ShapeDtypeStruct(shape, F32),
            jax.ShapeDtypeStruct((2 * classes, width), jnp.int32),
            TOKEN,
        ],
        compiler_params=pltpu.CompilerParams(vmem_limit_bytes=VMEM_BYTES),
        cost_estimate=pl.CostEstimate(
            flops=0, bytes_accessed=0, transcendentals=0
        ),
    )(offsets, velocities, *after)


def per_device(traces, owners, midpoint, offset_class, offsets, velocities):
    samples = traces.shape[1]
    classes, vels = offsets.shape[0], velocities.shape[0]
    count = samples // LANES
    key = (owners.reshape(-1) * CMP_DEV + midpoint) * classes + offset_class
    plan = Plan(traces, key, classes)
    cuts = [0, samples // 2, samples]
    chunks = list(zip(cuts[:-1], cuts[1:]))[::-1]
    parts, tokens = [], [plan.places]
    for start, stop in chunks:
        part, token = plan.bin(start, stop - start, stop == samples, tokens[-1:])
        parts.append(part)
        tokens.append(token)
    tables, spreads = [], []
    *table, token = moveout(offsets, velocities, samples, *chunks[0], tokens[-1:])
    tables.append(table)
    tokens.append(token)
    for at in range(len(chunks)):
        part = plan.exchange(0, parts[at])
        for place in range(1, len(plan.orders[0])):
            part, token = plan.merge(part, tokens[-1:])
            part = plan.exchange(place, part)
            tokens.append(token)
        spreads.append(part)
    rows, tokens = [], []
    for at, part in enumerate(spreads):
        if at:
            *table, token = moveout(offsets, velocities, samples, *chunks[at], tokens[-1:])
            tables.append(table)
            tokens.append(token)
        *spread, token = plan.spread(part, tokens[-1:])
        rows.append(plan.across(spread, at > 0))
        tokens.append(token)
    out = None
    for at, (start, stop) in enumerate(chunks):
        out = panels(
            start // LANES,
            stop // LANES,
            count,
            classes,
            vels,
            tables[at],
            rows[: at + 1][::-1],
            tokens[-1:] if not at else [],
            out,
        )
    return (out[0], out[1])


def solution(mesh):
    in_specs = (
        P(("inline", "xline"), None),
        P(("inline", "xline"), None),
        P(("inline", "xline")),
        P(("inline", "xline")),
        P(),
        P(),
    )
    out_specs = (P(("inline", "xline"), None, None), P(("inline", "xline"), None, None))
    return jax.shard_map(
        per_device, mesh=mesh, in_specs=in_specs, out_specs=out_specs, check_vma=False
    )
```

```python
import functools
import math

import jax
import jax.numpy as jnp
from jax import lax
from jax.experimental import pallas as pl
from jax.experimental.pallas import tpu as pltpu
from jax.sharding import PartitionSpec as P

HALF_WIN = 4
CMP_DEV = 8
LANES = 128
UNROLL = 8
PIECES = 2
VMEM_BYTES = 16 * 1024 * 1024
F32 = jnp.float32
BF16 = jnp.bfloat16
VMEM = pl.BlockSpec(memory_space=pltpu.VMEM)
SMEM = pl.BlockSpec(memory_space=pltpu.SMEM)
ANY = pl.BlockSpec(memory_space=pl.ANY)
TOKEN = jax.ShapeDtypeStruct((8, LANES), F32)

LANE_GATHER = lax.GatherDimensionNumbers(
    offset_dims=(),
    collapsed_slice_dims=(1,),
    start_index_map=(1,),
    operand_batching_dims=(0,),
    start_indices_batching_dims=(0,),
)


def take_lanes(rows, index):
    return lax.gather(
        rows,
        index[..., None],
        LANE_GATHER,
        (1, 1),
        mode=lax.GatherScatterMode.PROMISE_IN_BOUNDS,
    )


def bin_kernel(orders, count, kept_rows, *refs):
    members, data = refs[:orders], refs[orders : orders + count]
    outs, token_ref = refs[-2 * orders - 1 : -1], refs[-1]
    token_ref[...] = jnp.zeros(token_ref.shape, F32)
    per, cols = data[0].shape
    width = cols // orders
    tile = math.gcd(width, 256)
    for order in range(orders):
        member_ref = members[order]
        kept_ref, sent_ref = outs[2 * order : 2 * order + 2]
        rows = member_ref.shape[0]
        for start in range(0, kept_ref.shape[1], tile):
            stop = min(start + tile, kept_ref.shape[1])
            total = None
            for at, block in enumerate(data):
                if start < width:
                    values = block[:, order * width + start : order * width + stop]
                else:
                    values = jnp.ones((per, stop - start), BF16)
                part = jnp.dot(
                    member_ref[:, at * per : (at + 1) * per], values, preferred_element_type=F32
                )
                total = part if total is None else total + part
            kept_ref[:, start:stop] = total[:kept_rows]
            if kept_rows < rows:
                sent_ref[:, start:stop] = total[kept_rows:].astype(BF16)
            else:
                sent_ref[:, start:stop] = jnp.zeros((sent_ref.shape[0], stop - start), BF16)


def bin_rows(members, data, start, cols, counted, kept_rows, after):
    rows = members[0].shape[0]
    per = data[0].shape[0]
    sent_rows = max(rows - kept_rows, 16)
    in_specs = [pl.BlockSpec(member.shape, lambda t: (0, 0)) for member in members]
    in_specs += [pl.BlockSpec((per, cols), lambda t: (0, start // cols))] * len(data)
    in_specs += [ANY] * len(after)
    shapes = []
    for at in range(len(members)):
        width = cols // len(members) + (LANES if counted and at == len(members) - 1 else 0)
        shapes.append(jax.ShapeDtypeStruct((kept_rows, width), F32))
        shapes.append(jax.ShapeDtypeStruct((sent_rows, width), BF16))
    shapes.append(TOKEN)
    outs = pl.pallas_call(
        functools.partial(bin_kernel, len(members), len(data), kept_rows),
        grid=(1,),
        in_specs=in_specs,
        out_specs=[pl.BlockSpec(shape.shape, lambda t: (0, 0)) for shape in shapes],
        out_shape=shapes,
        compiler_params=pltpu.CompilerParams(vmem_limit_bytes=VMEM_BYTES),
        cost_estimate=pl.CostEstimate(
            flops=2 * rows * len(data) * per * cols,
            bytes_accessed=0,
            transcendentals=0,
        ),
    )(*members, *data, *after)
    return list(zip(outs[0:-1:2], outs[1:-1:2])), outs[-1]


def member_kernel(places_ref, *refs):
    for at, member_ref in enumerate(refs):
        row = lax.broadcasted_iota(jnp.int32, member_ref.shape, 0)
        own = jnp.broadcast_to(places_ref[2 * at : 2 * at + 1, :], row.shape)
        rim = jnp.broadcast_to(places_ref[2 * at + 1 : 2 * at + 2, :], row.shape)
        member_ref[...] = jnp.where((row == own) | (row == rim), 1.0, 0.0).astype(BF16)


def members_of(places, rows):
    places = jnp.stack(places)
    count = places.shape[0] // 2
    return pl.pallas_call(
        member_kernel,
        in_specs=[VMEM],
        out_specs=[VMEM] * count,
        out_shape=[jax.ShapeDtypeStruct((rows, places.shape[1]), BF16)] * count,
        compiler_params=pltpu.CompilerParams(vmem_limit_bytes=VMEM_BYTES),
        cost_estimate=pl.CostEstimate(
            flops=540 * rows * places.size // 2, bytes_accessed=0, transcendentals=0
        ),
    )(places)


def steps_of(count):
    return range(count - 1, 0, -1)


def target_of(place, step, count):
    return place ^ step if count & (count - 1) == 0 else (place + step) % count


class Plan:
    def __init__(self, traces, key, classes):
        self.inline = lax.axis_size("inline")
        self.xline = lax.axis_size("xline")
        self.me = lax.axis_index("inline")
        self.classes = classes
        self.dev_rows = CMP_DEV * classes
        self.line_rows = self.xline * self.dev_rows
        bits = [1 << b for b in range(self.inline.bit_length() - 1)]
        self.core, others = bits[0], bits[1:]
        self.orders = [others, others[::-1]] if len(others) > 1 else [others]
        self.codes = 1 << len(others)
        unit = 8 if self.codes % 4 == 0 else 16
        self.block_rows = -(-(self.line_rows + 2 * classes) // unit) * unit
        self.data = [traces, self.swap(traces, self.core)]
        self.keys = jnp.concatenate([key, self.swap(key, self.core)]).reshape(-1)
        self.members = members_of(
            [place for order in self.orders for place in self.places_of(order)],
            self.codes * self.block_rows,
        )

    def swap(self, value, bit):
        return lax.ppermute(value, "inline", [(i, i ^ bit) for i in range(self.inline)])

    def places_of(self, order):
        classes, line_rows = self.classes, self.line_rows
        line, local = self.keys // line_rows, self.keys % line_rows

        def row_of(target, row):
            apart = target ^ self.me
            code = jnp.zeros_like(target)
            for bit in order:
                code = code * 2 + jnp.where(apart & bit != 0, 1, 0)
            valid = (apart & self.core == 0) & (target >= 0) & (target < self.inline)
            return jnp.where(valid, code * self.block_rows + row, -1)

        own = row_of(line, local + classes)
        rim = jnp.where(
            local >= line_rows - classes,
            row_of(line + 1, local - (line_rows - classes)),
            jnp.where(local < classes, row_of(line - 1, local + classes + line_rows), -1),
        )
        return own, rim

    def bin(self, start, cols, counted, after):
        rows = self.codes * self.block_rows
        kept_rows = rows // 2 if self.orders[0] else rows
        return bin_rows(self.members, self.data, start, cols, counted, kept_rows, after)

    def exchange(self, place, parts):
        return [
            (kept, self.swap(sent, order[place])) for order, (kept, sent) in zip(self.orders, parts)
        ]

    def pairs(self):
        places = range(self.xline)
        return [[(i, int(target_of(i, step, self.xline))) for i in places] for step in steps_of(self.xline)]

    def merge(self, parts, after):
        half = parts[0][0].shape[0] // 2
        shapes = []
        for kept, _ in parts:
            shapes.append(jax.ShapeDtypeStruct((half, kept.shape[1]), F32))
            shapes.append(jax.ShapeDtypeStruct((half, kept.shape[1]), BF16))
        flat = [value for part in parts for value in part]
        outs = pl.pallas_call(
            functools.partial(merge_kernel, len(parts)),
            in_specs=[VMEM] * len(flat) + [ANY] * len(after),
            out_specs=[VMEM] * (len(shapes) + 1),
            out_shape=shapes + [TOKEN],
            compiler_params=pltpu.CompilerParams(vmem_limit_bytes=VMEM_BYTES),
            cost_estimate=cost_of(flat),
        )(*flat, *after)
        return list(zip(outs[0:-1:2], outs[1:-1:2])), outs[-1]

    def spread(self, parts, after):
        window = self.dev_rows + 2 * self.classes
        cols = sum(kept.shape[1] for kept, _ in parts)
        flat = [value for part in parts for value in part]
        kinds = [F32] + [BF16] * (self.xline - 1)
        return pl.pallas_call(
            functools.partial(spread_kernel, len(parts), self.xline, self.dev_rows),
            in_specs=[VMEM] * len(flat) + [ANY] * len(after),
            out_specs=[VMEM] * (len(kinds) + 1),
            out_shape=[jax.ShapeDtypeStruct((window, cols), kind) for kind in kinds] + [TOKEN],
            scratch_shapes=[pltpu.VMEM((parts[0][0].shape[0], cols), F32)],
            compiler_params=pltpu.CompilerParams(vmem_limit_bytes=VMEM_BYTES),
            cost_estimate=cost_of(flat),
        )(*flat, *after)

    def across(self, blocks, near_first):
        own, *sent = blocks
        moves = list(zip(sent, self.pairs()))
        if near_first:
            moves = moves[::-1]
        return [own] + [lax.ppermute(block, "xline", pairs) for block, pairs in moves]


def cost_of(values):
    size = sum(value.size * value.dtype.itemsize for value in values)
    return pl.CostEstimate(flops=0, bytes_accessed=2 * size, transcendentals=0)


def merge_kernel(count, *refs):
    ins, outs, token_ref = refs[: 2 * count], refs[-2 * count - 1 : -1], refs[-1]
    token_ref[...] = jnp.zeros(token_ref.shape, F32)
    for at in range(count):
        kept, sent = ins[2 * at : 2 * at + 2]
        half = kept.shape[0] // 2
        total = kept[...] + sent[...].astype(F32)
        outs[2 * at][...] = total[:half]
        outs[2 * at + 1][...] = total[half:].astype(BF16)


def spread_kernel(count, blocks, stride, *refs):
    ins, outs, token_ref, total_ref = refs[: 2 * count], refs[-blocks - 2 : -2], refs[-2], refs[-1]
    token_ref[...] = jnp.zeros(token_ref.shape, F32)
    start = 0
    for at in range(count):
        kept, sent = ins[2 * at : 2 * at + 2]
        stop = start + kept.shape[1]
        total_ref[:, start:stop] = kept[...] + sent[...].astype(F32)
        start = stop
    me = lax.axis_index("xline")
    places = [me] + [target_of(me, step, blocks) for step in steps_of(blocks)]
    for place, out in zip(places, outs):
        place = pl.multiple_of(place * stride, 8)
        out[...] = total_ref[pl.ds(place, out.shape[0]), :].astype(out.dtype)


def panel_kernel(classes, vels, first, last, count, pieces, waits, *refs):
    blocks_ref = refs[0]
    at = 1
    chunk_refs = []
    for number in pieces:
        chunk_refs.append(refs[at : at + number])
        at += number
    index_ref, low_ref, high_ref = refs[at : at + 3]
    at += 3 + waits
    if last < count:
        later_ref, stacked_later, semblance_later = refs[at : at + 3]
        at += 3
    stacked_out, semblance_out = refs[at : at + 2]
    at += 2
    if first > 0:
        carry_ref = refs[at]
        at += 1
    (
        plane_ref,
        source_ref,
        rim_source_ref,
        sum_ref,
        energy_ref,
        rim_ref,
        window_ref,
        scale_ref,
        band_ref,
        *staged,
    ) = refs[at:]
    mids = CMP_DEV
    span = last - first
    held = count - first
    lane = lax.broadcasted_iota(jnp.int32, (8, LANES), 1)
    sub = lax.broadcasted_iota(jnp.int32, (8, LANES), 0)
    sub16 = lax.broadcasted_iota(jnp.int32, (16, LANES), 0)

    block_at = 0
    for piece_refs in chunk_refs:
        for inner in range(piece_refs[0].shape[1] // LANES):
            where = slice(inner * LANES, (inner + 1) * LANES)
            block = piece_refs[0][:, where]
            for piece_ref in piece_refs[1:]:
                block = block + piece_ref[:, where].astype(F32)
            plane_ref[block_at] = block.astype(BF16).astype(F32) if block_at < held else block
            block_at += 1
    fold = None
    for h in range(classes):
        counts = plane_ref[held, pl.ds(classes + h, mids, stride=classes), :]
        fold = counts if fold is None else fold + counts
    scale_ref[...] = 1.0 / jnp.maximum(fold, 1.0)
    plane_ref[held] = jnp.zeros(plane_ref.shape[1:], F32)

    def later(here, after):
        return jnp.where(
            lane == LANES - 1,
            pltpu.roll(after, LANES - 1, 1),
            pltpu.roll(here, LANES - 1, 1),
        )

    def rim_rows(at):
        return jnp.where(
            sub < classes, plane_ref[at, 0:8, :], plane_ref[at, mids * classes : mids * classes + 8, :]
        )

    zeros = jnp.zeros((16, LANES), BF16)
    for at in range(held):
        for h in range(classes):
            here = plane_ref[at, pl.ds(classes + h, mids, stride=classes), :]
            after = plane_ref[at + 1, pl.ds(classes + h, mids, stride=classes), :]
            source_ref[h, at] = jnp.concatenate([here, later(here, after)], axis=0).astype(BF16)
        here, after = rim_rows(at), rim_rows(at + 1)
        rim_source_ref[at] = jnp.concatenate([here, later(here, after)], axis=0).astype(BF16)
    for at in (held, held + 1):
        for h in range(classes):
            source_ref[h, at] = zeros
        rim_source_ref[at] = zeros

    own_class = [sub16 % classes == h for h in range(classes)]
    group = 2 * classes
    shape = (mids, vels, LANES)
    rows = mids * vels
    source = lax.broadcasted_iota(jnp.int32, band_ref.shape, 0) - LANES
    target = lax.broadcasted_iota(jnp.int32, band_ref.shape, 1)
    band_ref[...] = jnp.where(jnp.abs(source - target) <= HALF_WIN, 1.0, 0.0).astype(BF16)
    edge = jnp.zeros(window_ref.shape[1:], BF16)
    window_ref[0] = edge
    if last < count:
        window_ref[span + 1] = later_ref[0]
        window_ref[span + 2] = later_ref[1]
    else:
        window_ref[span + 1] = edge

    def moved_out(j, at, where):
        base = [blocks_ref[h, j * span + at] - first for h in range(classes)]
        total = energy = None
        for h in range(classes):
            row = slice(h, h + 1)
            local = jnp.broadcast_to(index_ref[j, row, where], (8, LANES))
            index = jnp.concatenate([local, local], axis=0).astype(jnp.int16)
            low = jnp.broadcast_to(low_ref[j, row, where], (8, LANES))
            high = jnp.broadcast_to(high_ref[j, row, where], (8, LANES))
            inner = index & (LANES - 1)
            got = jnp.where(
                index < LANES,
                take_lanes(source_ref[h, base[h]], inner),
                take_lanes(source_ref[h, base[h] + 1], inner),
            ).astype(F32)
            moved = low * got[:8] + high * got[8:]
            total = moved if total is None else total + moved
            energy = moved * moved if energy is None else energy + moved * moved
        sum_ref[at, pl.ds(j, mids, stride=vels), :] = total
        energy_ref[at, pl.ds(j, mids, stride=vels), :] = energy
        near = rim_source_ref[base[0]]
        far = rim_source_ref[base[0] + 1]
        for h in range(1, classes):
            near = jnp.where(own_class[h], rim_source_ref[base[h]], near)
            far = jnp.where(own_class[h], rim_source_ref[base[h] + 1], far)
        local = index_ref[j, :, where]
        index = jnp.concatenate([local, local], axis=0).astype(jnp.int16)
        inner = index & (LANES - 1)
        got = jnp.where(index < LANES, take_lanes(near, inner), take_lanes(far, inner)).astype(F32)
        rim_ref[at, pl.ds(j, group, stride=vels), :] = (
            low_ref[j, :, where] * got[:8] + high_ref[j, :, where] * got[8:]
        )

    def three(low, mid, high):
        return jnp.concatenate([low, mid[:-1]], axis=0) + mid + jnp.concatenate([mid[1:], high], axis=0)

    begin = 0 if first == 0 else 1
    end = span + 1 if last < count else span
    copies = []
    if first > 0:
        stacked_ref, semblance_ref = stacked_out, semblance_out
    else:
        stacked_ref, semblance_ref, semaphores = staged

        def leave(source, out, begin, end):
            place = out.at[:, :, begin * LANES : end * LANES]
            copies.append(pltpu.make_async_copy(source, place, semaphores.at[len(copies)]))
            copies[-1].start()

        if last < count:
            leave(stacked_later, stacked_out, last, count)
            leave(semblance_later, semblance_out, last + 1, count)

    def per_block(at, _):
        where = pl.ds(pl.multiple_of(at * LANES, LANES), LANES)
        total = sum_ref[at].reshape(shape)
        rim = rim_ref[at].reshape(2, classes, vels, LANES)
        rim_sum = jnp.sum(rim, axis=1)
        rim_power = rim_sum * rim_sum
        rim_energy = jnp.sum(rim * rim, axis=1)
        power = three(rim_power[0:1], total * total, rim_power[1:2])
        energy = three(rim_energy[0:1], energy_ref[at].reshape(shape), rim_energy[1:2])
        window_ref[at + 1, :rows] = power.reshape(rows, LANES).astype(BF16)
        window_ref[at + 1, rows:] = energy.reshape(rows, LANES).astype(BF16)
        for m in range(mids):
            stacked_ref[m, :, where] = (total[m] * scale_ref[m : m + 1, :]).astype(BF16)
        return 0

    def per_window(at, blocks):
        values = jnp.concatenate([window_ref[at + i] for i in range(blocks + 2)], axis=1)
        band = band_ref[: (blocks + 2) * LANES, : blocks * LANES]
        summed = jnp.dot(values, band, preferred_element_type=F32)
        semblance = summed[:rows] / jnp.maximum(classes * summed[rows:], 1.0)
        semblance_ref[:, :, (at - begin) * LANES : (at - begin + blocks) * LANES] = semblance.reshape(
            mids, vels, blocks * LANES
        )

    pieces = PIECES if first == 0 and span % PIECES == 0 else 1
    top, finished = span, end
    for piece in range(pieces):
        low = top - span // pieces

        def per_velocity(j, _, blocks=range(low, top)):
            for at in blocks:
                moved_out(j, at, slice(at * LANES, (at + 1) * LANES))
            return 0

        lax.fori_loop(0, vels, per_velocity, 0, unroll=math.gcd(vels, UNROLL * pieces))
        lax.fori_loop(low, top, per_block, 0, unroll=math.gcd(top - low, 2 * pieces))
        if first == 0:
            leave(stacked_ref.at[:, :, low * LANES : top * LANES], stacked_out, low, top)
        ready = low + 1 if low else begin
        for at in range(ready, finished, 2):
            per_window(at, min(2, finished - at))
        if first == 0:
            leave(semblance_ref.at[:, :, ready * LANES : finished * LANES], semblance_out, ready, finished)
        top, finished = low, ready
    if first > 0:
        carry_ref[0] = window_ref[1]
        carry_ref[1] = window_ref[2]
    for copy in copies:
        copy.wait()


def panels(first, last, count, classes, vels, tables, rows, after, later):
    span = last - first
    held = count - first
    group = 2 * classes
    window_rows = 2 * CMP_DEV * vels
    flat = [piece for chunk in rows for piece in chunk]
    *tables, blocks = tables
    operands = [blocks, *flat, *tables, *after]
    in_specs = [SMEM] + [VMEM] * (len(flat) + len(tables)) + [ANY] * len(after)
    if later is not None:
        stacked, semblance, carry = later
        operands += [carry, stacked, semblance]
        in_specs += [VMEM] * 3
    staged = []
    if first > 0:
        outs = [
            jax.ShapeDtypeStruct((CMP_DEV, vels, span * LANES), BF16),
            jax.ShapeDtypeStruct((CMP_DEV, vels, (span - 1) * LANES), F32),
            jax.ShapeDtypeStruct((2, window_rows, LANES), BF16),
        ]
        specs = [VMEM] * 3
    else:
        outs = [
            jax.ShapeDtypeStruct((CMP_DEV, vels, count * LANES), BF16),
            jax.ShapeDtypeStruct((CMP_DEV, vels, count * LANES), F32),
        ]
        specs = [ANY] * 2
        done = span + (last < count)
        staged = [
            pltpu.VMEM((CMP_DEV, vels, span * LANES), BF16),
            pltpu.VMEM((CMP_DEV, vels, done * LANES), F32),
            pltpu.SemaphoreType.DMA((2 + 2 * PIECES,)),
        ]
    return pl.pallas_call(
        functools.partial(
            panel_kernel, classes, vels, first, last, count, [len(c) for c in rows], len(after)
        ),
        in_specs=in_specs,
        out_specs=specs,
        out_shape=outs,
        scratch_shapes=[
            pltpu.VMEM((held + 1, flat[0].shape[0], LANES), F32),
            pltpu.VMEM((classes, held + 2, 16, LANES), BF16),
            pltpu.VMEM((held + 2, 16, LANES), BF16),
            pltpu.VMEM((span, CMP_DEV * vels, LANES), F32),
            pltpu.VMEM((span, CMP_DEV * vels, LANES), F32),
            pltpu.VMEM((span, group * vels, LANES), F32),
            pltpu.VMEM((span + 3, window_rows, LANES), BF16),
            pltpu.VMEM((CMP_DEV, LANES), F32),
            pltpu.VMEM((4 * LANES, 2 * LANES), BF16),
            *staged,
        ],
        compiler_params=pltpu.CompilerParams(vmem_limit_bytes=VMEM_BYTES),
        cost_estimate=pl.CostEstimate(
            flops=14000 * CMP_DEV * vels * classes * span * LANES,
            bytes_accessed=(1 + span) * 512 * 1024,
            transcendentals=0,
        ),
    )(*operands)


def table_kernel(classes, start, samples, offsets_ref, velocities_ref, *refs):
    index_ref, low_ref, high_ref, blocks_ref, token_ref = refs[-5:]
    token_ref[...] = jnp.zeros(token_ref.shape, F32)
    vels, rows, cols = low_ref.shape
    lane = lax.broadcasted_iota(jnp.int32, (rows, LANES), 1)
    sub = lax.broadcasted_iota(jnp.int32, (rows, LANES), 0)
    offset = jnp.full((rows, LANES), offsets_ref[0], F32)
    for h in range(1, classes):
        offset = jnp.where(sub % classes == h, offsets_ref[h], offset)

    def per_velocity(j, blocks):
        blocks = list(blocks)
        slowness = offset / jnp.full((rows, LANES), velocities_ref[j], F32)
        square = slowness * slowness
        for at in range(cols // LANES):
            begin = start + at * LANES
            first = jnp.sqrt(square + float(begin) * float(begin)) - 0.01
            first = jnp.minimum(jnp.maximum(first, float(begin)), float(samples)).astype(jnp.int32)
            base = first // LANES
            flat = j * (cols // LANES) + at
            for wide in range(len(blocks)):
                blocks[wide] = jnp.where(lane == flat - wide * LANES, base, blocks[wide])
            time = (lane + begin).astype(F32)
            position = jnp.sqrt(time * time + square)
            floored = jnp.floor(position)
            fraction = position - floored
            index = jnp.minimum(floored, float(samples)).astype(jnp.int32)
            where = slice(at * LANES, (at + 1) * LANES)
            index_ref[j, :, where] = index - base * LANES
            low_ref[j, :, where] = (1.0 - fraction).astype(BF16).astype(F32)
            high_ref[j, :, where] = fraction.astype(BF16).astype(F32)
        return tuple(blocks)

    width = blocks_ref.shape[1] // LANES
    blocks = lax.fori_loop(
        0,
        vels,
        per_velocity,
        tuple(jnp.zeros((rows, LANES), jnp.int32) for _ in range(width)),
        unroll=math.gcd(vels, 4),
    )
    for wide in range(width):
        blocks_ref[:, wide * LANES : (wide + 1) * LANES] = blocks[wide]


def moveout(offsets, velocities, samples, start, stop, after):
    vels, classes = velocities.shape[0], offsets.shape[0]
    shape = (vels, 2 * classes, stop - start)
    width = pl.cdiv(vels * (stop - start) // LANES, LANES) * LANES
    return pl.pallas_call(
        functools.partial(table_kernel, classes, start, samples),
        in_specs=[SMEM, SMEM] + [ANY] * len(after),
        out_specs=[VMEM] * 5,
        out_shape=[
            jax.ShapeDtypeStruct(shape, jnp.int32),
            jax.ShapeDtypeStruct(shape, F32),
            jax.ShapeDtypeStruct(shape, F32),
            jax.ShapeDtypeStruct((2 * classes, width), jnp.int32),
            TOKEN,
        ],
        compiler_params=pltpu.CompilerParams(vmem_limit_bytes=VMEM_BYTES),
        cost_estimate=pl.CostEstimate(
            flops=0, bytes_accessed=0, transcendentals=0
        ),
    )(offsets, velocities, *after)


def per_device(traces, owners, midpoint, offset_class, offsets, velocities):
    samples = traces.shape[1]
    classes, vels = offsets.shape[0], velocities.shape[0]
    count = samples // LANES
    key = (owners * CMP_DEV + midpoint[:, None]) * classes + offset_class[:, None]
    plan = Plan(traces, key, classes)
    cuts = [0, samples // 2, samples]
    chunks = list(zip(cuts[:-1], cuts[1:]))[::-1]
    parts, tokens = [], []
    for start, stop in chunks:
        part, token = plan.bin(start, stop - start, stop == samples, tokens[-1:])
        parts.append(part)
        tokens.append(token)
    tables, spreads = [], []
    *table, token = moveout(offsets, velocities, samples, *chunks[0], tokens[-1:])
    tables.append(table)
    tokens.append(token)
    for at in range(len(chunks)):
        part = plan.exchange(0, parts[at])
        for place in range(1, len(plan.orders[0])):
            part, token = plan.merge(part, tokens[-1:])
            part = plan.exchange(place, part)
            tokens.append(token)
        spreads.append(part)
    rows = []
    for at, part in enumerate(spreads):
        if at:
            *table, token = moveout(offsets, velocities, samples, *chunks[at], tokens[-1:])
            tables.append(table)
            tokens.append(token)
        *spread, token = plan.spread(part, tokens[-1:])
        rows.append(plan.across(spread, at > 0))
        tokens.append(token)
    out = None
    for at, (start, stop) in enumerate(chunks):
        out = panels(
            start // LANES,
            stop // LANES,
            count,
            classes,
            vels,
            tables[at],
            rows[: at + 1][::-1],
            tokens[-1:] if not at else [],
            out,
        )
    return (out[0], out[1])


def solution(mesh):
    in_specs = (
        P(("inline", "xline"), None),
        P(("inline", "xline"), None),
        P(("inline", "xline")),
        P(("inline", "xline")),
        P(),
        P(),
    )
    out_specs = (P(("inline", "xline"), None, None), P(("inline", "xline"), None, None))
    return jax.shard_map(
        per_device, mesh=mesh, in_specs=in_specs, out_specs=out_specs, check_vma=False
    )
```

```python
import functools
import math

import jax
import jax.numpy as jnp
from jax import lax
from jax.experimental import pallas as pl
from jax.experimental.pallas import tpu as pltpu
from jax.sharding import PartitionSpec as P

HALF_WIN = 4
CMP_DEV = 8
LANES = 128
UNROLL = 8
PIECES = 4
VMEM_BYTES = 16 * 1024 * 1024
F32 = jnp.float32
BF16 = jnp.bfloat16
VMEM = pl.BlockSpec(memory_space=pltpu.VMEM)
SMEM = pl.BlockSpec(memory_space=pltpu.SMEM)
ANY = pl.BlockSpec(memory_space=pl.ANY)
TOKEN = jax.ShapeDtypeStruct((8, LANES), F32)

LANE_GATHER = lax.GatherDimensionNumbers(
    offset_dims=(),
    collapsed_slice_dims=(1,),
    start_index_map=(1,),
    operand_batching_dims=(0,),
    start_indices_batching_dims=(0,),
)


def take_lanes(rows, index):
    return lax.gather(
        rows,
        index[..., None],
        LANE_GATHER,
        (1, 1),
        mode=lax.GatherScatterMode.PROMISE_IN_BOUNDS,
    )


def bin_kernel(orders, count, kept_rows, *refs):
    members, data = refs[:orders], refs[orders : orders + count]
    outs, token_ref = refs[-2 * orders - 1 : -1], refs[-1]
    token_ref[...] = jnp.zeros(token_ref.shape, F32)
    per, cols = data[0].shape
    width = cols // orders
    tile = math.gcd(width, 256)
    for order in range(orders):
        member_ref = members[order]
        kept_ref, sent_ref = outs[2 * order : 2 * order + 2]
        rows = member_ref.shape[0]
        for start in range(0, kept_ref.shape[1], tile):
            stop = min(start + tile, kept_ref.shape[1])
            total = None
            for at, block in enumerate(data):
                if start < width:
                    values = block[:, order * width + start : order * width + stop]
                else:
                    values = jnp.ones((per, stop - start), BF16)
                part = jnp.dot(
                    member_ref[:, at * per : (at + 1) * per], values, preferred_element_type=F32
                )
                total = part if total is None else total + part
            kept_ref[:, start:stop] = total[:kept_rows]
            if kept_rows < rows:
                sent_ref[:, start:stop] = total[kept_rows:].astype(BF16)
            else:
                sent_ref[:, start:stop] = jnp.zeros((sent_ref.shape[0], stop - start), BF16)


def bin_rows(members, data, start, cols, counted, kept_rows, after):
    rows = members[0].shape[0]
    per = data[0].shape[0]
    sent_rows = max(rows - kept_rows, 16)
    in_specs = [pl.BlockSpec(member.shape, lambda t: (0, 0)) for member in members]
    in_specs += [pl.BlockSpec((per, cols), lambda t: (0, start // cols))] * len(data)
    in_specs += [ANY] * len(after)
    shapes = []
    for at in range(len(members)):
        width = cols // len(members) + (LANES if counted and at == len(members) - 1 else 0)
        shapes.append(jax.ShapeDtypeStruct((kept_rows, width), F32))
        shapes.append(jax.ShapeDtypeStruct((sent_rows, width), BF16))
    shapes.append(TOKEN)
    outs = pl.pallas_call(
        functools.partial(bin_kernel, len(members), len(data), kept_rows),
        grid=(1,),
        in_specs=in_specs,
        out_specs=[pl.BlockSpec(shape.shape, lambda t: (0, 0)) for shape in shapes],
        out_shape=shapes,
        compiler_params=pltpu.CompilerParams(vmem_limit_bytes=VMEM_BYTES),
        cost_estimate=pl.CostEstimate(
            flops=2 * rows * len(data) * per * cols,
            bytes_accessed=0,
            transcendentals=0,
        ),
    )(*members, *data, *after)
    return list(zip(outs[0:-1:2], outs[1:-1:2])), outs[-1]


def member_kernel(places_ref, *refs):
    for at, member_ref in enumerate(refs):
        row = lax.broadcasted_iota(jnp.int32, member_ref.shape, 0)
        own = jnp.broadcast_to(places_ref[2 * at : 2 * at + 1, :], row.shape)
        rim = jnp.broadcast_to(places_ref[2 * at + 1 : 2 * at + 2, :], row.shape)
        member_ref[...] = jnp.where((row == own) | (row == rim), 1.0, 0.0).astype(BF16)


def members_of(places, rows):
    places = jnp.stack(places)
    count = places.shape[0] // 2
    return pl.pallas_call(
        member_kernel,
        in_specs=[VMEM],
        out_specs=[VMEM] * count,
        out_shape=[jax.ShapeDtypeStruct((rows, places.shape[1]), BF16)] * count,
        compiler_params=pltpu.CompilerParams(vmem_limit_bytes=VMEM_BYTES),
        cost_estimate=pl.CostEstimate(
            flops=540 * rows * places.size // 2, bytes_accessed=0, transcendentals=0
        ),
    )(places)


def steps_of(count):
    return range(count - 1, 0, -1)


def target_of(place, step, count):
    return place ^ step if count & (count - 1) == 0 else (place + step) % count


class Plan:
    def __init__(self, traces, key, classes):
        self.inline = lax.axis_size("inline")
        self.xline = lax.axis_size("xline")
        self.me = lax.axis_index("inline")
        self.classes = classes
        self.dev_rows = CMP_DEV * classes
        self.line_rows = self.xline * self.dev_rows
        bits = [1 << b for b in range(self.inline.bit_length() - 1)]
        self.core, others = bits[0], bits[1:]
        self.orders = [others, others[::-1]] if len(others) > 1 else [others]
        self.codes = 1 << len(others)
        unit = 8 if self.codes % 4 == 0 else 16
        self.block_rows = -(-(self.line_rows + 2 * classes) // unit) * unit
        self.data = [traces, self.swap(traces, self.core)]
        self.keys = jnp.concatenate([key, self.swap(key, self.core)]).reshape(-1)
        self.members = members_of(
            [place for order in self.orders for place in self.places_of(order)],
            self.codes * self.block_rows,
        )

    def swap(self, value, bit):
        return lax.ppermute(value, "inline", [(i, i ^ bit) for i in range(self.inline)])

    def places_of(self, order):
        classes, line_rows = self.classes, self.line_rows
        line, local = self.keys // line_rows, self.keys % line_rows

        def row_of(target, row):
            apart = target ^ self.me
            code = jnp.zeros_like(target)
            for bit in order:
                code = code * 2 + jnp.where(apart & bit != 0, 1, 0)
            valid = (apart & self.core == 0) & (target >= 0) & (target < self.inline)
            return jnp.where(valid, code * self.block_rows + row, -1)

        own = row_of(line, local + classes)
        rim = jnp.where(
            local >= line_rows - classes,
            row_of(line + 1, local - (line_rows - classes)),
            jnp.where(local < classes, row_of(line - 1, local + classes + line_rows), -1),
        )
        return own, rim

    def bin(self, start, cols, counted, after):
        rows = self.codes * self.block_rows
        kept_rows = rows // 2 if self.orders[0] else rows
        return bin_rows(self.members, self.data, start, cols, counted, kept_rows, after)

    def exchange(self, place, parts):
        return [
            (kept, self.swap(sent, order[place])) for order, (kept, sent) in zip(self.orders, parts)
        ]

    def pairs(self):
        places = range(self.xline)
        return [[(i, int(target_of(i, step, self.xline))) for i in places] for step in steps_of(self.xline)]

    def merge(self, parts, after):
        half = parts[0][0].shape[0] // 2
        shapes = []
        for kept, _ in parts:
            shapes.append(jax.ShapeDtypeStruct((half, kept.shape[1]), F32))
            shapes.append(jax.ShapeDtypeStruct((half, kept.shape[1]), BF16))
        flat = [value for part in parts for value in part]
        outs = pl.pallas_call(
            functools.partial(merge_kernel, len(parts)),
            in_specs=[VMEM] * len(flat) + [ANY] * len(after),
            out_specs=[VMEM] * (len(shapes) + 1),
            out_shape=shapes + [TOKEN],
            compiler_params=pltpu.CompilerParams(vmem_limit_bytes=VMEM_BYTES),
            cost_estimate=cost_of(flat),
        )(*flat, *after)
        return list(zip(outs[0:-1:2], outs[1:-1:2])), outs[-1]

    def spread(self, parts, after):
        window = self.dev_rows + 2 * self.classes
        cols = sum(kept.shape[1] for kept, _ in parts)
        flat = [value for part in parts for value in part]
        kinds = [F32] + [BF16] * (self.xline - 1)
        return pl.pallas_call(
            functools.partial(spread_kernel, len(parts), self.xline, self.dev_rows),
            in_specs=[VMEM] * len(flat) + [ANY] * len(after),
            out_specs=[VMEM] * (len(kinds) + 1),
            out_shape=[jax.ShapeDtypeStruct((window, cols), kind) for kind in kinds] + [TOKEN],
            scratch_shapes=[pltpu.VMEM((parts[0][0].shape[0], cols), F32)],
            compiler_params=pltpu.CompilerParams(vmem_limit_bytes=VMEM_BYTES),
            cost_estimate=cost_of(flat),
        )(*flat, *after)

    def across(self, blocks, near_first):
        own, *sent = blocks
        moves = list(zip(sent, self.pairs()))
        if near_first:
            moves = moves[::-1]
        return [own] + [lax.ppermute(block, "xline", pairs) for block, pairs in moves]


def cost_of(values):
    size = sum(value.size * value.dtype.itemsize for value in values)
    return pl.CostEstimate(flops=0, bytes_accessed=2 * size, transcendentals=0)


def merge_kernel(count, *refs):
    ins, outs, token_ref = refs[: 2 * count], refs[-2 * count - 1 : -1], refs[-1]
    token_ref[...] = jnp.zeros(token_ref.shape, F32)
    for at in range(count):
        kept, sent = ins[2 * at : 2 * at + 2]
        half = kept.shape[0] // 2
        total = kept[...] + sent[...].astype(F32)
        outs[2 * at][...] = total[:half]
        outs[2 * at + 1][...] = total[half:].astype(BF16)


def spread_kernel(count, blocks, stride, *refs):
    ins, outs, token_ref, total_ref = refs[: 2 * count], refs[-blocks - 2 : -2], refs[-2], refs[-1]
    token_ref[...] = jnp.zeros(token_ref.shape, F32)
    start = 0
    for at in range(count):
        kept, sent = ins[2 * at : 2 * at + 2]
        stop = start + kept.shape[1]
        total_ref[:, start:stop] = kept[...] + sent[...].astype(F32)
        start = stop
    me = lax.axis_index("xline")
    places = [me] + [target_of(me, step, blocks) for step in steps_of(blocks)]
    for place, out in zip(places, outs):
        place = pl.multiple_of(place * stride, 8)
        out[...] = total_ref[pl.ds(place, out.shape[0]), :].astype(out.dtype)


def panel_kernel(classes, vels, first, last, count, pieces, waits, *refs):
    blocks_ref = refs[0]
    at = 1
    chunk_refs = []
    for number in pieces:
        chunk_refs.append(refs[at : at + number])
        at += number
    index_ref, low_ref, high_ref = refs[at : at + 3]
    at += 3 + waits
    if last < count:
        later_ref, stacked_later, semblance_later = refs[at : at + 3]
        at += 3
    stacked_out, semblance_out = refs[at : at + 2]
    at += 2
    if first > 0:
        carry_ref = refs[at]
        at += 1
    (
        plane_ref,
        source_ref,
        rim_source_ref,
        sum_ref,
        energy_ref,
        rim_ref,
        window_ref,
        scale_ref,
        band_ref,
        *staged,
    ) = refs[at:]
    mids = CMP_DEV
    span = last - first
    held = count - first
    lane = lax.broadcasted_iota(jnp.int32, (8, LANES), 1)
    sub = lax.broadcasted_iota(jnp.int32, (8, LANES), 0)
    sub16 = lax.broadcasted_iota(jnp.int32, (16, LANES), 0)

    block_at = 0
    for piece_refs in chunk_refs:
        for inner in range(piece_refs[0].shape[1] // LANES):
            where = slice(inner * LANES, (inner + 1) * LANES)
            block = piece_refs[0][:, where]
            for piece_ref in piece_refs[1:]:
                block = block + piece_ref[:, where].astype(F32)
            plane_ref[block_at] = block.astype(BF16).astype(F32) if block_at < held else block
            block_at += 1
    fold = None
    for h in range(classes):
        counts = plane_ref[held, pl.ds(classes + h, mids, stride=classes), :]
        fold = counts if fold is None else fold + counts
    scale_ref[...] = 1.0 / jnp.maximum(fold, 1.0)
    plane_ref[held] = jnp.zeros(plane_ref.shape[1:], F32)

    def later(here, after):
        return jnp.where(
            lane == LANES - 1,
            pltpu.roll(after, LANES - 1, 1),
            pltpu.roll(here, LANES - 1, 1),
        )

    def rim_rows(at):
        return jnp.where(
            sub < classes, plane_ref[at, 0:8, :], plane_ref[at, mids * classes : mids * classes + 8, :]
        )

    zeros = jnp.zeros((16, LANES), BF16)
    for at in range(held):
        for h in range(classes):
            here = plane_ref[at, pl.ds(classes + h, mids, stride=classes), :]
            after = plane_ref[at + 1, pl.ds(classes + h, mids, stride=classes), :]
            source_ref[h, at] = jnp.concatenate([here, later(here, after)], axis=0).astype(BF16)
        here, after = rim_rows(at), rim_rows(at + 1)
        rim_source_ref[at] = jnp.concatenate([here, later(here, after)], axis=0).astype(BF16)
    for at in (held, held + 1):
        for h in range(classes):
            source_ref[h, at] = zeros
        rim_source_ref[at] = zeros

    own_class = [sub16 % classes == h for h in range(classes)]
    group = 2 * classes
    shape = (mids, vels, LANES)
    rows = mids * vels
    source = lax.broadcasted_iota(jnp.int32, band_ref.shape, 0) - LANES
    target = lax.broadcasted_iota(jnp.int32, band_ref.shape, 1)
    band_ref[...] = jnp.where(jnp.abs(source - target) <= HALF_WIN, 1.0, 0.0).astype(BF16)
    edge = jnp.zeros(window_ref.shape[1:], BF16)
    window_ref[0] = edge
    if last < count:
        window_ref[span + 1] = later_ref[0]
        window_ref[span + 2] = later_ref[1]
    else:
        window_ref[span + 1] = edge

    def moved_out(j, at, where):
        base = [blocks_ref[h, j * span + at] - first for h in range(classes)]
        total = energy = None
        for h in range(classes):
            row = slice(h, h + 1)
            local = jnp.broadcast_to(index_ref[j, row, where], (8, LANES))
            index = jnp.concatenate([local, local], axis=0).astype(jnp.int16)
            low = jnp.broadcast_to(low_ref[j, row, where], (8, LANES))
            high = jnp.broadcast_to(high_ref[j, row, where], (8, LANES))
            inner = index & (LANES - 1)
            got = jnp.where(
                index < LANES,
                take_lanes(source_ref[h, base[h]], inner),
                take_lanes(source_ref[h, base[h] + 1], inner),
            ).astype(F32)
            moved = low * got[:8] + high * got[8:]
            total = moved if total is None else total + moved
            energy = moved * moved if energy is None else energy + moved * moved
        sum_ref[at, pl.ds(j, mids, stride=vels), :] = total
        energy_ref[at, pl.ds(j, mids, stride=vels), :] = energy
        near = rim_source_ref[base[0]]
        far = rim_source_ref[base[0] + 1]
        for h in range(1, classes):
            near = jnp.where(own_class[h], rim_source_ref[base[h]], near)
            far = jnp.where(own_class[h], rim_source_ref[base[h] + 1], far)
        local = index_ref[j, :, where]
        index = jnp.concatenate([local, local], axis=0).astype(jnp.int16)
        inner = index & (LANES - 1)
        got = jnp.where(index < LANES, take_lanes(near, inner), take_lanes(far, inner)).astype(F32)
        rim_ref[at, pl.ds(j, group, stride=vels), :] = (
            low_ref[j, :, where] * got[:8] + high_ref[j, :, where] * got[8:]
        )

    def three(low, mid, high):
        return jnp.concatenate([low, mid[:-1]], axis=0) + mid + jnp.concatenate([mid[1:], high], axis=0)

    begin = 0 if first == 0 else 1
    end = span + 1 if last < count else span
    copies = []
    if first > 0:
        stacked_ref, semblance_ref = stacked_out, semblance_out
    else:
        stacked_ref, semblance_ref, semaphores = staged

        def leave(source, out, begin, end):
            place = out.at[:, :, begin * LANES : end * LANES]
            copies.append(pltpu.make_async_copy(source, place, semaphores.at[len(copies)]))
            copies[-1].start()

        if last < count:
            leave(stacked_later, stacked_out, last, count)
            leave(semblance_later, semblance_out, last + 1, count)

    def per_block(at, _):
        where = pl.ds(pl.multiple_of(at * LANES, LANES), LANES)
        total = sum_ref[at].reshape(shape)
        rim = rim_ref[at].reshape(2, classes, vels, LANES)
        rim_sum = jnp.sum(rim, axis=1)
        rim_power = rim_sum * rim_sum
        rim_energy = jnp.sum(rim * rim, axis=1)
        power = three(rim_power[0:1], total * total, rim_power[1:2])
        energy = three(rim_energy[0:1], energy_ref[at].reshape(shape), rim_energy[1:2])
        window_ref[at + 1, :rows] = power.reshape(rows, LANES).astype(BF16)
        window_ref[at + 1, rows:] = energy.reshape(rows, LANES).astype(BF16)
        for m in range(mids):
            stacked_ref[m, :, where] = (total[m] * scale_ref[m : m + 1, :]).astype(BF16)
        return 0

    def per_window(at, blocks):
        values = jnp.concatenate([window_ref[at + i] for i in range(blocks + 2)], axis=1)
        band = band_ref[: (blocks + 2) * LANES, : blocks * LANES]
        summed = jnp.dot(values, band, preferred_element_type=F32)
        semblance = summed[:rows] / jnp.maximum(classes * summed[rows:], 1.0)
        semblance_ref[:, :, (at - begin) * LANES : (at - begin + blocks) * LANES] = semblance.reshape(
            mids, vels, blocks * LANES
        )

    pieces = PIECES if first == 0 and span % PIECES == 0 else 1
    top, finished = span, end
    for piece in range(pieces):
        low = top - span // pieces

        def per_velocity(j, _, blocks=range(low, top)):
            for at in blocks:
                moved_out(j, at, slice(at * LANES, (at + 1) * LANES))
            return 0

        lax.fori_loop(0, vels, per_velocity, 0, unroll=math.gcd(vels, UNROLL * pieces))
        lax.fori_loop(low, top, per_block, 0, unroll=math.gcd(top - low, 2 * pieces))
        if first == 0:
            leave(stacked_ref.at[:, :, low * LANES : top * LANES], stacked_out, low, top)
        ready = low + 1 if low else begin
        for at in range(ready, finished, 2):
            per_window(at, min(2, finished - at))
        if first == 0:
            leave(semblance_ref.at[:, :, ready * LANES : finished * LANES], semblance_out, ready, finished)
        top, finished = low, ready
    if first > 0:
        carry_ref[0] = window_ref[1]
        carry_ref[1] = window_ref[2]
    for copy in copies:
        copy.wait()


def panels(first, last, count, classes, vels, tables, rows, after, later):
    span = last - first
    held = count - first
    group = 2 * classes
    window_rows = 2 * CMP_DEV * vels
    flat = [piece for chunk in rows for piece in chunk]
    *tables, blocks = tables
    operands = [blocks, *flat, *tables, *after]
    in_specs = [SMEM] + [VMEM] * (len(flat) + len(tables)) + [ANY] * len(after)
    if later is not None:
        stacked, semblance, carry = later
        operands += [carry, stacked, semblance]
        in_specs += [VMEM] * 3
    staged = []
    if first > 0:
        outs = [
            jax.ShapeDtypeStruct((CMP_DEV, vels, span * LANES), BF16),
            jax.ShapeDtypeStruct((CMP_DEV, vels, (span - 1) * LANES), F32),
            jax.ShapeDtypeStruct((2, window_rows, LANES), BF16),
        ]
        specs = [VMEM] * 3
    else:
        outs = [
            jax.ShapeDtypeStruct((CMP_DEV, vels, count * LANES), BF16),
            jax.ShapeDtypeStruct((CMP_DEV, vels, count * LANES), F32),
        ]
        specs = [ANY] * 2
        done = span + (last < count)
        staged = [
            pltpu.VMEM((CMP_DEV, vels, span * LANES), BF16),
            pltpu.VMEM((CMP_DEV, vels, done * LANES), F32),
            pltpu.SemaphoreType.DMA((2 + 2 * PIECES,)),
        ]
    return pl.pallas_call(
        functools.partial(
            panel_kernel, classes, vels, first, last, count, [len(c) for c in rows], len(after)
        ),
        in_specs=in_specs,
        out_specs=specs,
        out_shape=outs,
        scratch_shapes=[
            pltpu.VMEM((held + 1, flat[0].shape[0], LANES), F32),
            pltpu.VMEM((classes, held + 2, 16, LANES), BF16),
            pltpu.VMEM((held + 2, 16, LANES), BF16),
            pltpu.VMEM((span, CMP_DEV * vels, LANES), F32),
            pltpu.VMEM((span, CMP_DEV * vels, LANES), F32),
            pltpu.VMEM((span, group * vels, LANES), F32),
            pltpu.VMEM((span + 3, window_rows, LANES), BF16),
            pltpu.VMEM((CMP_DEV, LANES), F32),
            pltpu.VMEM((4 * LANES, 2 * LANES), BF16),
            *staged,
        ],
        compiler_params=pltpu.CompilerParams(vmem_limit_bytes=VMEM_BYTES),
        cost_estimate=pl.CostEstimate(
            flops=14000 * CMP_DEV * vels * classes * span * LANES,
            bytes_accessed=(1 + span) * 512 * 1024,
            transcendentals=0,
        ),
    )(*operands)


def table_kernel(classes, start, samples, offsets_ref, velocities_ref, *refs):
    index_ref, low_ref, high_ref, blocks_ref, token_ref = refs[-5:]
    token_ref[...] = jnp.zeros(token_ref.shape, F32)
    vels, rows, cols = low_ref.shape
    lane = lax.broadcasted_iota(jnp.int32, (rows, LANES), 1)
    sub = lax.broadcasted_iota(jnp.int32, (rows, LANES), 0)
    offset = jnp.full((rows, LANES), offsets_ref[0], F32)
    for h in range(1, classes):
        offset = jnp.where(sub % classes == h, offsets_ref[h], offset)

    def per_velocity(j, blocks):
        blocks = list(blocks)
        slowness = offset / jnp.full((rows, LANES), velocities_ref[j], F32)
        square = slowness * slowness
        for at in range(cols // LANES):
            begin = start + at * LANES
            first = jnp.sqrt(square + float(begin) * float(begin)) - 0.01
            first = jnp.minimum(jnp.maximum(first, float(begin)), float(samples)).astype(jnp.int32)
            base = first // LANES
            flat = j * (cols // LANES) + at
            for wide in range(len(blocks)):
                blocks[wide] = jnp.where(lane == flat - wide * LANES, base, blocks[wide])
            time = (lane + begin).astype(F32)
            position = jnp.sqrt(time * time + square)
            floored = jnp.floor(position)
            fraction = position - floored
            index = jnp.minimum(floored, float(samples)).astype(jnp.int32)
            where = slice(at * LANES, (at + 1) * LANES)
            index_ref[j, :, where] = index - base * LANES
            low_ref[j, :, where] = (1.0 - fraction).astype(BF16).astype(F32)
            high_ref[j, :, where] = fraction.astype(BF16).astype(F32)
        return tuple(blocks)

    width = blocks_ref.shape[1] // LANES
    blocks = lax.fori_loop(
        0,
        vels,
        per_velocity,
        tuple(jnp.zeros((rows, LANES), jnp.int32) for _ in range(width)),
        unroll=math.gcd(vels, 4),
    )
    for wide in range(width):
        blocks_ref[:, wide * LANES : (wide + 1) * LANES] = blocks[wide]


def moveout(offsets, velocities, samples, start, stop, after):
    vels, classes = velocities.shape[0], offsets.shape[0]
    shape = (vels, 2 * classes, stop - start)
    width = pl.cdiv(vels * (stop - start) // LANES, LANES) * LANES
    return pl.pallas_call(
        functools.partial(table_kernel, classes, start, samples),
        in_specs=[SMEM, SMEM] + [ANY] * len(after),
        out_specs=[VMEM] * 5,
        out_shape=[
            jax.ShapeDtypeStruct(shape, jnp.int32),
            jax.ShapeDtypeStruct(shape, F32),
            jax.ShapeDtypeStruct(shape, F32),
            jax.ShapeDtypeStruct((2 * classes, width), jnp.int32),
            TOKEN,
        ],
        compiler_params=pltpu.CompilerParams(vmem_limit_bytes=VMEM_BYTES),
        cost_estimate=pl.CostEstimate(
            flops=0, bytes_accessed=0, transcendentals=0
        ),
    )(offsets, velocities, *after)


def per_device(traces, owners, midpoint, offset_class, offsets, velocities):
    samples = traces.shape[1]
    classes, vels = offsets.shape[0], velocities.shape[0]
    count = samples // LANES
    key = (owners * CMP_DEV + midpoint[:, None]) * classes + offset_class[:, None]
    plan = Plan(traces, key, classes)
    cuts = [0, samples // 2, samples]
    chunks = list(zip(cuts[:-1], cuts[1:]))[::-1]
    parts, tokens = [], []
    for start, stop in chunks:
        part, token = plan.bin(start, stop - start, stop == samples, tokens[-1:])
        parts.append(part)
        tokens.append(token)
    tables, spreads = [], []
    *table, token = moveout(offsets, velocities, samples, *chunks[0], tokens[-1:])
    tables.append(table)
    tokens.append(token)
    for at in range(len(chunks)):
        part = plan.exchange(0, parts[at])
        for place in range(1, len(plan.orders[0])):
            part, token = plan.merge(part, tokens[-1:])
            part = plan.exchange(place, part)
            tokens.append(token)
        spreads.append(part)
    rows = []
    for at, part in enumerate(spreads):
        *spread, token = plan.spread(part, tokens[-1:])
        tokens.append(token)
        rows.append(plan.across(spread, at > 0))
        if at:
            *table, token = moveout(offsets, velocities, samples, *chunks[at], tokens[-1:])
            tables.append(table)
            tokens.append(token)
    out = None
    for at, (start, stop) in enumerate(chunks):
        out = panels(
            start // LANES,
            stop // LANES,
            count,
            classes,
            vels,
            tables[at],
            rows[: at + 1][::-1],
            tokens[-1:] if not at else [],
            out,
        )
    return (out[0], out[1])


def solution(mesh):
    in_specs = (
        P(("inline", "xline"), None),
        P(("inline", "xline"), None),
        P(("inline", "xline")),
        P(("inline", "xline")),
        P(),
        P(),
    )
    out_specs = (P(("inline", "xline"), None, None), P(("inline", "xline"), None, None))
    return jax.shard_map(
        per_device, mesh=mesh, in_specs=in_specs, out_specs=out_specs, check_vma=False
    )
```

```python
import functools
import math

import jax
import jax.numpy as jnp
from jax import lax
from jax.experimental import pallas as pl
from jax.experimental.pallas import tpu as pltpu
from jax.sharding import PartitionSpec as P

HALF_WIN = 4
CMP_DEV = 8
LANES = 128
UNROLL = 8
PIECES = 4
VMEM_BYTES = 16 * 1024 * 1024
F32 = jnp.float32
BF16 = jnp.bfloat16
VMEM = pl.BlockSpec(memory_space=pltpu.VMEM)
SMEM = pl.BlockSpec(memory_space=pltpu.SMEM)
ANY = pl.BlockSpec(memory_space=pl.ANY)
TOKEN = jax.ShapeDtypeStruct((8, LANES), F32)

LANE_GATHER = lax.GatherDimensionNumbers(
    offset_dims=(),
    collapsed_slice_dims=(1,),
    start_index_map=(1,),
    operand_batching_dims=(0,),
    start_indices_batching_dims=(0,),
)


def take_lanes(rows, index):
    return lax.gather(
        rows,
        index[..., None],
        LANE_GATHER,
        (1, 1),
        mode=lax.GatherScatterMode.PROMISE_IN_BOUNDS,
    )


def bin_kernel(orders, count, kept_rows, *refs):
    members, data = refs[:orders], refs[orders : orders + count]
    outs, token_ref = refs[-2 * orders - 1 : -1], refs[-1]
    token_ref[...] = jnp.zeros(token_ref.shape, F32)
    per, cols = data[0].shape
    width = cols // orders
    tile = math.gcd(width, 256)
    for order in range(orders):
        member_ref = members[order]
        kept_ref, sent_ref = outs[2 * order : 2 * order + 2]
        rows = member_ref.shape[0]
        for start in range(0, kept_ref.shape[1], tile):
            stop = min(start + tile, kept_ref.shape[1])
            total = None
            for at, block in enumerate(data):
                if start < width:
                    values = block[:, order * width + start : order * width + stop]
                else:
                    values = jnp.ones((per, stop - start), BF16)
                part = jnp.dot(
                    member_ref[:, at * per : (at + 1) * per], values, preferred_element_type=F32
                )
                total = part if total is None else total + part
            kept_ref[:, start:stop] = total[:kept_rows]
            if kept_rows < rows:
                sent_ref[:, start:stop] = total[kept_rows:].astype(BF16)
            else:
                sent_ref[:, start:stop] = jnp.zeros((sent_ref.shape[0], stop - start), BF16)


def bin_rows(members, data, start, cols, counted, kept_rows, after):
    rows = members[0].shape[0]
    per = data[0].shape[0]
    sent_rows = max(rows - kept_rows, 16)
    in_specs = [pl.BlockSpec(member.shape, lambda t: (0, 0)) for member in members]
    in_specs += [pl.BlockSpec((per, cols), lambda t: (0, start // cols))] * len(data)
    in_specs += [ANY] * len(after)
    shapes = []
    for at in range(len(members)):
        width = cols // len(members) + (LANES if counted and at == len(members) - 1 else 0)
        shapes.append(jax.ShapeDtypeStruct((kept_rows, width), F32))
        shapes.append(jax.ShapeDtypeStruct((sent_rows, width), BF16))
    shapes.append(TOKEN)
    outs = pl.pallas_call(
        functools.partial(bin_kernel, len(members), len(data), kept_rows),
        grid=(1,),
        in_specs=in_specs,
        out_specs=[pl.BlockSpec(shape.shape, lambda t: (0, 0)) for shape in shapes],
        out_shape=shapes,
        compiler_params=pltpu.CompilerParams(vmem_limit_bytes=VMEM_BYTES),
        cost_estimate=pl.CostEstimate(
            flops=2 * rows * len(data) * per * cols,
            bytes_accessed=0,
            transcendentals=0,
        ),
    )(*members, *data, *after)
    return list(zip(outs[0:-1:2], outs[1:-1:2])), outs[-1]


def member_kernel(places_ref, *refs):
    for at, member_ref in enumerate(refs):
        row = lax.broadcasted_iota(jnp.int32, member_ref.shape, 0)
        own = jnp.broadcast_to(places_ref[2 * at : 2 * at + 1, :], row.shape)
        rim = jnp.broadcast_to(places_ref[2 * at + 1 : 2 * at + 2, :], row.shape)
        member_ref[...] = jnp.where((row == own) | (row == rim), 1.0, 0.0).astype(BF16)


def members_of(places, rows):
    places = jnp.stack(places)
    count = places.shape[0] // 2
    return pl.pallas_call(
        member_kernel,
        in_specs=[VMEM],
        out_specs=[VMEM] * count,
        out_shape=[jax.ShapeDtypeStruct((rows, places.shape[1]), BF16)] * count,
        compiler_params=pltpu.CompilerParams(vmem_limit_bytes=VMEM_BYTES),
        cost_estimate=pl.CostEstimate(
            flops=540 * rows * places.size // 2, bytes_accessed=0, transcendentals=0
        ),
    )(places)


def steps_of(count):
    return range(count - 1, 0, -1)


def target_of(place, step, count):
    return place ^ step if count & (count - 1) == 0 else (place + step) % count


class Plan:
    def __init__(self, traces, key, classes):
        self.inline = lax.axis_size("inline")
        self.xline = lax.axis_size("xline")
        self.me = lax.axis_index("inline")
        self.classes = classes
        self.dev_rows = CMP_DEV * classes
        self.line_rows = self.xline * self.dev_rows
        bits = [1 << b for b in range(self.inline.bit_length() - 1)]
        self.core, others = bits[0], bits[1:]
        self.orders = [others, others[::-1]] if len(others) > 1 else [others]
        self.codes = 1 << len(others)
        unit = 8 if self.codes % 4 == 0 else 16
        self.block_rows = -(-(self.line_rows + 2 * classes) // unit) * unit
        self.data = [traces, self.swap(traces, self.core)]
        self.keys = jnp.concatenate([key, self.swap(key, self.core)]).reshape(-1)
        self.members = members_of(
            [place for order in self.orders for place in self.places_of(order)],
            self.codes * self.block_rows,
        )

    def swap(self, value, bit):
        return lax.ppermute(value, "inline", [(i, i ^ bit) for i in range(self.inline)])

    def places_of(self, order):
        classes, line_rows = self.classes, self.line_rows
        line, local = self.keys // line_rows, self.keys % line_rows

        def row_of(target, row):
            apart = target ^ self.me
            code = jnp.zeros_like(target)
            for bit in order:
                code = code * 2 + jnp.where(apart & bit != 0, 1, 0)
            valid = (apart & self.core == 0) & (target >= 0) & (target < self.inline)
            return jnp.where(valid, code * self.block_rows + row, -1)

        own = row_of(line, local + classes)
        rim = jnp.where(
            local >= line_rows - classes,
            row_of(line + 1, local - (line_rows - classes)),
            jnp.where(local < classes, row_of(line - 1, local + classes + line_rows), -1),
        )
        return own, rim

    def bin(self, start, cols, counted, after):
        rows = self.codes * self.block_rows
        kept_rows = rows // 2 if self.orders[0] else rows
        return bin_rows(self.members, self.data, start, cols, counted, kept_rows, after)

    def exchange(self, place, parts):
        return [
            (kept, self.swap(sent, order[place])) for order, (kept, sent) in zip(self.orders, parts)
        ]

    def pairs(self):
        places = range(self.xline)
        return [[(i, int(target_of(i, step, self.xline))) for i in places] for step in steps_of(self.xline)]

    def merge(self, parts, after):
        half = parts[0][0].shape[0] // 2
        shapes = []
        for kept, _ in parts:
            shapes.append(jax.ShapeDtypeStruct((half, kept.shape[1]), F32))
            shapes.append(jax.ShapeDtypeStruct((half, kept.shape[1]), BF16))
        flat = [value for part in parts for value in part]
        outs = pl.pallas_call(
            functools.partial(merge_kernel, len(parts)),
            in_specs=[VMEM] * len(flat) + [ANY] * len(after),
            out_specs=[VMEM] * (len(shapes) + 1),
            out_shape=shapes + [TOKEN],
            compiler_params=pltpu.CompilerParams(vmem_limit_bytes=VMEM_BYTES),
            cost_estimate=cost_of(flat),
        )(*flat, *after)
        return list(zip(outs[0:-1:2], outs[1:-1:2])), outs[-1]

    def spread(self, parts, after):
        window = self.dev_rows + 2 * self.classes
        cols = sum(kept.shape[1] for kept, _ in parts)
        flat = [value for part in parts for value in part]
        kinds = [F32] + [BF16] * (self.xline - 1)
        return pl.pallas_call(
            functools.partial(spread_kernel, len(parts), self.xline, self.dev_rows),
            in_specs=[VMEM] * len(flat) + [ANY] * len(after),
            out_specs=[VMEM] * (len(kinds) + 1),
            out_shape=[jax.ShapeDtypeStruct((window, cols), kind) for kind in kinds] + [TOKEN],
            scratch_shapes=[pltpu.VMEM((parts[0][0].shape[0], cols), F32)],
            compiler_params=pltpu.CompilerParams(vmem_limit_bytes=VMEM_BYTES),
            cost_estimate=cost_of(flat),
        )(*flat, *after)

    def across(self, blocks, near_first):
        own, *sent = blocks
        moves = list(zip(sent, self.pairs()))
        if near_first:
            moves = moves[::-1]
        return [own] + [lax.ppermute(block, "xline", pairs) for block, pairs in moves]


def cost_of(values):
    size = sum(value.size * value.dtype.itemsize for value in values)
    return pl.CostEstimate(flops=0, bytes_accessed=2 * size, transcendentals=0)


def merge_kernel(count, *refs):
    ins, outs, token_ref = refs[: 2 * count], refs[-2 * count - 1 : -1], refs[-1]
    token_ref[...] = jnp.zeros(token_ref.shape, F32)
    for at in range(count):
        kept, sent = ins[2 * at : 2 * at + 2]
        half = kept.shape[0] // 2
        total = kept[...] + sent[...].astype(F32)
        outs[2 * at][...] = total[:half]
        outs[2 * at + 1][...] = total[half:].astype(BF16)


def spread_kernel(count, blocks, stride, *refs):
    ins, outs, token_ref, total_ref = refs[: 2 * count], refs[-blocks - 2 : -2], refs[-2], refs[-1]
    token_ref[...] = jnp.zeros(token_ref.shape, F32)
    start = 0
    for at in range(count):
        kept, sent = ins[2 * at : 2 * at + 2]
        stop = start + kept.shape[1]
        total_ref[:, start:stop] = kept[...] + sent[...].astype(F32)
        start = stop
    me = lax.axis_index("xline")
    places = [me] + [target_of(me, step, blocks) for step in steps_of(blocks)]
    for place, out in zip(places, outs):
        place = pl.multiple_of(place * stride, 8)
        out[...] = total_ref[pl.ds(place, out.shape[0]), :].astype(out.dtype)


def panel_kernel(classes, vels, first, last, count, pieces, waits, *refs):
    blocks_ref = refs[0]
    at = 1
    chunk_refs = []
    for number in pieces:
        chunk_refs.append(refs[at : at + number])
        at += number
    index_ref, low_ref, high_ref = refs[at : at + 3]
    at += 3 + waits
    if last < count:
        later_ref, stacked_later, semblance_later = refs[at : at + 3]
        at += 3
    stacked_out, semblance_out = refs[at : at + 2]
    at += 2
    if first > 0:
        carry_ref = refs[at]
        at += 1
    (
        plane_ref,
        source_ref,
        rim_source_ref,
        sum_ref,
        energy_ref,
        rim_ref,
        window_ref,
        scale_ref,
        band_ref,
        *staged,
    ) = refs[at:]
    mids = CMP_DEV
    span = last - first
    held = count - first
    lane = lax.broadcasted_iota(jnp.int32, (8, LANES), 1)
    sub = lax.broadcasted_iota(jnp.int32, (8, LANES), 0)
    sub16 = lax.broadcasted_iota(jnp.int32, (16, LANES), 0)

    block_at = 0
    for piece_refs in chunk_refs:
        for inner in range(piece_refs[0].shape[1] // LANES):
            where = slice(inner * LANES, (inner + 1) * LANES)
            block = piece_refs[0][:, where]
            for piece_ref in piece_refs[1:]:
                block = block + piece_ref[:, where].astype(F32)
            plane_ref[block_at] = block.astype(BF16).astype(F32) if block_at < held else block
            block_at += 1
    fold = None
    for h in range(classes):
        counts = plane_ref[held, pl.ds(classes + h, mids, stride=classes), :]
        fold = counts if fold is None else fold + counts
    scale_ref[...] = 1.0 / jnp.maximum(fold, 1.0)
    plane_ref[held] = jnp.zeros(plane_ref.shape[1:], F32)

    def later(here, after):
        return jnp.where(
            lane == LANES - 1,
            pltpu.roll(after, LANES - 1, 1),
            pltpu.roll(here, LANES - 1, 1),
        )

    def rim_rows(at):
        return jnp.where(
            sub < classes, plane_ref[at, 0:8, :], plane_ref[at, mids * classes : mids * classes + 8, :]
        )

    zeros = jnp.zeros((16, LANES), BF16)
    for at in range(held):
        for h in range(classes):
            here = plane_ref[at, pl.ds(classes + h, mids, stride=classes), :]
            after = plane_ref[at + 1, pl.ds(classes + h, mids, stride=classes), :]
            source_ref[h, at] = jnp.concatenate([here, later(here, after)], axis=0).astype(BF16)
        here, after = rim_rows(at), rim_rows(at + 1)
        rim_source_ref[at] = jnp.concatenate([here, later(here, after)], axis=0).astype(BF16)
    for at in (held, held + 1):
        for h in range(classes):
            source_ref[h, at] = zeros
        rim_source_ref[at] = zeros

    own_class = [sub16 % classes == h for h in range(classes)]
    group = 2 * classes
    shape = (mids, vels, LANES)
    rows = mids * vels
    source = lax.broadcasted_iota(jnp.int32, band_ref.shape, 0) - LANES
    target = lax.broadcasted_iota(jnp.int32, band_ref.shape, 1)
    band_ref[...] = jnp.where(jnp.abs(source - target) <= HALF_WIN, 1.0, 0.0).astype(BF16)
    edge = jnp.zeros(window_ref.shape[1:], BF16)
    window_ref[0] = edge
    if last < count:
        window_ref[span + 1] = later_ref[0]
        window_ref[span + 2] = later_ref[1]
    else:
        window_ref[span + 1] = edge

    def moved_out(j, at, where):
        base = [blocks_ref[h, j * span + at] - first for h in range(classes)]
        total = energy = None
        for h in range(classes):
            row = slice(h, h + 1)
            local = jnp.broadcast_to(index_ref[j, row, where], (8, LANES))
            index = jnp.concatenate([local, local], axis=0).astype(jnp.int16)
            low = jnp.broadcast_to(low_ref[j, row, where], (8, LANES))
            high = jnp.broadcast_to(high_ref[j, row, where], (8, LANES))
            inner = index & (LANES - 1)
            got = jnp.where(
                index < LANES,
                take_lanes(source_ref[h, base[h]], inner),
                take_lanes(source_ref[h, base[h] + 1], inner),
            ).astype(F32)
            moved = low * got[:8] + high * got[8:]
            total = moved if total is None else total + moved
            energy = moved * moved if energy is None else energy + moved * moved
        sum_ref[at, pl.ds(j, mids, stride=vels), :] = total
        energy_ref[at, pl.ds(j, mids, stride=vels), :] = energy
        near = rim_source_ref[base[0]]
        far = rim_source_ref[base[0] + 1]
        for h in range(1, classes):
            near = jnp.where(own_class[h], rim_source_ref[base[h]], near)
            far = jnp.where(own_class[h], rim_source_ref[base[h] + 1], far)
        local = index_ref[j, :, where]
        index = jnp.concatenate([local, local], axis=0).astype(jnp.int16)
        inner = index & (LANES - 1)
        got = jnp.where(index < LANES, take_lanes(near, inner), take_lanes(far, inner)).astype(F32)
        rim_ref[at, pl.ds(j, group, stride=vels), :] = (
            low_ref[j, :, where] * got[:8] + high_ref[j, :, where] * got[8:]
        )

    def three(low, mid, high):
        return jnp.concatenate([low, mid[:-1]], axis=0) + mid + jnp.concatenate([mid[1:], high], axis=0)

    begin = 0 if first == 0 else 1
    end = span + 1 if last < count else span
    copies = []
    if first > 0:
        stacked_ref, semblance_ref = stacked_out, semblance_out
    else:
        stacked_ref, semblance_ref, semaphores = staged

        def leave(source, out, begin, end):
            place = out.at[:, :, begin * LANES : end * LANES]
            copies.append(pltpu.make_async_copy(source, place, semaphores.at[len(copies)]))
            copies[-1].start()

        if last < count:
            leave(stacked_later, stacked_out, last, count)
            leave(semblance_later, semblance_out, last + 1, count)

    def per_block(at, _):
        where = pl.ds(pl.multiple_of(at * LANES, LANES), LANES)
        total = sum_ref[at].reshape(shape)
        rim = rim_ref[at].reshape(2, classes, vels, LANES)
        rim_sum = jnp.sum(rim, axis=1)
        rim_power = rim_sum * rim_sum
        rim_energy = jnp.sum(rim * rim, axis=1)
        power = three(rim_power[0:1], total * total, rim_power[1:2])
        energy = three(rim_energy[0:1], energy_ref[at].reshape(shape), rim_energy[1:2])
        window_ref[at + 1, :rows] = power.reshape(rows, LANES).astype(BF16)
        window_ref[at + 1, rows:] = energy.reshape(rows, LANES).astype(BF16)
        for m in range(mids):
            stacked_ref[m, :, where] = (total[m] * scale_ref[m : m + 1, :]).astype(BF16)
        return 0

    def per_window(at, blocks):
        values = jnp.concatenate([window_ref[at + i] for i in range(blocks + 2)], axis=1)
        band = band_ref[: (blocks + 2) * LANES, : blocks * LANES]
        summed = jnp.dot(values, band, preferred_element_type=F32)
        semblance = summed[:rows] / jnp.maximum(classes * summed[rows:], 1.0)
        semblance_ref[:, :, (at - begin) * LANES : (at - begin + blocks) * LANES] = semblance.reshape(
            mids, vels, blocks * LANES
        )

    pieces = PIECES if first == 0 and span % PIECES == 0 else 1
    top, finished = span, end
    for piece in range(pieces):
        low = top - span // pieces

        def per_velocity(j, _, blocks=range(low, top)):
            for at in blocks:
                moved_out(j, at, slice(at * LANES, (at + 1) * LANES))
            return 0

        lax.fori_loop(0, vels, per_velocity, 0, unroll=math.gcd(vels, UNROLL * pieces))
        lax.fori_loop(low, top, per_block, 0, unroll=math.gcd(top - low, 4))
        if first == 0:
            leave(stacked_ref.at[:, :, low * LANES : top * LANES], stacked_out, low, top)
        ready = low + 1 if low else begin
        for at in range(ready, finished, 2):
            per_window(at, min(2, finished - at))
        if first == 0:
            leave(semblance_ref.at[:, :, ready * LANES : finished * LANES], semblance_out, ready, finished)
        top, finished = low, ready
    if first > 0:
        carry_ref[0] = window_ref[1]
        carry_ref[1] = window_ref[2]
    for copy in copies:
        copy.wait()


def panels(first, last, count, classes, vels, tables, rows, after, later):
    span = last - first
    held = count - first
    group = 2 * classes
    window_rows = 2 * CMP_DEV * vels
    flat = [piece for chunk in rows for piece in chunk]
    *tables, blocks = tables
    operands = [blocks, *flat, *tables, *after]
    in_specs = [SMEM] + [VMEM] * (len(flat) + len(tables)) + [ANY] * len(after)
    if later is not None:
        stacked, semblance, carry = later
        operands += [carry, stacked, semblance]
        in_specs += [VMEM] * 3
    staged = []
    if first > 0:
        outs = [
            jax.ShapeDtypeStruct((CMP_DEV, vels, span * LANES), BF16),
            jax.ShapeDtypeStruct((CMP_DEV, vels, (span - 1) * LANES), F32),
            jax.ShapeDtypeStruct((2, window_rows, LANES), BF16),
        ]
        specs = [VMEM] * 3
    else:
        outs = [
            jax.ShapeDtypeStruct((CMP_DEV, vels, count * LANES), BF16),
            jax.ShapeDtypeStruct((CMP_DEV, vels, count * LANES), F32),
        ]
        specs = [ANY] * 2
        done = span + (last < count)
        staged = [
            pltpu.VMEM((CMP_DEV, vels, span * LANES), BF16),
            pltpu.VMEM((CMP_DEV, vels, done * LANES), F32),
            pltpu.SemaphoreType.DMA((2 + 2 * PIECES,)),
        ]
    return pl.pallas_call(
        functools.partial(
            panel_kernel, classes, vels, first, last, count, [len(c) for c in rows], len(after)
        ),
        in_specs=in_specs,
        out_specs=specs,
        out_shape=outs,
        scratch_shapes=[
            pltpu.VMEM((held + 1, flat[0].shape[0], LANES), F32),
            pltpu.VMEM((classes, held + 2, 16, LANES), BF16),
            pltpu.VMEM((held + 2, 16, LANES), BF16),
            pltpu.VMEM((span, CMP_DEV * vels, LANES), F32),
            pltpu.VMEM((span, CMP_DEV * vels, LANES), F32),
            pltpu.VMEM((span, group * vels, LANES), F32),
            pltpu.VMEM((span + 3, window_rows, LANES), BF16),
            pltpu.VMEM((CMP_DEV, LANES), F32),
            pltpu.VMEM((4 * LANES, 2 * LANES), BF16),
            *staged,
        ],
        compiler_params=pltpu.CompilerParams(vmem_limit_bytes=VMEM_BYTES),
        cost_estimate=pl.CostEstimate(
            flops=14000 * CMP_DEV * vels * classes * span * LANES,
            bytes_accessed=(1 + span) * 512 * 1024,
            transcendentals=0,
        ),
    )(*operands)


def table_kernel(classes, start, samples, offsets_ref, velocities_ref, *refs):
    index_ref, low_ref, high_ref, blocks_ref, token_ref = refs[-5:]
    token_ref[...] = jnp.zeros(token_ref.shape, F32)
    vels, rows, cols = low_ref.shape
    lane = lax.broadcasted_iota(jnp.int32, (rows, LANES), 1)
    sub = lax.broadcasted_iota(jnp.int32, (rows, LANES), 0)
    offset = jnp.full((rows, LANES), offsets_ref[0], F32)
    for h in range(1, classes):
        offset = jnp.where(sub % classes == h, offsets_ref[h], offset)

    def per_velocity(j, blocks):
        blocks = list(blocks)
        slowness = offset / jnp.full((rows, LANES), velocities_ref[j], F32)
        square = slowness * slowness
        for at in range(cols // LANES):
            begin = start + at * LANES
            first = jnp.sqrt(square + float(begin) * float(begin)) - 0.01
            first = jnp.minimum(jnp.maximum(first, float(begin)), float(samples)).astype(jnp.int32)
            base = first // LANES
            flat = j * (cols // LANES) + at
            for wide in range(len(blocks)):
                blocks[wide] = jnp.where(lane == flat - wide * LANES, base, blocks[wide])
            time = (lane + begin).astype(F32)
            position = jnp.sqrt(time * time + square)
            floored = jnp.floor(position)
            fraction = position - floored
            index = jnp.minimum(floored, float(samples)).astype(jnp.int32)
            where = slice(at * LANES, (at + 1) * LANES)
            index_ref[j, :, where] = index - base * LANES
            low_ref[j, :, where] = (1.0 - fraction).astype(BF16).astype(F32)
            high_ref[j, :, where] = fraction.astype(BF16).astype(F32)
        return tuple(blocks)

    width = blocks_ref.shape[1] // LANES
    blocks = lax.fori_loop(
        0,
        vels,
        per_velocity,
        tuple(jnp.zeros((rows, LANES), jnp.int32) for _ in range(width)),
        unroll=math.gcd(vels, 4),
    )
    for wide in range(width):
        blocks_ref[:, wide * LANES : (wide + 1) * LANES] = blocks[wide]


def moveout(offsets, velocities, samples, start, stop, after):
    vels, classes = velocities.shape[0], offsets.shape[0]
    shape = (vels, 2 * classes, stop - start)
    width = pl.cdiv(vels * (stop - start) // LANES, LANES) * LANES
    return pl.pallas_call(
        functools.partial(table_kernel, classes, start, samples),
        in_specs=[SMEM, SMEM] + [ANY] * len(after),
        out_specs=[VMEM] * 5,
        out_shape=[
            jax.ShapeDtypeStruct(shape, jnp.int32),
            jax.ShapeDtypeStruct(shape, F32),
            jax.ShapeDtypeStruct(shape, F32),
            jax.ShapeDtypeStruct((2 * classes, width), jnp.int32),
            TOKEN,
        ],
        compiler_params=pltpu.CompilerParams(vmem_limit_bytes=VMEM_BYTES),
        cost_estimate=pl.CostEstimate(
            flops=0, bytes_accessed=0, transcendentals=0
        ),
    )(offsets, velocities, *after)


def per_device(traces, owners, midpoint, offset_class, offsets, velocities):
    samples = traces.shape[1]
    classes, vels = offsets.shape[0], velocities.shape[0]
    count = samples // LANES
    key = (owners * CMP_DEV + midpoint[:, None]) * classes + offset_class[:, None]
    plan = Plan(traces, key, classes)
    cuts = [0, samples // 2, samples]
    chunks = list(zip(cuts[:-1], cuts[1:]))[::-1]
    parts, tokens = [], []
    for start, stop in chunks:
        part, token = plan.bin(start, stop - start, stop == samples, tokens[-1:])
        parts.append(part)
        tokens.append(token)
    tables, spreads = [], []
    *table, token = moveout(offsets, velocities, samples, *chunks[0], tokens[-1:])
    tables.append(table)
    tokens.append(token)
    for at in range(len(chunks)):
        part = plan.exchange(0, parts[at])
        for place in range(1, len(plan.orders[0])):
            part, token = plan.merge(part, tokens[-1:])
            part = plan.exchange(place, part)
            tokens.append(token)
        spreads.append(part)
    rows = []
    for at, part in enumerate(spreads):
        *spread, token = plan.spread(part, tokens[-1:])
        tokens.append(token)
        rows.append(plan.across(spread, at > 0))
        if at:
            *table, token = moveout(offsets, velocities, samples, *chunks[at], tokens[-1:])
            tables.append(table)
            tokens.append(token)
    out = None
    for at, (start, stop) in enumerate(chunks):
        out = panels(
            start // LANES,
            stop // LANES,
            count,
            classes,
            vels,
            tables[at],
            rows[: at + 1][::-1],
            tokens[-1:] if not at else [],
            out,
        )
    return (out[0], out[1])


def solution(mesh):
    in_specs = (
        P(("inline", "xline"), None),
        P(("inline", "xline"), None),
        P(("inline", "xline")),
        P(("inline", "xline")),
        P(),
        P(),
    )
    out_specs = (P(("inline", "xline"), None, None), P(("inline", "xline"), None, None))
    return jax.shard_map(
        per_device, mesh=mesh, in_specs=in_specs, out_specs=out_specs, check_vma=False
    )
```
